32 devices in a mesh: ctx: 8 (over z, y), shard: 4 (over x, core).
Axes of the slice: x: 2, y: 2, z: 4, core: 2. Of those that a mesh axis runs over, the one named last changes fastest.
Arguments:
- tokens: bfloat16 [8, 1024, 1024], P('shard', 'ctx'), may hold values from -6 to 6
- cotangent: bfloat16 [8, 1024, 1024], P('shard', 'ctx'), may hold values from -6 to 6
- lengths: int32 [8], P('shard'), may hold values from 256 to 1024, as said below
- unit_owner: int32 [187], replicated, may hold values from 0 to 3, as said below
- master: float32 [280, 64, 1024], P('shard'), as said below
- first_moment: float32 [280, 64, 1024], P('shard')
- second_moment: float32 [280, 64, 1024], P('shard'), as said below
- norm_gains: float32 [2, 1024], replicated, may hold values from 0.5 to 1.5
- gain_first: float32 [2, 1024], replicated
- gain_second: float32 [2, 1024], replicated, as said below
Outputs:
- output: bfloat16 [8, 1024, 1024], P('shard', 'ctx')
- token_grad: bfloat16 [8, 1024, 1024], P('shard', 'ctx')
- new_master: float32 [280, 64, 1024], P('shard')
- new_first: float32 [280, 64, 1024], P('shard')
- new_second: float32 [280, 64, 1024], P('shard')
- new_gains: float32 [2, 1024], replicated
- new_gain_first: float32 [2, 1024], replicated
- new_gain_second: float32 [2, 1024], replicated
The draws below stay inside these ranges and needn't reach their ends.
Inputs may be any that keep to these rules, and one draw needn't show every extreme that they name: Slot s holds lengths[s] real tokens, then padding; in each aligned group of 2 slots one slot is full. `unit_owner`: no owner holds more than 70 units; one owner holds exactly 70. `master`: slots that no unit maps to are unused. `second_moment`: all entries positive. `gain_second`: all entries positive.
All inputs are finite; a program needn't handle non-finite values.
Results may differ from the reference program's by a relative error of at most 0.018.
The reference program's roundings to bfloat16 on the way count: a program that leaves them out, or rounds other values in their place, can miss the bound.
Values may be sent and summed in bfloat16 or wider, within the bound.
A program may use at most 384 MiB of HBM per device.

```python
import jax
import jax.numpy as jnp
from jax import lax

D = 1024
HEADS = 16
HEAD_DIM = 64
FF = 2624
UNIT = 64
SLOTS_DEV = 2
STEP = 10
SEQ = 1024
SLOTS = 8
UNITS = 187
CAP = 70
N_SHARD = 4


def owner_draw(key):
    groups = SLOTS // SLOTS_DEV
    unit_order = jax.random.permutation(jax.random.fold_in(key, 101), UNITS).astype(jnp.int32)
    heavy_owner = jax.random.randint(jax.random.fold_in(key, 102), (), 0, groups)
    other_owner = jnp.maximum(unit_order - CAP, 0) * (groups - 1) // (UNITS - CAP)
    other_owner = other_owner + (other_owner >= heavy_owner).astype(jnp.int32)
    return jnp.where(unit_order < CAP, heavy_owner, other_owner).astype(jnp.int32)


def slot_kinds(key):
    groups = SLOTS // SLOTS_DEV
    unit_owner = owner_draw(key)
    owner_marks = (unit_owner[:, None] == jnp.arange(groups, dtype=jnp.int32)[None, :]).astype(jnp.int32)
    owner_ranks = jnp.cumsum(owner_marks, axis=0) - 1
    places = unit_owner * CAP + jnp.sum(owner_ranks * owner_marks, axis=1)
    starts = jnp.arange(UNITS, dtype=jnp.int32) * UNIT
    unit_kind = (starts >= 2 * D).astype(jnp.int32) + (starts >= 3 * D).astype(jnp.int32) + (starts >= 4 * D).astype(jnp.int32) + (starts >= 4 * D + 2 * FF).astype(jnp.int32)
    return jnp.full((groups * CAP,), 5, jnp.int32).at[places].set(unit_kind)


def grad_sizes(slot_kind):
    summed = (SLOTS * SEQ) ** 0.5
    return summed * jnp.array([3.1, 2.1, 0.5, 0.33, 0.54, 0.5], jnp.float32)[slot_kind]


def gain_sizes():
    summed = (SLOTS * SEQ) ** 0.5
    return summed * jnp.array([6.9, 0.76], jnp.float32)


def draw_lengths(key, part):
    key = jax.random.fold_in(key, 3)
    drawn_length = jax.random.randint(jax.random.fold_in(key, 1), (SLOTS,), SEQ // 4, SEQ + 1)
    full_slot = jax.random.randint(jax.random.fold_in(key, 2), (SLOTS // SLOTS_DEV,), 0, SLOTS_DEV)
    slot_index = jnp.arange(SLOTS, dtype=jnp.int32)
    is_full = slot_index % SLOTS_DEV == full_slot[slot_index // SLOTS_DEV]
    return jnp.where(is_full, SEQ, drawn_length).astype(jnp.int32)


def draw_unit_owner(key, part):
    return owner_draw(key)


def draw_master(key, part):
    slot_kind = slot_kinds(key)
    key = jax.random.fold_in(key, 7)
    spread = jnp.array([1.5 / D ** 0.5, 1.0 / D ** 0.5, 4.0 / D ** 0.5, 1.0 / D ** 0.5, 1.0 / FF ** 0.5, 1.0 / D ** 0.5], jnp.float32)[slot_kind]
    array_shape = (slot_kind.shape[0], UNIT, D)
    noise_draw = jax.random.normal(key, array_shape, jnp.float32)
    return noise_draw * spread[:, None, None]


def draw_first_moment(key, part):
    slot_kind = slot_kinds(key)
    key = jax.random.fold_in(key, 11)
    spread = 0.111 * grad_sizes(slot_kind)
    array_shape = (slot_kind.shape[0], UNIT, D)
    noise_draw = jax.random.normal(key, array_shape, jnp.float32)
    return noise_draw * spread[:, None, None]


def draw_second_moment(key, part):
    slot_kind = slot_kinds(key)
    key = jax.random.fold_in(key, 13)
    spread = grad_sizes(slot_kind)
    spread = 0.0204 * spread * spread
    array_shape = (slot_kind.shape[0], UNIT, D)
    factor = jnp.exp(jax.random.uniform(key, array_shape, jnp.float32, 0.0, 1.3863))
    return factor * spread[:, None, None]


def draw_gain_first(key, part):
    key = jax.random.fold_in(key, 17)
    spread = 0.111 * gain_sizes()
    noise_draw = jax.random.normal(key, (2, D), jnp.float32)
    return noise_draw * spread[:, None]


def draw_gain_second(key, part):
    key = jax.random.fold_in(key, 19)
    spread = gain_sizes()
    spread = 0.0204 * spread * spread
    factor = jnp.exp(jax.random.uniform(key, (2, D), jnp.float32, 0.0, 1.3863))
    return factor * spread[:, None]


def level_of(key, extent, shards, smallest, top_value):
    def one(axis_at, parts):
        draws = jax.random.uniform(jax.random.fold_in(jax.random.fold_in(key, 6), axis_at), (parts,), jnp.float32, smallest / len(shards), top_value / len(shards))
        return jnp.repeat(jnp.exp(draws), extent[axis_at] // parts).reshape((-1,) + (1,) * (len(extent) - axis_at - 1))

    level = one(*shards[0])
    for cut in shards[1:]:
        level = level * one(*cut)
    return level


def normal_values(own_key, extent, width, bound, pieces=(), kind=jnp.bfloat16):
    entries = width * jax.random.normal(own_key, extent, jnp.float32)
    if pieces:
        entries = entries * level_of(own_key, extent, pieces, -0.22, 0.18)
    return jnp.clip(entries, -bound, bound).astype(kind)


def setup_inputs(seed: int = 0) -> dict:
    splits = jax.random.split(jax.random.key(seed), 11)
    tokens = normal_values(splits[0], (SLOTS, SEQ, D), 1.0, 6.0, ((0, 4), (1, 8)))
    cotangent = normal_values(splits[1], (SLOTS, SEQ, D), 1.0, 6.0, ((0, 4), (1, 8)))
    lengths = draw_lengths(jax.random.fold_in(splits[10], 71), 0)
    unit_owner = draw_unit_owner(jax.random.fold_in(splits[10], 71), 0)
    master = draw_master(jax.random.fold_in(splits[10], 71), 0)
    first_moment = draw_first_moment(jax.random.fold_in(splits[10], 71), 0)
    second_moment = draw_second_moment(jax.random.fold_in(splits[10], 71), 0)
    norm_gains = jnp.clip(1.0 + 0.1 * jax.random.normal(splits[7], (2, D), jnp.float32), 0.5, 1.5)
    gain_first = draw_gain_first(jax.random.fold_in(splits[10], 71), 0)
    gain_second = draw_gain_second(jax.random.fold_in(splits[10], 71), 0)
    return dict(tokens=tokens, cotangent=cotangent, lengths=lengths, unit_owner=unit_owner, master=master, first_moment=first_moment, second_moment=second_moment, norm_gains=norm_gains, gain_first=gain_first, gain_second=gain_second)


@jax.custom_vjp
def low(v):
    return lax.optimization_barrier(v.astype(jnp.bfloat16)).astype(jnp.float32)

@jax.custom_vjp
def low_back(v):
    return v

def low_keep(v):
    return (low(v), None)

def low_pass(kept, grad):
    return (grad,)

def back_keep(v):
    return (v, None)

def back_low(kept, grad):
    return (low(grad),)
low.defvjp(low_keep, low_pass)
low_back.defvjp(back_keep, back_low)
eps_norm = 1e-05
rope_base = 160000.0
mask_fill = -1e+30
beta_one = 0.9
beta_two = 0.98
adam_eps = 1e-06
rate_matrix = 0.03
rate_gain = 0.6
decay_matrix = 0.01
highest = lax.Precision.HIGHEST

def product_nt(left, right):
    return lax.dot_general(left, right, (((1,), (1,)), ((), ())), precision=highest)

def layer_norm(values, gain):
    row_mean = lax.optimization_barrier(jnp.mean(values, axis=-1, keepdims=True))
    centred = values - row_mean
    variance = lax.optimization_barrier(jnp.mean(centred * centred, axis=-1, keepdims=True))
    return centred * lax.rsqrt(variance + eps_norm) * gain

def rope_tables(positions):
    half_dim = HEAD_DIM // 2
    inverse = rope_base ** (-2.0 * jnp.arange(half_dim, dtype=jnp.float32) / HEAD_DIM)
    angles = positions.astype(jnp.float32)[:, None] * inverse[None, :]
    angles = jnp.concatenate([angles, angles], axis=1)
    return (jnp.cos(angles), jnp.sin(angles))

def rotate(values, cosine, sine_table):
    half_dim = HEAD_DIM // 2
    turned = jnp.concatenate([-values[..., half_dim:], values[..., :half_dim]], axis=-1)
    return values * cosine[:, None, :] + turned * sine_table[:, None, :]

def unit_places(unit_owner, capacity, groups):
    owner_marks = (unit_owner[:, None] == jnp.arange(groups, dtype=jnp.int32)[None, :]).astype(jnp.int32)
    owner_ranks = jnp.cumsum(owner_marks, axis=0) - 1
    slot_index = lax.optimization_barrier(jnp.sum(owner_ranks * owner_marks, axis=1))
    return (unit_owner * capacity + slot_index).astype(jnp.int32)

def gated_gelu(upper_proj):
    return jax.nn.gelu(upper_proj[:, :FF], approximate=False) * upper_proj[:, FF:]

def adam_update(weight, gradient, first_old, second_old, step_rate, weight_decay):
    first_new = beta_one * first_old + (1.0 - beta_one) * gradient
    second_new = beta_two * second_old + (1.0 - beta_two) * gradient * gradient
    first_fix = 1.0 - beta_one ** STEP
    second_fix = 1.0 - beta_two ** STEP
    adam_step = first_new / first_fix / (jnp.sqrt(second_new / second_fix) + adam_eps)
    return (weight - step_rate * (adam_step + weight_decay * weight), first_new, second_new)

def attend(head_parts, valid_rows):
    query_head, key_head, value_head = head_parts
    scores = low_back(product_nt(query_head, key_head) * 0.125)
    scores = jnp.where(valid_rows[None, :], scores, mask_fill)
    row_top = lax.optimization_barrier(jnp.max(scores, axis=-1, keepdims=True))
    exponent = jnp.exp(scores - row_top)
    weights = exponent / lax.optimization_barrier(jnp.sum(exponent, axis=-1, keepdims=True))
    return jnp.dot(low(weights), value_head, precision=highest)

def slot_layer(matrices, norm_gains, slot_tokens, slot_cotangent, length):
    w_qkv, w_out, w_up, w_down = matrices
    positions = jnp.arange(SEQ, dtype=jnp.int32)
    valid_rows = positions < length
    cosine, sine_table = rope_tables(positions)
    norm_one = low(layer_norm(slot_tokens, norm_gains[0]))
    qkv_proj = low_back(product_nt(norm_one, w_qkv))
    query_all = low(rotate(qkv_proj[:, :D].reshape(SEQ, HEADS, HEAD_DIM), cosine, sine_table))
    key_all = low(rotate(qkv_proj[:, D:2 * D].reshape(SEQ, HEADS, HEAD_DIM), cosine, sine_table))
    value_all = low(qkv_proj[:, 2 * D:].reshape(SEQ, HEADS, HEAD_DIM))
    per_head = jax.checkpoint(lambda head_parts: attend(head_parts, valid_rows))
    heads_out = lax.map(per_head, (jnp.transpose(query_all, (1, 0, 2)), jnp.transpose(key_all, (1, 0, 2)), jnp.transpose(value_all, (1, 0, 2))))
    mixed = low(low_back(jnp.transpose(heads_out, (1, 0, 2)).reshape(SEQ, D)))
    attn_out = low_back(product_nt(mixed, w_out))
    middle = slot_tokens + attn_out
    norm_two = low(layer_norm(middle, norm_gains[1]))
    upper_proj = low_back(product_nt(norm_two, w_up))
    hidden = low(gated_gelu(upper_proj))
    down_out = low_back(jnp.dot(hidden, w_down, precision=highest))
    result = middle + down_out
    loss_sum = jnp.sum(result * slot_cotangent * valid_rows[:, None].astype(jnp.float32))
    return (loss_sum, result)

def reference(tokens, cotangent, lengths, unit_owner, master, first_moment, second_moment, norm_gains, gain_first, gain_second):
    places = unit_places(unit_owner, CAP, N_SHARD)
    cotangent_wide = cotangent.astype(jnp.float32)
    checked_layer = jax.checkpoint(slot_layer)

    def forward(master_wide, gains_wide, tokens_wide):
        stacked = low(jnp.take(master_wide, places, axis=0).reshape(UNITS * UNIT, D))
        matrices = (stacked[:3 * D], stacked[3 * D:4 * D], stacked[4 * D:4 * D + 2 * FF], stacked[4 * D + 2 * FF:])

        def one_slot(loss_sum, slot_inputs):
            slot_tokens, slot_cotangent, length = slot_inputs
            slot_loss, result = checked_layer(matrices, gains_wide, slot_tokens, slot_cotangent, length)
            return (loss_sum + slot_loss, result)
        return lax.scan(one_slot, jnp.zeros((), jnp.float32), (tokens_wide, cotangent_wide, lengths))
    loss_sum, pullback, results = jax.vjp(forward, master, norm_gains, tokens.astype(jnp.float32), has_aux=True)
    grad_master, grad_gains, grad_tokens = pullback(jnp.ones((), jnp.float32))
    new_master, new_first, new_second = adam_update(master, grad_master, first_moment, second_moment, rate_matrix, decay_matrix)
    new_gains, new_gain_first, new_gain_second = adam_update(norm_gains, grad_gains, gain_first, gain_second, rate_gain, 0.0)
    return (results.astype(jnp.bfloat16), grad_tokens.astype(jnp.bfloat16), new_master, new_first, new_second, new_gains, new_gain_first, new_gain_second)
```

```python
import functools

import jax
import jax.numpy as jnp
from jax import lax
from jax.experimental import pallas as pl
from jax.experimental.pallas import tpu as pltpu
from jax.sharding import PartitionSpec as P

HEADS = 16
HEAD_DIM = 64
FF = 2624
STEP = 10
MESH = pl.DeviceIdType.MESH
DMA = pltpu.SemaphoreType.DMA

eps_norm = 1e-05
rope_base = 160000.0
mask_fill = -1e30
beta_one = 0.9
beta_two = 0.98
adam_eps = 1e-06
rate_matrix = 0.03
rate_gain = 0.6
decay_matrix = 0.01
BOTH = ("ctx", "shard")
VMEM_BYTES = 60 * 2**20


def transposed(left, right):
    return lax.dot_general(
        left, right, (((1,), (1,)), ((), ())), preferred_element_type=jnp.float32
    )


def leading(left, right):
    return lax.dot_general(
        left, right, (((0,), (0,)), ((), ())), preferred_element_type=jnp.float32
    )


def layer_norm(values, gain):
    row_mean = jnp.mean(values, axis=-1, keepdims=True)
    centred = values - row_mean
    variance = jnp.mean(centred * centred, axis=-1, keepdims=True)
    return centred * lax.rsqrt(variance + eps_norm) * gain


def rope_tables(positions, heads):
    half_dim = HEAD_DIM // 2
    inverse = rope_base ** (-2.0 * jnp.arange(half_dim, dtype=jnp.float32) / HEAD_DIM)
    angles = positions.astype(jnp.float32)[:, None] * inverse[None, :]
    cosine, sine = jnp.cos(angles), jnp.sin(angles)
    cosine = jnp.concatenate([cosine, cosine] * heads, axis=1)
    sine = jnp.concatenate([-sine, sine] * heads, axis=1)
    return (cosine, sine)


def half_turned(values):
    width = values.shape[-1]
    half = HEAD_DIM // 2
    lane = lax.broadcasted_iota(jnp.int32, values.shape, values.ndim - 1)
    if width == HEAD_DIM:
        return jnp.concatenate([values[:, half:], values[:, :half]], axis=1)
    ahead = pltpu.roll(values, width - half, axis=1)
    behind = pltpu.roll(values, half, axis=1)
    return jnp.where(lane % HEAD_DIM < half, ahead, behind)


def unit_places(unit_owner, capacity, groups):
    owner_marks = (unit_owner[:, None] == jnp.arange(groups, dtype=jnp.int32)[None, :]).astype(
        jnp.int32
    )
    owner_ranks = jnp.cumsum(owner_marks, axis=0) - 1
    return jnp.sum(owner_ranks * owner_marks, axis=1)


def gated_gelu(upper_proj):
    return jax.nn.gelu(upper_proj[:, :FF], approximate=False) * upper_proj[:, FF:]


def adam_update(weight, gradient, first_old, second_old, step_rate, weight_decay):
    first_new = beta_one * first_old + (1.0 - beta_one) * gradient
    second_new = beta_two * second_old + (1.0 - beta_two) * gradient * gradient
    first_fix = 1.0 - beta_one**STEP
    second_fix = 1.0 - beta_two**STEP
    adam_step = first_new / first_fix / (jnp.sqrt(second_new / second_fix) + adam_eps)
    return (weight - step_rate * (adam_step + weight_decay * weight), first_new, second_new)


def qkv_kernel(norm_ref, w_ref, cos_ref, sin_ref, out_ref):
    tile = pl.program_id(0)
    turned_tiles = 2 * pl.num_programs(0) // 3
    values = transposed(norm_ref[...], w_ref[...])

    @pl.when(tile < turned_tiles)
    def _():
        out_ref[...] = (values * cos_ref[...] + half_turned(values) * sin_ref[...]).astype(
            out_ref.dtype
        )

    @pl.when(tile >= turned_tiles)
    def _():
        out_ref[...] = values.astype(out_ref.dtype)


def qkv_call(norm_one, w_qkv, cosine, sine):
    rows, width = norm_one.shape
    cols = 256
    return pl.pallas_call(
        qkv_kernel,
        grid=(3 * width // cols,),
        in_specs=[
            pl.BlockSpec((rows, width), lambda i: (0, 0)),
            pl.BlockSpec((cols, width), lambda i: (i, 0)),
            pl.BlockSpec((rows, cols), lambda i: (0, 0)),
            pl.BlockSpec((rows, cols), lambda i: (0, 0)),
        ],
        out_specs=pl.BlockSpec((rows, cols), lambda i: (0, i)),
        out_shape=jax.ShapeDtypeStruct((rows, 3 * width), jnp.bfloat16),
        name="qkv",
    )(norm_one, w_qkv, cosine, sine)


def head_only(values, head):
    width = values.shape[-1]
    if width == HEAD_DIM:
        return values
    lane = lax.broadcasted_iota(jnp.int32, values.shape, 1)
    return jnp.where(lane // HEAD_DIM == head, values, jnp.zeros_like(values))


def attend_slot(q_ref, k_ref, v_ref, bias, out_ref, wide_ref, lse_ref, chunk):
    seq, width = k_ref.shape
    heads = width // HEAD_DIM
    keys = [head_only(k_ref[...], h) for h in range(heads)]
    values = [head_only(v_ref[...], h) for h in range(heads)]

    def step(i, _):
        rows = pl.ds(pl.multiple_of(i * chunk, chunk), chunk)
        query = q_ref[rows, :] * jnp.bfloat16(0.125)
        total = None
        stats = None
        for h in range(heads):
            scores = transposed(query, keys[h]) + bias
            top = jnp.max(scores, axis=-1, keepdims=True)
            weights = jnp.exp(scores - top)
            norm = jnp.sum(weights, axis=-1, keepdims=True)
            low = (weights * (1.0 / norm)).astype(jnp.bfloat16)
            part = jnp.dot(low, values[h], preferred_element_type=jnp.float32)
            lse = jnp.broadcast_to(top + jnp.log(norm), (chunk, width))
            total = part if total is None else total + part
            if stats is None:
                stats = lse
            else:
                lane = lax.broadcasted_iota(jnp.int32, lse.shape, 1)
                stats = jnp.where(lane // HEAD_DIM == h, lse, stats)
        out_ref[rows, :] = total.astype(jnp.bfloat16)
        wide_ref[rows, :] = total
        lse_ref[rows, :] = stats
        return 0

    lax.fori_loop(0, seq // chunk, step, 0)


def attend_back_slot(
    q_ref, k_ref, v_ref, g_ref, wide_ref, lse_ref, bias, cos, sin, dq_ref, dk_ref, dv_ref, acc_k, acc_v, chunk
):
    seq, width = k_ref.shape
    heads = width // HEAD_DIM
    keys = [head_only(k_ref[...], h) for h in range(heads)]
    values = [head_only(v_ref[...], h) for h in range(heads)]
    acc_k[...] = jnp.zeros_like(acc_k)
    acc_v[...] = jnp.zeros_like(acc_v)

    def turned_back(grad, rows):
        return grad * cos[rows, :] - half_turned(grad) * sin[rows, :]

    def step(i, _):
        rows = pl.ds(pl.multiple_of(i * chunk, chunk), chunk)
        query = q_ref[rows, :]
        grad = g_ref[rows, :]
        lse_all = lse_ref[rows, :]
        both = grad.astype(jnp.float32) * wide_ref[rows, :]
        total = None
        for h in range(heads):
            lse = lse_all[:, h * HEAD_DIM : h * HEAD_DIM + 1]
            delta = jnp.sum(head_only(both, h), axis=-1, keepdims=True)
            scores = transposed(query * jnp.bfloat16(0.125), keys[h])
            weights = jnp.exp(scores + (bias - lse))
            back = transposed(grad, values[h])
            low = (weights * (back - delta)).astype(jnp.bfloat16)
            part = jnp.dot(low, keys[h], preferred_element_type=jnp.float32)
            total = part if total is None else total + part
            acc_v[...] += leading(weights.astype(jnp.bfloat16), head_only(grad, h))
            acc_k[...] += leading(low, head_only(query, h))
        dq_ref[rows, :] = turned_back(total * 0.125, rows).astype(jnp.bfloat16)
        return 0

    lax.fori_loop(0, seq // chunk, step, 0)
    every = slice(None)
    dk_ref[...] = turned_back(acc_k[...] * 0.125, every).astype(jnp.bfloat16)
    dv_ref[...] = acc_v[...].astype(jnp.bfloat16)


def attend_kernel(slots, chunk, qkv_ref, bias_ref, out_ref, wide_ref, lse_ref):
    for s in range(slots):
        attend_slot(
            qkv_ref.at[0, s], qkv_ref.at[1, s], qkv_ref.at[2, s], bias_ref[s],
            out_ref.at[s], wide_ref.at[s], lse_ref.at[s], chunk,
        )


def attend_call(qkv, bias):
    _, slots, seq, width = qkv.shape
    chunk = 256
    return pl.pallas_call(
        functools.partial(attend_kernel, slots, chunk),
        out_shape=(
            jax.ShapeDtypeStruct((slots, seq, width), jnp.bfloat16),
            jax.ShapeDtypeStruct((slots, seq, width), jnp.float32),
            jax.ShapeDtypeStruct((slots, seq, width), jnp.float32),
        ),
        compiler_params=pltpu.CompilerParams(vmem_limit_bytes=VMEM_BYTES),
        name="attend",
    )(qkv, bias)


def attend_back_kernel(slots, chunk, qkv_ref, g_ref, wide_ref, lse_ref, bias_ref, cos_ref, sin_ref, out_ref, acc_k, acc_v):
    for s in range(slots):
        attend_back_slot(
            qkv_ref.at[0, s], qkv_ref.at[1, s], qkv_ref.at[2, s], g_ref.at[s],
            wide_ref.at[s], lse_ref.at[s], bias_ref[s], cos_ref, sin_ref,
            out_ref.at[0, s], out_ref.at[1, s], out_ref.at[2, s], acc_k, acc_v, chunk,
        )


def attend_back_call(qkv, grad_heads, wide, lse, bias, cosine, sine):
    _, slots, seq, width = qkv.shape
    chunk = 256
    return pl.pallas_call(
        functools.partial(attend_back_kernel, slots, chunk),
        out_shape=jax.ShapeDtypeStruct(qkv.shape, jnp.bfloat16),
        scratch_shapes=[pltpu.VMEM((seq, width), jnp.float32)] * 2,
        compiler_params=pltpu.CompilerParams(vmem_limit_bytes=VMEM_BYTES),
        name="attend_back",
    )(qkv, grad_heads, wide, lse, bias, cosine, sine)


def adam_kernel(per, unit_ref, used_ref, *refs):
    grads = refs[:per]
    master, first, second, new_master, new_first, new_second = refs[per:]
    for j in range(per):
        slot = pl.program_id(0) * per + j
        keep = used_ref[slot].astype(jnp.float32)
        grad = grads[j][0].astype(jnp.float32) * keep
        weight, one, two = adam_update(
            master[j], grad, first[j], second[j], rate_matrix, decay_matrix
        )
        new_master[j] = weight
        new_first[j] = one
        new_second[j] = two


def adam_call(unit_of_slot, used, grads, master, first, second):
    capacity, rows, width = master.shape
    per = 2 if capacity % 2 == 0 else 1

    def unit_spec(j):
        return pl.BlockSpec((1, rows, width), lambda i, units, used: (units[i * per + j], 0, 0))

    slot_spec = pl.BlockSpec((per, rows, width), lambda i, units, used: (i, 0, 0))
    return pl.pallas_call(
        functools.partial(adam_kernel, per),
        grid_spec=pltpu.PrefetchScalarGridSpec(
            num_scalar_prefetch=2,
            grid=(capacity // per,),
            in_specs=[unit_spec(j) for j in range(per)] + [slot_spec] * 3,
            out_specs=[slot_spec] * 3,
        ),
        out_shape=[jax.ShapeDtypeStruct(master.shape, jnp.float32)] * 3,
        compiler_params=pltpu.CompilerParams(vmem_limit_bytes=VMEM_BYTES),
        name="adamw",
    )(unit_of_slot, used, *([grads] * per), master, first, second)


def place():
    ctx, shard = lax.axis_index("ctx"), lax.axis_index("shard")
    return ctx // 2, ctx % 2, shard // 2, shard % 2


def device_at(z, y, x, core):
    return (z * 2 + y, x * 2 + core)


def block_at(z, y, x, core):
    return (z * 2 + y) * 4 + x * 2 + core


def remote(src, dst, send, recv, device):
    return pltpu.make_async_remote_copy(
        src_ref=src, dst_ref=dst, send_sem=send, recv_sem=recv, device_id=device, device_id_type=MESH
    )


def greet(devices):
    barrier = pltpu.get_barrier_semaphore()
    for device in devices:
        pl.semaphore_signal(barrier, inc=1, device_id=device, device_id_type=MESH)
    pl.semaphore_wait(barrier, len(devices))


def gather_kernel(units, x_ref, out_ref, lsem, zs, zr, as_, ar, bs, br, a2s, a2r, b2s, b2r, ss, sr, sas, sar, sbs, sbr, sa2s, sa2r, sb2s, sb2r):
    nz = 4
    z, y, x, core = place()
    half = units // 2
    me = block_at(z, y, x, core)
    xn = device_at(z, y, 1 - x, core)
    yn = device_at(z, 1 - y, x, core)
    sib = device_at(z, y, x, 1 - core)
    greet([xn, yn, sib] + [device_at((z + d) % nz, y, x, core) for d in (1, 2, 3)])
    own = pltpu.make_async_copy(x_ref, out_ref.at[me], lsem)
    own.start()

    def part(i, p):
        return out_ref.at[i].at[pl.ds(p * half, half)]

    def moved(ref, send, recv, device):
        return remote(ref, ref, send, recv, device)

    def z_copy(d):
        return remote(x_ref, out_ref.at[me], zs.at[d - 1], zr.at[d - 1], device_at((z + d) % nz, y, x, core))

    def z_got(zb, d):
        ref = out_ref.at[block_at(zb, y, x, core)]
        return moved(ref, zs.at[nz - d - 1], zr.at[nz - d - 1], xn)

    def a_copy(zb, xb):
        return moved(part(block_at(zb, y, xb, core), 0), as_.at[zb], ar.at[zb], xn)

    def b_copy(zb, yb):
        return moved(part(block_at(zb, yb, x, core), 1), bs.at[zb], br.at[zb], yn)

    def a2_copy(zb, yb, xb):
        j = zb * 2 + xb
        return moved(part(block_at(zb, yb, xb, core), 0), a2s.at[j], a2r.at[j], yn)

    def b2_copy(zb, yb, xb):
        j = zb * 2 + yb
        return moved(part(block_at(zb, yb, xb, core), 1), b2s.at[j], b2r.at[j], xn)

    def s_copy(zb, c):
        return moved(out_ref.at[block_at(zb, y, x, c)], ss.at[zb], sr.at[zb], sib)

    def sa_copy(zb, c):
        return moved(part(block_at(zb, y, 1 - x, c), 0), sas.at[zb], sar.at[zb], sib)

    def sb_copy(zb, c):
        return moved(part(block_at(zb, 1 - y, x, c), 1), sbs.at[zb], sbr.at[zb], sib)

    def sa2_copy(zb, xb, c):
        j = zb * 2 + xb
        return moved(part(block_at(zb, 1 - y, xb, c), 0), sa2s.at[j], sa2r.at[j], sib)

    def sb2_copy(zb, yb, c):
        j = zb * 2 + yb
        return moved(part(block_at(zb, yb, 1 - x, c), 1), sb2s.at[j], sb2r.at[j], sib)

    def first(zb):
        a_copy(zb, x).start()
        b_copy(zb, y).start()
        a2_copy(zb, y, x).start()
        b2_copy(zb, y, x).start()
        s_copy(zb, core).start()

    def second(zb):
        a_copy(zb, 1 - x).wait_recv()
        a2_copy(zb, y, 1 - x).start()
        sa_copy(zb, core).start()
        b_copy(zb, 1 - y).wait_recv()
        b2_copy(zb, 1 - y, x).start()
        sb_copy(zb, core).start()

    for d in (1, 3, 2):
        z_copy(d).start()
    own.wait()
    order = [z, (z + 1) % nz, (z + 3) % nz, (z + 2) % nz]
    first(z)
    for n, d in enumerate((1, 3, 2)):
        zb = (z + d) % nz
        z_got(zb, d).wait_recv()
        first(zb)
        second(order[n])
    second(order[3])
    for zb in order:
        for xb in (x, 1 - x):
            a2_copy(zb, 1 - y, xb).wait_recv()
            sa2_copy(zb, xb, core).start()
        for yb in (y, 1 - y):
            b2_copy(zb, yb, 1 - x).wait_recv()
            sb2_copy(zb, yb, core).start()
    for d in (1, 2, 3):
        z_copy(d).wait_send()
    for zb in range(nz):
        a_copy(zb, x).wait_send()
        b_copy(zb, y).wait_send()
        s_copy(zb, core).wait_send()
        s_copy(zb, 1 - core).wait_recv()
        sa_copy(zb, core).wait_send()
        sa_copy(zb, 1 - core).wait_recv()
        sb_copy(zb, core).wait_send()
        sb_copy(zb, 1 - core).wait_recv()
        for q in range(2):
            a2_copy(zb, y, q).wait_send()
            b2_copy(zb, q, x).wait_send()
            sa2_copy(zb, q, core).wait_send()
            sa2_copy(zb, q, 1 - core).wait_recv()
            sb2_copy(zb, q, core).wait_send()
            sb2_copy(zb, q, 1 - core).wait_recv()


def gather_call(block, collective_id):
    units = block.shape[0]
    sems = [DMA] + [DMA((3,))] * 2 + [DMA((4,))] * 4 + [DMA((8,))] * 4 + [DMA((4,))] * 6 + [DMA((8,))] * 4
    out = pl.pallas_call(
        functools.partial(gather_kernel, units),
        out_shape=jax.ShapeDtypeStruct((32,) + block.shape, block.dtype),
        in_specs=[pl.BlockSpec(memory_space=pl.ANY)],
        out_specs=pl.BlockSpec(memory_space=pl.ANY),
        scratch_shapes=sems,
        compiler_params=pltpu.CompilerParams(collective_id=collective_id, has_side_effects=True),
        name="gather_units",
    )(block)
    return out.reshape((-1,) + block.shape[1:])


def swap_kernel(parts, n, x_ref, out_ref, lsem, send, recv):
    ctx, shard = lax.axis_index("ctx"), lax.axis_index("shard")
    rows, width = x_ref.shape[2], out_ref.shape[3]
    greet([(lax.rem(ctx + d, n), shard) for d in range(1, n)])

    def src(to):
        return x_ref.at[:, :, :, pl.ds(pl.multiple_of(to * width, width), width)]

    def dst(owner):
        return out_ref.at[:, :, pl.ds(pl.multiple_of(owner * rows, rows), rows), :]

    def copy(d):
        to = lax.rem(ctx + d, n)
        return remote(src(to), dst(ctx), send.at[d], recv.at[d], (to, shard))

    own = pltpu.make_async_copy(src(ctx), dst(ctx), lsem)
    own.start()
    for d in range(1, n):
        copy(d).start()
    own.wait()
    for d in range(1, n):
        copy(d).wait()


def swap_back_kernel(parts, n, x_ref, out_ref, lsem, send, recv):
    ctx, shard = lax.axis_index("ctx"), lax.axis_index("shard")
    rows, width = out_ref.shape[2], x_ref.shape[3]
    greet([(lax.rem(ctx + d, n), shard) for d in range(1, n)])

    def src(to):
        return x_ref.at[:, :, pl.ds(pl.multiple_of(to * rows, rows), rows), :]

    def dst(owner):
        return out_ref.at[:, :, :, pl.ds(pl.multiple_of(owner * width, width), width)]

    def copy(d):
        to = lax.rem(ctx + d, n)
        return remote(src(to), dst(ctx), send.at[d], recv.at[d], (to, shard))

    own = pltpu.make_async_copy(src(ctx), dst(ctx), lsem)
    own.start()
    for d in range(1, n):
        copy(d).start()
    own.wait()
    for d in range(1, n):
        copy(d).wait()


def swap_call(values, n, back, collective_id, name):
    parts, slots, rows, cols = values.shape
    shape = (parts, slots, rows // n, cols * n) if back else (parts, slots, rows * n, cols // n)
    vmem = pl.BlockSpec(memory_space=pltpu.VMEM)
    return pl.pallas_call(
        functools.partial(swap_back_kernel if back else swap_kernel, parts, n),
        out_shape=jax.ShapeDtypeStruct(shape, values.dtype),
        in_specs=[vmem],
        out_specs=vmem,
        scratch_shapes=[DMA, DMA((n,)), DMA((n,))],
        compiler_params=pltpu.CompilerParams(
            collective_id=collective_id, has_side_effects=True, vmem_limit_bytes=VMEM_BYTES
        ),
        name=name,
    )(values)


def to_heads(values, n, fast, collective_id, name):
    if fast:
        return swap_call(values, n, False, collective_id, name)
    return lax.all_to_all(values, "ctx", split_axis=3, concat_axis=2, tiled=True)


def to_rows(values, n, fast, collective_id, name):
    if fast:
        return swap_call(values, n, True, collective_id, name)
    return lax.all_to_all(values, "ctx", split_axis=2, concat_axis=3, tiled=True)


def shards(
    fast,
    tokens,
    cotangent,
    lengths,
    unit_owner,
    master,
    first_moment,
    second_moment,
    norm_gains,
    gain_first,
    gain_second,
):
    slots, block_len, width = tokens.shape
    groups = lax.axis_size("shard")
    n = lax.axis_size("ctx")
    ctx, shard = lax.axis_index("ctx"), lax.axis_index("shard")
    capacity, unit_rows, _ = master.shape
    units = unit_owner.shape[0]
    rows_all = slots * block_len
    seq = block_len * n
    device_count = n * groups
    my_width = width // n

    per = -(-units // device_count)
    padded = per * device_count
    rank = unit_places(unit_owner, capacity, groups)
    piece = ctx * groups * per + jnp.arange(groups * per, dtype=jnp.int32)
    piece_units = jnp.minimum(piece, units - 1)
    owners = unit_owner[piece_units]
    mine = (owners == shard) & (piece < units)
    given = jnp.where(
        mine[:, None, None], jnp.take(master, rank[piece_units], axis=0, mode="clip"), 0.0
    ).astype(jnp.bfloat16)
    own_units = lax.psum_scatter(given, "shard", scatter_dimension=0, tiled=True)
    if fast:
        stack = gather_call(own_units, 0)
    else:
        stack = lax.all_gather(own_units, BOTH, axis=0, tiled=True)
    stacked = stack.reshape(padded * unit_rows, width)
    w_out = stacked[3 * width : 4 * width]
    w_up = stacked[4 * width : 4 * width + 2 * FF]
    w_down = stacked[4 * width + 2 * FF : 4 * width + 3 * FF]

    positions = ctx * block_len + jnp.arange(block_len, dtype=jnp.int32)
    tile_heads = 256 // HEAD_DIM
    cos_rows, sin_rows = rope_tables(jnp.tile(positions, slots), tile_heads)
    cos_seq, sin_seq = rope_tables(jnp.arange(seq, dtype=jnp.int32), my_width // HEAD_DIM)
    live_rows = (positions[None, :] < lengths[:, None]).astype(jnp.float32)
    bias = jnp.where(
        jnp.arange(seq, dtype=jnp.int32)[None, :] < lengths[:, None], 0.0, mask_fill
    ).astype(jnp.float32)[:, None, :]

    inputs = tokens.astype(jnp.float32).reshape(rows_all, width)
    norm_one = layer_norm(inputs, norm_gains[0]).astype(jnp.bfloat16)
    qkv = qkv_call(norm_one, stacked, cos_rows, sin_rows)
    qkv_rows = jnp.transpose(qkv.reshape(slots, block_len, 3, width), (2, 0, 1, 3))
    qkv_heads = to_heads(qkv_rows, n, fast, 1, "swap_qkv")
    mixed_heads, wide, lse = attend_call(qkv_heads, bias)
    mixed_low = to_rows(mixed_heads[None], n, fast, 2, "swap_mixed").reshape(rows_all, width)

    middle = inputs + transposed(mixed_low, w_out)
    norm_two = layer_norm(middle, norm_gains[1]).astype(jnp.bfloat16)
    upper_proj = transposed(norm_two, w_up)
    hidden_low = gated_gelu(upper_proj).astype(jnp.bfloat16)
    result = middle + jnp.dot(hidden_low, w_down, preferred_element_type=jnp.float32)
    output = result.astype(jnp.bfloat16).reshape(slots, block_len, width)

    grad_result = cotangent.astype(jnp.float32).reshape(rows_all, width) * live_rows.reshape(
        rows_all, 1
    )
    grad_down_low = grad_result.astype(jnp.bfloat16)
    grad_w_down = leading(hidden_low, grad_down_low)
    grad_hidden = transposed(grad_down_low, w_down)
    gelu_value, gelu_back = jax.vjp(gated_gelu, upper_proj)
    grad_upper_low = gelu_back(grad_hidden)[0].astype(jnp.bfloat16)
    grad_w_up = leading(grad_upper_low, norm_two)
    grad_norm_two = jnp.dot(grad_upper_low, w_up, preferred_element_type=jnp.float32)
    norm_value, norm_back_two = jax.vjp(layer_norm, middle, norm_gains[1])
    grad_middle_part, grad_gain_two = norm_back_two(grad_norm_two)
    grad_middle = grad_result + grad_middle_part
    grad_attn_low = grad_middle.astype(jnp.bfloat16)
    grad_w_out = leading(grad_attn_low, mixed_low)
    grad_heads_rows = jnp.dot(grad_attn_low, w_out, preferred_element_type=jnp.float32).astype(
        jnp.bfloat16
    )
    grad_heads = to_heads(
        grad_heads_rows.reshape(1, slots, block_len, width), n, fast, 3, "swap_grad"
    )[0]
    grad_qkv_heads = attend_back_call(qkv_heads, grad_heads, wide, lse, bias, cos_seq, sin_seq)
    grad_qkv_rows = to_rows(grad_qkv_heads, n, fast, 4, "swap_grad_qkv")
    grad_qkv_low = jnp.transpose(grad_qkv_rows, (1, 2, 0, 3)).reshape(rows_all, 3 * width)

    grad_w_qkv = leading(grad_qkv_low, norm_one)
    grad_norm_one = jnp.dot(
        grad_qkv_low, stacked[: 3 * width], preferred_element_type=jnp.float32
    )
    first_value, norm_back_one = jax.vjp(layer_norm, inputs, norm_gains[0])
    grad_input_part, grad_gain_one = norm_back_one(grad_norm_one)
    token_grad = (
        (grad_middle + grad_input_part).astype(jnp.bfloat16).reshape(slots, block_len, width)
    )

    unit_grads = jnp.concatenate(
        [
            grad_w_qkv.astype(jnp.bfloat16),
            grad_w_out.astype(jnp.bfloat16),
            grad_w_up.astype(jnp.bfloat16),
            grad_w_down.astype(jnp.bfloat16),
            jnp.zeros(((padded - units) * unit_rows, width), jnp.bfloat16),
        ],
        axis=0,
    ).reshape(padded, unit_rows, width)
    own_grads = lax.psum_scatter(unit_grads, BOTH, scatter_dimension=0, tiled=True)
    if fast:
        all_grads = gather_call(own_grads, 0)
    else:
        all_grads = lax.all_gather(own_grads, BOTH, axis=0, tiled=True)
    gain_grad = lax.psum(jnp.stack([grad_gain_one, grad_gain_two]), BOTH)

    slot_index = jnp.where(unit_owner == shard, rank, capacity)
    unit_of_slot = (
        jnp.zeros((capacity + 1,), jnp.int32)
        .at[slot_index]
        .set(jnp.arange(units, dtype=jnp.int32))[:capacity]
    )
    used = (jnp.arange(capacity) < jnp.sum(unit_owner == shard)).astype(jnp.int32)
    new_master, new_first, new_second = adam_call(
        unit_of_slot, used, all_grads, master, first_moment, second_moment
    )
    new_gains, new_gain_first, new_gain_second = adam_update(
        norm_gains, gain_grad, gain_first, gain_second, rate_gain, 0.0
    )
    return (
        output,
        token_grad,
        new_master,
        new_first,
        new_second,
        new_gains,
        new_gain_first,
        new_gain_second,
    )


def solution(mesh):
    fast = dict(mesh.shape) == {"ctx": 8, "shard": 4}
    return jax.shard_map(
        functools.partial(shards, fast),
        mesh=mesh,
        in_specs=(
            P("shard", "ctx", None),
            P("shard", "ctx", None),
            P("shard"),
            P(),
            P("shard", None, None),
            P("shard", None, None),
            P("shard", None, None),
            P(),
            P(),
            P(),
        ),
        out_specs=(
            P("shard", "ctx", None),
            P("shard", "ctx", None),
            P("shard", None, None),
            P("shard", None, None),
            P("shard", None, None),
            P(),
            P(),
            P(),
        ),
        check_vma=False,
    )
```

```python
import functools

import jax
import jax.numpy as jnp
from jax import lax
from jax.experimental import pallas as pl
from jax.experimental.pallas import tpu as pltpu
from jax.sharding import PartitionSpec as P

HEADS = 16
HEAD_DIM = 64
FF = 2624
STEP = 10
MESH = pl.DeviceIdType.MESH
DMA = pltpu.SemaphoreType.DMA

eps_norm = 1e-05
rope_base = 160000.0
mask_fill = -1e30
beta_one = 0.9
beta_two = 0.98
adam_eps = 1e-06
rate_matrix = 0.03
rate_gain = 0.6
decay_matrix = 0.01
BOTH = ("ctx", "shard")
VMEM_BYTES = 60 * 2**20


def transposed(left, right):
    return lax.dot_general(
        left, right, (((1,), (1,)), ((), ())), preferred_element_type=jnp.float32
    )


def leading(left, right):
    return lax.dot_general(
        left, right, (((0,), (0,)), ((), ())), preferred_element_type=jnp.float32
    )


def layer_norm(values, gain):
    row_mean = jnp.mean(values, axis=-1, keepdims=True)
    centred = values - row_mean
    variance = jnp.mean(centred * centred, axis=-1, keepdims=True)
    return centred * lax.rsqrt(variance + eps_norm) * gain


def rope_tables(positions, heads):
    half_dim = HEAD_DIM // 2
    inverse = rope_base ** (-2.0 * jnp.arange(half_dim, dtype=jnp.float32) / HEAD_DIM)
    angles = positions.astype(jnp.float32)[:, None] * inverse[None, :]
    cosine, sine = jnp.cos(angles), jnp.sin(angles)
    cosine = jnp.concatenate([cosine, cosine] * heads, axis=1)
    sine = jnp.concatenate([-sine, sine] * heads, axis=1)
    return (cosine, sine)


def half_turned(values):
    width = values.shape[-1]
    half = HEAD_DIM // 2
    lane = lax.broadcasted_iota(jnp.int32, values.shape, values.ndim - 1)
    if width == HEAD_DIM:
        return jnp.concatenate([values[:, half:], values[:, :half]], axis=1)
    ahead = pltpu.roll(values, width - half, axis=1)
    behind = pltpu.roll(values, half, axis=1)
    return jnp.where(lane % HEAD_DIM < half, ahead, behind)


def unit_places(unit_owner, capacity, groups):
    owner_marks = (unit_owner[:, None] == jnp.arange(groups, dtype=jnp.int32)[None, :]).astype(
        jnp.int32
    )
    owner_ranks = jnp.cumsum(owner_marks, axis=0) - 1
    return jnp.sum(owner_ranks * owner_marks, axis=1)


def gated_gelu(upper_proj):
    return jax.nn.gelu(upper_proj[:, :FF], approximate=False) * upper_proj[:, FF:]


def adam_update(weight, gradient, first_old, second_old, step_rate, weight_decay):
    first_new = beta_one * first_old + (1.0 - beta_one) * gradient
    second_new = beta_two * second_old + (1.0 - beta_two) * gradient * gradient
    first_fix = 1.0 - beta_one**STEP
    second_fix = 1.0 - beta_two**STEP
    adam_step = first_new / first_fix / (jnp.sqrt(second_new / second_fix) + adam_eps)
    return (weight - step_rate * (adam_step + weight_decay * weight), first_new, second_new)


def qkv_kernel(norm_ref, w_ref, cos_ref, sin_ref, out_ref):
    tile = pl.program_id(0)
    turned_tiles = 2 * pl.num_programs(0) // 3
    values = transposed(norm_ref[...], w_ref[...])

    @pl.when(tile < turned_tiles)
    def _():
        out_ref[0] = (values * cos_ref[...] + half_turned(values) * sin_ref[...]).astype(
            out_ref.dtype
        )

    @pl.when(tile >= turned_tiles)
    def _():
        out_ref[0] = values.astype(out_ref.dtype)


def qkv_call(norm_one, w_qkv, cosine, sine):
    rows, width = norm_one.shape
    cols = 256
    tiles = width // cols
    return pl.pallas_call(
        qkv_kernel,
        grid=(3 * width // cols,),
        in_specs=[
            pl.BlockSpec((rows, width), lambda i: (0, 0)),
            pl.BlockSpec((cols, width), lambda i: (i, 0)),
            pl.BlockSpec((rows, cols), lambda i: (0, 0)),
            pl.BlockSpec((rows, cols), lambda i: (0, 0)),
        ],
        out_specs=pl.BlockSpec((1, rows, cols), lambda i: (i // tiles, 0, i % tiles)),
        out_shape=jax.ShapeDtypeStruct((3, rows, width), jnp.bfloat16),
        name="qkv",
    )(norm_one, w_qkv, cosine, sine)


def head_only(values, head):
    width = values.shape[-1]
    if width == HEAD_DIM:
        return values
    lane = lax.broadcasted_iota(jnp.int32, values.shape, 1)
    return jnp.where(lane // HEAD_DIM == head, values, jnp.zeros_like(values))


def attend_slot(q_ref, k_ref, v_ref, bias, out_ref, wide_ref, lse_ref, chunk):
    seq, width = k_ref.shape
    heads = width // HEAD_DIM
    keys = [head_only(k_ref[...], h) for h in range(heads)]
    values = [head_only(v_ref[...], h) for h in range(heads)]

    def step(i, _):
        rows = pl.ds(pl.multiple_of(i * chunk, chunk), chunk)
        query = q_ref[rows, :] * jnp.bfloat16(0.125)
        total = None
        stats = None
        for h in range(heads):
            scores = transposed(query, keys[h]) + bias
            top = jnp.max(scores, axis=-1, keepdims=True)
            weights = jnp.exp(scores - top)
            norm = jnp.sum(weights, axis=-1, keepdims=True)
            low = (weights * (1.0 / norm)).astype(jnp.bfloat16)
            part = jnp.dot(low, values[h], preferred_element_type=jnp.float32)
            lse = jnp.broadcast_to(top + jnp.log(norm), (chunk, width))
            total = part if total is None else total + part
            if stats is None:
                stats = lse
            else:
                lane = lax.broadcasted_iota(jnp.int32, lse.shape, 1)
                stats = jnp.where(lane // HEAD_DIM == h, lse, stats)
        out_ref[rows, :] = total.astype(jnp.bfloat16)
        wide_ref[rows, :] = total
        lse_ref[rows, :] = stats
        return 0

    lax.fori_loop(0, seq // chunk, step, 0)


def attend_back_slot(
    q_ref, k_ref, v_ref, g_ref, wide_ref, lse_ref, bias, cos, sin, dq_ref, dk_ref, dv_ref, acc_k, acc_v, chunk
):
    seq, width = k_ref.shape
    heads = width // HEAD_DIM
    keys = [head_only(k_ref[...], h) for h in range(heads)]
    values = [head_only(v_ref[...], h) for h in range(heads)]
    acc_k[...] = jnp.zeros_like(acc_k)
    acc_v[...] = jnp.zeros_like(acc_v)

    def turned_back(grad, rows):
        return grad * cos[rows, :] - half_turned(grad) * sin[rows, :]

    def step(i, _):
        rows = pl.ds(pl.multiple_of(i * chunk, chunk), chunk)
        query = q_ref[rows, :]
        grad = g_ref[rows, :]
        lse_all = lse_ref[rows, :]
        both = grad.astype(jnp.float32) * wide_ref[rows, :]
        total = None
        for h in range(heads):
            lse = lse_all[:, h * HEAD_DIM : h * HEAD_DIM + 1]
            delta = jnp.sum(head_only(both, h), axis=-1, keepdims=True)
            scores = transposed(query * jnp.bfloat16(0.125), keys[h])
            weights = jnp.exp(scores + (bias - lse))
            back = transposed(grad, values[h])
            low = (weights * (back - delta)).astype(jnp.bfloat16)
            part = jnp.dot(low, keys[h], preferred_element_type=jnp.float32)
            total = part if total is None else total + part
            acc_v[...] += leading(weights.astype(jnp.bfloat16), head_only(grad, h))
            acc_k[...] += leading(low, head_only(query, h))
        dq_ref[rows, :] = turned_back(total * 0.125, rows).astype(jnp.bfloat16)
        return 0

    lax.fori_loop(0, seq // chunk, step, 0)
    every = slice(None)
    dk_ref[...] = turned_back(acc_k[...] * 0.125, every).astype(jnp.bfloat16)
    dv_ref[...] = acc_v[...].astype(jnp.bfloat16)


def attend_kernel(slots, chunk, qkv_ref, bias_ref, out_ref, wide_ref, lse_ref):
    for s in range(slots):
        attend_slot(
            qkv_ref.at[0, s], qkv_ref.at[1, s], qkv_ref.at[2, s], bias_ref[s],
            out_ref.at[s], wide_ref.at[s], lse_ref.at[s], chunk,
        )


def attend_call(qkv, bias):
    _, slots, seq, width = qkv.shape
    chunk = 256
    return pl.pallas_call(
        functools.partial(attend_kernel, slots, chunk),
        out_shape=(
            jax.ShapeDtypeStruct((slots, seq, width), jnp.bfloat16),
            jax.ShapeDtypeStruct((slots, seq, width), jnp.float32),
            jax.ShapeDtypeStruct((slots, seq, width), jnp.float32),
        ),
        compiler_params=pltpu.CompilerParams(vmem_limit_bytes=VMEM_BYTES),
        name="attend",
    )(qkv, bias)


def attend_back_kernel(slots, chunk, qkv_ref, g_ref, wide_ref, lse_ref, bias_ref, cos_ref, sin_ref, out_ref, acc_k, acc_v):
    for s in range(slots):
        attend_back_slot(
            qkv_ref.at[0, s], qkv_ref.at[1, s], qkv_ref.at[2, s], g_ref.at[s],
            wide_ref.at[s], lse_ref.at[s], bias_ref[s], cos_ref, sin_ref,
            out_ref.at[0, s], out_ref.at[1, s], out_ref.at[2, s], acc_k, acc_v, chunk,
        )


def attend_back_call(qkv, grad_heads, wide, lse, bias, cosine, sine):
    _, slots, seq, width = qkv.shape
    chunk = 256
    return pl.pallas_call(
        functools.partial(attend_back_kernel, slots, chunk),
        out_shape=jax.ShapeDtypeStruct(qkv.shape, jnp.bfloat16),
        scratch_shapes=[pltpu.VMEM((seq, width), jnp.float32)] * 2,
        compiler_params=pltpu.CompilerParams(vmem_limit_bytes=VMEM_BYTES),
        name="attend_back",
    )(qkv, grad_heads, wide, lse, bias, cosine, sine)


def adam_kernel(per, unit_ref, a_ref, b_ref, *refs):
    grads = (refs[:per], refs[per : 2 * per])
    master, first, second, new_master, new_first, new_second = refs[2 * per :]
    for j in range(per):
        slot = pl.program_id(0) * per + j
        unit = unit_ref[slot]
        grad = jnp.where(unit == 0, grads[0][j][0], grads[1][j][0]).astype(jnp.float32)
        grad = jnp.where(unit >= 0, grad, 0.0)
        weight, one, two = adam_update(
            master[j], grad, first[j], second[j], rate_matrix, decay_matrix
        )
        new_master[j] = weight
        new_first[j] = one
        new_second[j] = two


def adam_call(kind, at_a, at_b, grads_a, grads_b, master, first, second):
    capacity, rows, width = master.shape
    per = max(p for p in range(1, 8) if capacity % p == 0)

    def unit_spec(j, chunk):
        return pl.BlockSpec(
            (1, rows, width), lambda i, kind, *at: (at[chunk][i * per + j], 0, 0)
        )

    slot_spec = pl.BlockSpec((per, rows, width), lambda i, kind, *at: (i, 0, 0))
    return pl.pallas_call(
        functools.partial(adam_kernel, per),
        grid_spec=pltpu.PrefetchScalarGridSpec(
            num_scalar_prefetch=3,
            grid=(capacity // per,),
            in_specs=[unit_spec(j, c) for c in range(2) for j in range(per)] + [slot_spec] * 3,
            out_specs=[slot_spec] * 3,
        ),
        out_shape=[jax.ShapeDtypeStruct(master.shape, jnp.float32)] * 3,
        compiler_params=pltpu.CompilerParams(vmem_limit_bytes=VMEM_BYTES),
        name="adamw",
    )(kind, at_a, at_b, *([grads_a] * per), *([grads_b] * per), master, first, second)


def place():
    ctx, shard = lax.axis_index("ctx"), lax.axis_index("shard")
    return ctx // 2, ctx % 2, shard // 2, shard % 2


def device_at(z, y, x, core):
    return (z * 2 + y, x * 2 + core)


def piece_at(zb, c, h, a, b):
    return (((zb * 2 + c) * 2 + h) * 2 + a) * 2 + b


def remote(src, dst, send, recv, device):
    return pltpu.make_async_remote_copy(
        src_ref=src, dst_ref=dst, send_sem=send, recv_sem=recv, device_id=device, device_id_type=MESH
    )


def greet(devices):
    barrier = pltpu.get_barrier_semaphore()
    for device in devices:
        pl.semaphore_signal(barrier, inc=1, device_id=device, device_id_type=MESH)
    pl.semaphore_wait(barrier, len(devices))


GATHER_SEMS = [DMA((2,)), DMA((2, 4, 2)), DMA((2, 4, 2)), DMA((2, 4)), DMA((2, 4)), DMA((2, 4, 2)), DMA((2, 4, 2)), DMA((4,)), DMA((4,))]

class Gather:
    def __init__(self, own, buf, sems):
        self.own, self.buf = own, buf
        self.lsem, self.zs, self.zr, self.fs, self.fr, self.ts, self.tr, self.ss, self.sr = sems
        self.z, self.y, self.x, self.core = place()
        z, y, x, core = self.z, self.y, self.x, self.core
        self.xn = device_at(z, y, 1 - x, core)
        self.yn = device_at(z, 1 - y, x, core)
        self.sib = device_at(z, y, x, 1 - core)
    def side(self, h):
        return (self.y, self.x) if h == 0 else (self.x, self.y)
    def near(self, h):
        return (self.xn, self.yn) if h == 0 else (self.yn, self.xn)
    def keep(self, h):
        a, b = self.side(h)
        return pltpu.make_async_copy(self.own.at[h], self.buf.at[piece_at(self.z, self.core, h, a, b)], self.lsem.at[h])
    def up(self, d, h, step, src=None):
        a, b = self.side(h)
        ref = self.buf.at[piece_at(self.z + d, self.core, h, a, b)]
        k = 0 if step > 0 else 1
        hop = -d if step > 0 else d
        return remote(ref if src is None else src, ref, self.zs.at[k, hop, h], self.zr.at[k, hop, h],
                      device_at(self.z + step, self.y, self.x, self.core))
    def got(self, d, h):
        a, b = self.side(h)
        ref = self.buf.at[piece_at(self.z + d, self.core, h, a, b)]
        k = 0 if d < 0 else 1
        hop = abs(d) - 1
        remote(ref, ref, self.zs.at[k, hop, h], self.zr.at[k, hop, h], self.xn).wait_recv()
    def first(self, zb, h, mine, src=None):
        a, b = self.side(h)
        b = b if mine else 1 - b
        ref = self.buf.at[piece_at(zb, self.core, h, a, b)]
        return remote(ref if src is None else src, ref, self.fs.at[h, zb], self.fr.at[h, zb], self.near(h)[0])
    def second(self, zb, h, j, mine, src=None):
        a, b = self.side(h)
        a = a if mine else 1 - a
        b = b if j == 0 else 1 - b
        if True:
            ref = self.buf.at[piece_at(zb, self.core, h, a, b)]
        return remote(ref if src is None else src, ref, self.ts.at[h, zb, j], self.tr.at[h, zb, j], self.near(h)[1])
    def whole(self, zb, c):
        ref = self.buf.at[pl.ds((zb * 2 + c) * 8, 8)]
        return remote(ref, ref, self.ss.at[zb], self.sr.at[zb], self.sib)
    def start(self):
        for h in range(2):
            self.keep(h).start()
        for h in range(2):
            @pl.when(self.z < 3)
            def _():
                self.up(0, h, 1, self.own.at[h]).start()
            @pl.when(self.z > 0)
            def _():
                self.up(0, h, -1, self.own.at[h]).start()
            self.first(self.z, h, True, self.own.at[h]).start()
        for h in range(2):
            self.second(self.z, h, 0, True, self.own.at[h]).start()
        for h in range(2):
            self.keep(h).wait()
    def line(self, d, z_ok=None):
        def work():
            zb = self.z + d
            for h in range(2):
                self.got(d, h)
                if d < 0:
                    @pl.when(self.z < 3)
                    def _():
                        self.up(d, h, 1).start()
                else:
                    @pl.when(self.z > 0)
                    def _():
                        self.up(d, h, -1).start()
                self.first(zb, h, True).start()
            for h in range(2):
                self.second(zb, h, 0, True).start()
        self.there(d, work)
    def there(self, d, work):
        if d == 0:
            work()
        else:
            pl.when((self.z + d >= 0) & (self.z + d < 4))(work)
    def cross(self, d):
        def work():
            zb = self.z + d
            for h in range(2):
                self.first(zb, h, False).wait_recv()
                self.second(zb, h, 1, True).start()
        self.there(d, work)
    def close(self, d):
        def work():
            zb = self.z + d
            for h in range(2):
                for j in range(2):
                    self.second(zb, h, j, False).wait_recv()
            self.whole(zb, self.core).start()
        self.there(d, work)
    def finish(self):
        for h in range(2):
            for d in range(4):
                @pl.when((self.z - d >= 0) & (self.z < 3))
                def _():
                    self.up(-d, h, 1).wait_send()
                @pl.when((self.z + d < 4) & (self.z > 0))
                def _():
                    self.up(d, h, -1).wait_send()
        for zb in range(4):
            for h in range(2):
                self.first(zb, h, True).wait_send()
                for j in range(2):
                    self.second(zb, h, j, True).wait_send()
            self.whole(zb, self.core).wait_send()
            self.whole(zb, 1 - self.core).wait_recv()


def reduce_scratch(rows, width):
    buf = lambda n: pltpu.VMEM((n, rows, width), jnp.bfloat16)
    return [buf(32), buf(32), buf(16), buf(8), buf(6),
            DMA((4,)), DMA((4,)), DMA((4,)), DMA((4, 2)), DMA((4, 2)), DMA((4, 2)), DMA((4, 2)), DMA((4, 2)), DMA((4, 2))]

class Reduce:
    def __init__(self, partial, refs):
        self.partial = partial
        (self.acc, self.got0, self.got1, self.got2, self.got3,
         self.lsem, self.s0, self.r0, self.s1, self.r1, self.s2, self.r2, self.s3, self.r3) = refs
        self.z, self.y, self.x, self.core = z, y, x, core = place()
        self.xn = device_at(z, y, 1 - x, core)
        self.yn = device_at(z, 1 - y, x, core)
        self.sib = device_at(z, y, x, 1 - core)
        self.rows = partial.shape[1]
    def zb(self, t):
        return (self.z + (2, 1, 3, 0)[t]) % 4
    def side(self, h):
        return (self.y, self.x) if h == 0 else (self.x, self.y)
    def near(self, h):
        return (self.yn, self.xn) if h == 0 else (self.xn, self.yn)
    def send0(self, t):
        zb = self.zb(t)
        return remote(self.partial.at[pl.ds((zb * 2 + 1 - self.core) * 8, 8)], self.got0.at[pl.ds(zb * 8, 8)], self.s0.at[zb], self.r0.at[zb], self.sib)
    def keep(self, t):
        zb = self.zb(t)
        return pltpu.make_async_copy(self.partial.at[pl.ds((zb * 2 + self.core) * 8, 8)], self.acc.at[pl.ds(zb * 8, 8)], self.lsem.at[zb])
    def send1(self, t, h):
        zb = self.zb(t)
        a, b = self.side(h)
        return remote(self.acc.at[pl.ds(zb * 8 + h * 4 + (1 - a) * 2, 2)], self.got1.at[pl.ds(zb * 4 + h * 2, 2)], self.s1.at[zb, h], self.r1.at[zb, h], self.near(h)[0])
    def send2(self, t, h):
        zb = self.zb(t)
        a, b = self.side(h)
        return remote(self.acc.at[zb * 8 + h * 4 + a * 2 + 1 - b], self.got2.at[zb * 2 + h], self.s2.at[zb, h], self.r2.at[zb, h], self.near(h)[1])
    def send3(self, t, h):
        zb = self.zb(t)
        a, b = self.side(h)
        d = (2, 1, 3)[t]
        return remote(self.acc.at[zb * 8 + h * 4 + a * 2 + b], self.got3.at[(d - 1) * 2 + h], self.s3.at[d - 1, h], self.r3.at[d - 1, h], device_at(zb, self.y, self.x, self.core))
    def add(self, dst, src, count):
        ref, at = src
        step = 32
        tiles = self.rows // step
        def body(i, _):
            p, r = i // tiles, (i % tiles) * step
            rows = pl.ds(pl.multiple_of(r, step), step)
            self.acc[dst + p, rows, :] = self.acc[dst + p, rows, :] + ref[at + p, rows, :]
            return 0
        lax.fori_loop(0, count * tiles, body, 0)
    def start(self):
        for t in range(4):
            self.send0(t).start()
            self.keep(t).start()
    def add0(self, t):
        zb = self.zb(t)
        self.keep(t).wait()
        self.send0(t).wait_recv()
        for h in range(2):
            a, b = self.side(h)
            lo = h * 4 + (1 - a) * 2
            self.add(zb * 8 + lo, (self.got0, zb * 8 + lo), 2)
            self.send1(t, h).start()
        for h in range(2):
            a, b = self.side(h)
            lo = h * 4 + a * 2
            self.add(zb * 8 + lo, (self.got0, zb * 8 + lo), 2)
    def add1(self, t):
        zb = self.zb(t)
        for h in range(2):
            a, b = self.side(h)
            self.send1(t, h).wait_recv()
            lo = h * 4 + a * 2
            self.add(zb * 8 + lo + 1 - b, (self.got1, zb * 4 + h * 2 + 1 - b), 1)
            self.send2(t, h).start()
            self.add(zb * 8 + lo + b, (self.got1, zb * 4 + h * 2 + b), 1)
    def add2(self, t):
        zb = self.zb(t)
        for h in range(2):
            a, b = self.side(h)
            self.send2(t, h).wait_recv()
            self.add(zb * 8 + h * 4 + a * 2 + b, (self.got2, zb * 2 + h), 1)
            if t < 3:
                self.send3(t, h).start()
    def add3(self):
        for t in range(3):
            for h in range(2):
                self.send3(t, h).wait_recv()
        step = 32
        for h in range(2):
            a, b = self.side(h)
            at = self.z * 8 + h * 4 + a * 2 + b
            def body(i, _):
                rows = pl.ds(pl.multiple_of(i * step, step), step)
                total = self.acc[at, rows, :].astype(jnp.float32)
                for q in range(3):
                    total = total + self.got3[q * 2 + h, rows, :].astype(jnp.float32)
                self.acc[at, rows, :] = total.astype(jnp.bfloat16)
                return 0
            lax.fori_loop(0, self.rows // step, body, 0)
    def own(self, h):
        a, b = self.side(h)
        return self.acc.at[self.z * 8 + h * 4 + a * 2 + b]
    def finish(self):
        for t in range(4):
            self.send0(t).wait_send()
            for h in range(2):
                self.send1(t, h).wait_send()
                self.send2(t, h).wait_send()
                if t < 3:
                    self.send3(t, h).wait_send()

class Own:
    def __init__(self, get): self.at = self; self.get = get
    def __getitem__(self, h): return self.get(h)


def line_neighbours():
    z, y, x, core = place()
    return [device_at(z, y, 1 - x, core), device_at(z, 1 - y, x, core), device_at(z, y, x, 1 - core)] + [
        device_at((z + d) % 4, y, x, core) for d in (1, 2, 3)
    ]


def run_gathers(first, second):
    pair = (first, second)
    for g in pair:
        g.start()
    for g in pair:
        g.line(-1), g.line(1), g.cross(0)
    for g in pair:
        g.line(-2), g.line(2), g.cross(-1), g.cross(1), g.close(0)
    for g in pair:
        g.line(-3), g.line(3), g.cross(-2), g.cross(2), g.close(-1), g.close(1)
    for g in pair:
        g.cross(-3), g.cross(3), g.close(-2), g.close(2)
    for g in pair:
        g.close(-3), g.close(3)
    for g in pair:
        g.finish()


def spread_kernel(a_ref, b_ref, oa_ref, ob_ref, got_a, got_b, new_a, new_b, own_a, own_b, send, recv, *sems):
    z, y, x, core = place()
    m = len(GATHER_SEMS)
    ga = Gather(own_a, oa_ref, sems[:m])
    gb = Gather(own_b, ob_ref, sems[m:])
    greet(line_neighbours())
    jobs = ((a_ref, got_a, new_a, own_a), (b_ref, got_b, new_b, own_b))

    def to_core(i):
        given, got, new, own = jobs[i]
        return remote(given.at[1 - core], got, send.at[i], recv.at[i], ga.sib)

    def to_x(i):
        given, got, new, own = jobs[i]
        return remote(got.at[1 - x], new, send.at[2 + i], recv.at[2 + i], ga.xn)

    for i in range(2):
        to_core(i).start()
    for i in range(2):
        given, got, new, own = jobs[i]
        to_core(i).wait_recv()
        got[1 - x] = got[1 - x] + given[core, 1 - x]
        to_x(i).start()
        own[...] = got[x] + given[core, x]
    for i in range(2):
        given, got, new, own = jobs[i]
        to_x(i).wait_recv()
        own[...] = own[...] + new[...]
    run_gathers(ga, gb)
    for i in range(2):
        to_core(i).wait_send()
        to_x(i).wait_send()


def spread_call(given_a, given_b, collective_id):
    scratch = []
    for lead in (1, 0, 0):
        for g in (given_a, given_b):
            scratch.append(pltpu.VMEM(g.shape[1:] if lead else g.shape[2:], g.dtype))
    vmem = pl.BlockSpec(memory_space=pltpu.VMEM)
    any_ = pl.BlockSpec(memory_space=pl.ANY)
    return pl.pallas_call(
        spread_kernel,
        out_shape=tuple(
            jax.ShapeDtypeStruct((64,) + g.shape[3:], g.dtype) for g in (given_a, given_b)
        ),
        in_specs=[vmem] * 2,
        out_specs=(any_,) * 2,
        scratch_shapes=scratch + [DMA((4,)), DMA((4,))] + GATHER_SEMS * 2,
        compiler_params=pltpu.CompilerParams(
            collective_id=collective_id, has_side_effects=True, vmem_limit_bytes=VMEM_BYTES
        ),
        name="spread_units",
    )(given_a, given_b)


GAIN_SEMS = [DMA((6,)), DMA((6,))]


class GainSum:
    def __init__(self, ref, got, line, sems):
        self.ref, self.got, self.all = ref, got, line
        self.send, self.recv = sems
        self.z, self.y, self.x, self.core = place()

    def step(self, i):
        z, y, x, core = self.z, self.y, self.x, self.core
        to = (device_at(z, y, x, 1 - core), device_at(z, y, 1 - x, core), device_at(z, 1 - y, x, core))[i]
        return remote(self.ref, self.got.at[i], self.send.at[i], self.recv.at[i], to)

    def far(self, d):
        to = device_at((self.z + d) % 4, self.y, self.x, self.core)
        return remote(self.ref, self.all.at[self.z], self.send.at[2 + d], self.recv.at[2 + d], to)

    def begin(self, i):
        self.step(i).start()

    def end(self, i):
        self.step(i).wait()
        self.ref[...] = self.ref[...] + self.got[i]

    def begin_far(self):
        for d in (1, 2, 3):
            self.far(d).start()
        self.all[self.z] = self.ref[...]

    def end_far(self, out):
        for d in (1, 2, 3):
            self.far(d).wait()
        total = self.all[0]
        for i in range(1, 4):
            total = total + self.all[i]
        out[...] = total


def sum_kernel(a_ref, b_ref, gain_ref, oa_ref, ob_ref, og_ref, gain, gain_got, gain_all, *refs):
    n = len(reduce_scratch(1, 1))
    m = len(GATHER_SEMS)
    ra, rb = Reduce(a_ref, refs[:n]), Reduce(b_ref, refs[n : 2 * n])
    refs = refs[2 * n :]
    ga, gb = Gather(Own(ra.own), oa_ref, refs[:m]), Gather(Own(rb.own), ob_ref, refs[m : 2 * m])
    gs = GainSum(gain, gain_got, gain_all, refs[2 * m :])
    greet(line_neighbours())
    gain[...] = gain_ref[...]
    gs.begin(0)
    rb.start()
    ra.start()
    for t in range(4):
        rb.add0(t)
    gs.end(0), gs.begin(1)
    rb.add1(0)
    rb.add1(1), rb.add2(0)
    gs.end(1), gs.begin(2)
    rb.add1(2), rb.add2(1)
    ra.add0(0), ra.add0(1)
    gs.end(2), gs.begin_far()
    rb.add1(3), rb.add2(2)
    ra.add0(2), ra.add0(3)
    rb.add2(3)
    ra.add1(0)
    rb.add3()
    gb.start()
    ra.add1(1), ra.add2(0)
    ra.add1(2), ra.add2(1)
    gb.line(-1), gb.line(1)
    ra.add1(3), ra.add2(2)
    gb.cross(0)
    ra.add2(3)
    gb.line(-2), gb.line(2)
    ra.add3()
    gb.cross(-1), gb.cross(1)
    ga.start()
    gb.close(0)
    gb.line(-3), gb.line(3)
    ga.line(-1), ga.line(1)
    gb.cross(-2), gb.cross(2)
    ga.cross(0)
    gb.close(-1), gb.close(1)
    ga.line(-2), ga.line(2)
    gb.cross(-3), gb.cross(3)
    ga.cross(-1), ga.cross(1)
    gb.close(-2), gb.close(2)
    ga.close(0)
    ga.line(-3), ga.line(3)
    gb.close(-3), gb.close(3)
    ga.cross(-2), ga.cross(2)
    ga.close(-1), ga.close(1)
    ga.cross(-3), ga.cross(3)
    ga.close(-2), ga.close(2)
    ga.close(-3), ga.close(3)
    gs.end_far(og_ref)
    ra.finish(), rb.finish(), ga.finish(), gb.finish()


def sum_call(grads_a, grads_b, gain_part, collective_id):
    any_ = pl.BlockSpec(memory_space=pl.ANY)
    vmem = pl.BlockSpec(memory_space=pltpu.VMEM)
    width = grads_a.shape[2]
    gain = gain_part.shape
    return pl.pallas_call(
        sum_kernel,
        out_shape=(
            jax.ShapeDtypeStruct(grads_a.shape, grads_a.dtype),
            jax.ShapeDtypeStruct(grads_b.shape, grads_b.dtype),
            jax.ShapeDtypeStruct(gain, jnp.float32),
        ),
        in_specs=[any_, any_, vmem],
        out_specs=(any_, any_, vmem),
        scratch_shapes=[
            pltpu.VMEM(gain, jnp.float32),
            pltpu.VMEM((3,) + gain, jnp.float32),
            pltpu.VMEM((4,) + gain, jnp.float32),
        ]
        + reduce_scratch(grads_a.shape[1], width)
        + reduce_scratch(grads_b.shape[1], width)
        + GATHER_SEMS * 2
        + GAIN_SEMS,
        compiler_params=pltpu.CompilerParams(
            collective_id=collective_id, has_side_effects=True, vmem_limit_bytes=VMEM_BYTES
        ),
        name="sum_units",
    )(grads_a, grads_b, gain_part)


def swap_kernel(parts, n, x_ref, out_ref, lsem, send, recv):
    ctx, shard = lax.axis_index("ctx"), lax.axis_index("shard")
    rows, width = x_ref.shape[2], out_ref.shape[3]
    greet([(lax.rem(ctx + d, n), shard) for d in range(1, n)])

    def src(to):
        return x_ref.at[:, :, :, pl.ds(pl.multiple_of(to * width, width), width)]

    def dst(owner):
        return out_ref.at[:, :, pl.ds(pl.multiple_of(owner * rows, rows), rows), :]

    def copy(d):
        to = lax.rem(ctx + d, n)
        return remote(src(to), dst(ctx), send.at[d], recv.at[d], (to, shard))

    own = pltpu.make_async_copy(src(ctx), dst(ctx), lsem)
    own.start()
    for d in range(1, n):
        copy(d).start()
    own.wait()
    for d in range(1, n):
        copy(d).wait()


def swap_back_kernel(parts, n, x_ref, out_ref, lsem, send, recv):
    ctx, shard = lax.axis_index("ctx"), lax.axis_index("shard")
    rows, width = out_ref.shape[2], x_ref.shape[3]
    greet([(lax.rem(ctx + d, n), shard) for d in range(1, n)])

    def src(to):
        return x_ref.at[:, :, pl.ds(pl.multiple_of(to * rows, rows), rows), :]

    def dst(owner):
        return out_ref.at[:, :, :, pl.ds(pl.multiple_of(owner * width, width), width)]

    def copy(d):
        to = lax.rem(ctx + d, n)
        return remote(src(to), dst(ctx), send.at[d], recv.at[d], (to, shard))

    own = pltpu.make_async_copy(src(ctx), dst(ctx), lsem)
    own.start()
    for d in range(1, n):
        copy(d).start()
    own.wait()
    for d in range(1, n):
        copy(d).wait()


def swap_call(values, n, back, collective_id, name):
    parts, slots, rows, cols = values.shape
    shape = (parts, slots, rows // n, cols * n) if back else (parts, slots, rows * n, cols // n)
    vmem = pl.BlockSpec(memory_space=pltpu.VMEM)
    return pl.pallas_call(
        functools.partial(swap_back_kernel if back else swap_kernel, parts, n),
        out_shape=jax.ShapeDtypeStruct(shape, values.dtype),
        in_specs=[vmem],
        out_specs=vmem,
        scratch_shapes=[DMA, DMA((n,)), DMA((n,))],
        compiler_params=pltpu.CompilerParams(
            collective_id=collective_id, has_side_effects=True, vmem_limit_bytes=VMEM_BYTES
        ),
        name=name,
    )(values)


def to_heads(values, n, fast, collective_id, name):
    if fast:
        return swap_call(values, n, False, collective_id, name)
    return lax.all_to_all(values, "ctx", split_axis=3, concat_axis=2, tiled=True)


def to_rows(values, n, fast, collective_id, name):
    if fast:
        return swap_call(values, n, True, collective_id, name)
    return lax.all_to_all(values, "ctx", split_axis=2, concat_axis=3, tiled=True)


def shards(
    fast,
    tokens,
    cotangent,
    lengths,
    unit_owner,
    master,
    first_moment,
    second_moment,
    norm_gains,
    gain_first,
    gain_second,
):
    slots, block_len, width = tokens.shape
    groups = lax.axis_size("shard")
    n = lax.axis_size("ctx")
    ctx, shard = lax.axis_index("ctx"), lax.axis_index("shard")
    capacity, unit_rows, _ = master.shape
    units = unit_owner.shape[0]
    rows_all = slots * block_len
    seq = block_len * n
    device_count = n * groups
    my_width = width // n

    split = 4 * width // unit_rows
    rank = unit_places(unit_owner, capacity, groups)

    def share_of(first, count, per, wanted):
        at = wanted[..., None] * per + jnp.arange(per, dtype=jnp.int32)
        unit = first + jnp.minimum(at, count - 1)
        mine = (unit_owner[unit] == shard) & (at < count)
        shape = at.shape[:-1] + (per * unit_rows, width)
        taken = jnp.take(master, rank[unit].reshape(-1), axis=0, mode="clip")
        kept = jnp.where(mine.reshape(-1, 1, 1), taken, 0.0).astype(jnp.bfloat16)
        return kept.reshape(shape)

    chunks = ((0, split), (split, units - split))
    if fast:
        z, y, x, core = place()
        wanted = jnp.stack(
            [
                jnp.stack([jnp.stack([piece_at(z, c, 0, y, q), piece_at(z, c, 1, q, y)]) for q in range(2)])
                for c in range(2)
            ]
        )
        given = [share_of(first, count, -(-count // 64), wanted) for first, count in chunks]
        stack_a, stack_b = spread_call(given[0], given[1], 0)
    else:
        wanted = ctx * groups + jnp.arange(groups, dtype=jnp.int32)
        stacks = []
        for first, count in chunks:
            given = share_of(first, count, -(-count // device_count), wanted)
            own = lax.psum_scatter(given, "shard", scatter_dimension=0, tiled=True)
            stacks.append(lax.all_gather(own, BOTH, axis=0, tiled=True))
        stack_a, stack_b = stacks
    stack_a = stack_a.reshape(-1, width)
    stack_b = stack_b.reshape(-1, width)
    w_out = stack_a[3 * width : 4 * width]
    w_up = stack_b[: 2 * FF]
    w_down = stack_b[2 * FF : 3 * FF]

    positions = ctx * block_len + jnp.arange(block_len, dtype=jnp.int32)
    tile_heads = 256 // HEAD_DIM
    cos_rows, sin_rows = rope_tables(jnp.tile(positions, slots), tile_heads)
    cos_seq, sin_seq = rope_tables(jnp.arange(seq, dtype=jnp.int32), my_width // HEAD_DIM)
    live_rows = (positions[None, :] < lengths[:, None]).astype(jnp.float32)
    bias = jnp.where(
        jnp.arange(seq, dtype=jnp.int32)[None, :] < lengths[:, None], 0.0, mask_fill
    ).astype(jnp.float32)[:, None, :]

    inputs = tokens.astype(jnp.float32).reshape(rows_all, width)
    norm_one = layer_norm(inputs, norm_gains[0]).astype(jnp.bfloat16)
    qkv = qkv_call(norm_one, stack_a, cos_rows, sin_rows)
    qkv_rows = qkv.reshape(3, slots, block_len, width)
    qkv_heads = to_heads(qkv_rows, n, fast, 1, "swap_qkv")
    mixed_heads, wide, lse = attend_call(qkv_heads, bias)
    mixed_low = to_rows(mixed_heads[None], n, fast, 2, "swap_mixed").reshape(rows_all, width)

    middle = inputs + transposed(mixed_low, w_out)
    norm_two = layer_norm(middle, norm_gains[1]).astype(jnp.bfloat16)
    upper_proj = transposed(norm_two, w_up)
    hidden_low = gated_gelu(upper_proj).astype(jnp.bfloat16)
    result = middle + jnp.dot(hidden_low, w_down, preferred_element_type=jnp.float32)
    output = result.astype(jnp.bfloat16).reshape(slots, block_len, width)

    grad_result = cotangent.astype(jnp.float32).reshape(rows_all, width) * live_rows.reshape(
        rows_all, 1
    )
    grad_down_low = grad_result.astype(jnp.bfloat16)
    grad_w_down = leading(hidden_low, grad_down_low)
    grad_hidden = transposed(grad_down_low, w_down)
    _, gelu_back = jax.vjp(gated_gelu, upper_proj)
    grad_upper_low = gelu_back(grad_hidden)[0].astype(jnp.bfloat16)
    grad_w_up = leading(grad_upper_low, norm_two)
    grad_norm_two = jnp.dot(grad_upper_low, w_up, preferred_element_type=jnp.float32)
    _, norm_back_two = jax.vjp(layer_norm, middle, norm_gains[1])
    grad_middle_part, grad_gain_two = norm_back_two(grad_norm_two)
    grad_middle = grad_result + grad_middle_part
    grad_attn_low = grad_middle.astype(jnp.bfloat16)
    grad_w_out = leading(grad_attn_low, mixed_low)
    grad_heads_rows = jnp.dot(grad_attn_low, w_out, preferred_element_type=jnp.float32).astype(
        jnp.bfloat16
    )
    grad_heads = to_heads(
        grad_heads_rows.reshape(1, slots, block_len, width), n, fast, 3, "swap_grad"
    )[0]
    grad_qkv_heads = attend_back_call(qkv_heads, grad_heads, wide, lse, bias, cos_seq, sin_seq)
    grad_qkv_rows = to_rows(grad_qkv_heads, n, fast, 4, "swap_grad_qkv")
    grad_qkv_low = grad_qkv_rows.reshape(3, rows_all, width)
    grad_norm_one = sum(
        jnp.dot(
            grad_qkv_low[i],
            stack_a[i * width : (i + 1) * width],
            preferred_element_type=jnp.float32,
        )
        for i in range(3)
    )
    _, norm_back_one = jax.vjp(layer_norm, inputs, norm_gains[0])
    grad_input_part, grad_gain_one = norm_back_one(grad_norm_one)
    token_grad = (
        (grad_middle + grad_input_part).astype(jnp.bfloat16).reshape(slots, block_len, width)
    )

    low = jnp.bfloat16
    grads_a = jnp.concatenate(
        [leading(grad_qkv_low[i], norm_one).astype(low) for i in range(3)]
        + [grad_w_out.astype(low)]
        + [jnp.zeros((stack_a.shape[0] - split * unit_rows, width), low)],
        axis=0,
    )
    grads_b = jnp.concatenate(
        [
            grad_w_up.astype(low),
            grad_w_down.astype(low),
            jnp.zeros((stack_b.shape[0] - (units - split) * unit_rows, width), low),
        ],
        axis=0,
    )
    gain_part = jnp.zeros((8, width), jnp.float32).at[:2].set(
        jnp.stack([grad_gain_one, grad_gain_two])
    )
    if fast:
        all_a, all_b, gain_grad = sum_call(
            grads_a.reshape(64, -1, width), grads_b.reshape(64, -1, width), gain_part, 5
        )
    else:
        all_a, all_b = (
            lax.all_gather(
                lax.psum_scatter(g, BOTH, scatter_dimension=0, tiled=True), BOTH, axis=0, tiled=True
            )
            for g in (grads_a, grads_b)
        )
        gain_grad = lax.psum(gain_part, BOTH)
    gain_grad = gain_grad[:2]
    all_a = all_a.reshape(-1, unit_rows, width)
    all_b = all_b.reshape(-1, unit_rows, width)

    slot_index = jnp.where(unit_owner == shard, rank, capacity)
    unit_of_slot = (
        jnp.full((capacity + 1,), -1, jnp.int32)
        .at[slot_index]
        .set(jnp.arange(units, dtype=jnp.int32))[:capacity]
    )
    kind = jnp.where(unit_of_slot < 0, -1, (unit_of_slot >= split).astype(jnp.int32))
    at_a = jnp.maximum(lax.cummax(jnp.where(kind == 0, unit_of_slot, -1)), 0)
    at_b = jnp.maximum(lax.cummax(jnp.where(kind == 1, unit_of_slot, -1)) - split, 0)
    new_master, new_first, new_second = adam_call(
        kind, at_a, at_b, all_a, all_b, master, first_moment, second_moment
    )
    new_gains, new_gain_first, new_gain_second = adam_update(
        norm_gains, gain_grad, gain_first, gain_second, rate_gain, 0.0
    )
    return (
        output,
        token_grad,
        new_master,
        new_first,
        new_second,
        new_gains,
        new_gain_first,
        new_gain_second,
    )


def solution(mesh):
    fast = dict(mesh.shape) == {"ctx": 8, "shard": 4}
    return jax.shard_map(
        functools.partial(shards, fast),
        mesh=mesh,
        in_specs=(
            P("shard", "ctx", None),
            P("shard", "ctx", None),
            P("shard"),
            P(),
            P("shard", None, None),
            P("shard", None, None),
            P("shard", None, None),
            P(),
            P(),
            P(),
        ),
        out_specs=(
            P("shard", "ctx", None),
            P("shard", "ctx", None),
            P("shard", None, None),
            P("shard", None, None),
            P("shard", None, None),
            P(),
            P(),
            P(),
        ),
        check_vma=False,
    )
```

```python
import functools

import jax
import jax.numpy as jnp
from jax import lax
from jax.experimental import pallas as pl
from jax.experimental.pallas import tpu as pltpu
from jax.sharding import PartitionSpec as P

HEADS = 16
HEAD_DIM = 64
FF = 2624
FF_WIDE = -(-FF // 128) * 128
STEP = 10
MESH = pl.DeviceIdType.MESH
DMA = pltpu.SemaphoreType.DMA

eps_norm = 1e-05
rope_base = 160000.0
mask_fill = -1e30
beta_one = 0.9
beta_two = 0.98
adam_eps = 1e-06
rate_matrix = 0.03
rate_gain = 0.6
decay_matrix = 0.01
BOTH = ("ctx", "shard")
VMEM_BYTES = 60 * 2**20


def transposed(left, right):
    return lax.dot_general(
        left, right, (((1,), (1,)), ((), ())), preferred_element_type=jnp.float32
    )


def leading(left, right):
    return lax.dot_general(
        left, right, (((0,), (0,)), ((), ())), preferred_element_type=jnp.float32
    )


def layer_norm(values, gain):
    row_mean = jnp.mean(values, axis=-1, keepdims=True)
    centred = values - row_mean
    variance = jnp.mean(centred * centred, axis=-1, keepdims=True)
    return centred * lax.rsqrt(variance + eps_norm) * gain


def rope_tables(positions, heads):
    half_dim = HEAD_DIM // 2
    inverse = rope_base ** (-2.0 * jnp.arange(half_dim, dtype=jnp.float32) / HEAD_DIM)
    angles = positions.astype(jnp.float32)[:, None] * inverse[None, :]
    cosine, sine = jnp.cos(angles), jnp.sin(angles)
    cosine = jnp.concatenate([cosine, cosine] * heads, axis=1)
    sine = jnp.concatenate([-sine, sine] * heads, axis=1)
    return (cosine, sine)


def half_turned(values):
    width = values.shape[-1]
    half = HEAD_DIM // 2
    lane = lax.broadcasted_iota(jnp.int32, values.shape, values.ndim - 1)
    if width == HEAD_DIM:
        return jnp.concatenate([values[:, half:], values[:, :half]], axis=1)
    ahead = pltpu.roll(values, width - half, axis=1)
    behind = pltpu.roll(values, half, axis=1)
    return jnp.where(lane % HEAD_DIM < half, ahead, behind)


def unit_places(unit_owner, chosen):
    every = jnp.arange(unit_owner.shape[0], dtype=jnp.int32)
    owner = jnp.sum(jnp.where(every == chosen[:, None], unit_owner, 0), axis=1)
    below = (every < chosen[:, None]) & (unit_owner == owner[:, None])
    return owner, jnp.sum(below.astype(jnp.int32), axis=1)


def gated_gelu(upper_proj):
    return jax.nn.gelu(upper_proj[:, :FF_WIDE], approximate=False) * upper_proj[:, FF_WIDE:]


def adam_update(weight, gradient, first_old, second_old, step_rate, weight_decay):
    first_new = beta_one * first_old + (1.0 - beta_one) * gradient
    second_new = beta_two * second_old + (1.0 - beta_two) * gradient * gradient
    first_fix = 1.0 - beta_one**STEP
    second_fix = 1.0 - beta_two**STEP
    adam_step = first_new / first_fix / (jnp.sqrt(second_new / second_fix) + adam_eps)
    return (weight - step_rate * (adam_step + weight_decay * weight), first_new, second_new)


def qkv_kernel(norm_ref, w_ref, cos_ref, sin_ref, out_ref):
    tile = pl.program_id(0)
    turned_tiles = 2 * pl.num_programs(0) // 3
    values = transposed(norm_ref[...], w_ref[...])

    @pl.when(tile < turned_tiles)
    def _():
        out_ref[0] = (values * cos_ref[...] + half_turned(values) * sin_ref[...]).astype(
            out_ref.dtype
        )

    @pl.when(tile >= turned_tiles)
    def _():
        out_ref[0] = values.astype(out_ref.dtype)


def qkv_call(norm_one, w_qkv, cosine, sine):
    rows, width = norm_one.shape
    cols = 256
    tiles = width // cols
    return pl.pallas_call(
        qkv_kernel,
        grid=(3 * width // cols,),
        in_specs=[
            pl.BlockSpec((rows, width), lambda i: (0, 0)),
            pl.BlockSpec((cols, width), lambda i: (i, 0)),
            pl.BlockSpec((rows, cols), lambda i: (0, 0)),
            pl.BlockSpec((rows, cols), lambda i: (0, 0)),
        ],
        out_specs=pl.BlockSpec((1, rows, cols), lambda i: (i // tiles, 0, i % tiles)),
        out_shape=jax.ShapeDtypeStruct((3, rows, width), jnp.bfloat16),
        name="qkv",
    )(norm_one, w_qkv, cosine, sine)


def head_only(values, head):
    width = values.shape[-1]
    if width == HEAD_DIM:
        return values
    lane = lax.broadcasted_iota(jnp.int32, values.shape, 1)
    return jnp.where(lane // HEAD_DIM == head, values, jnp.zeros_like(values))


def attend_step(i, q_ref, k_ref, v_ref, bias, out_ref, wide_ref, lse_ref, chunk):
    width = k_ref.shape[1]
    heads = width // HEAD_DIM
    rows = pl.ds(pl.multiple_of(i * chunk, chunk), chunk)
    query = q_ref[rows, :] * jnp.bfloat16(0.125)
    total = None
    stats = None
    for h in range(heads):
        scores = transposed(query, head_only(k_ref[...], h)) + bias
        top = jnp.max(scores, axis=-1, keepdims=True)
        weights = jnp.exp(scores - top)
        norm = jnp.sum(weights, axis=-1, keepdims=True)
        low = (weights * (1.0 / norm)).astype(jnp.bfloat16)
        part = jnp.dot(low, head_only(v_ref[...], h), preferred_element_type=jnp.float32)
        lse = jnp.broadcast_to(top + jnp.log(norm), (chunk, width))
        total = part if total is None else total + part
        if stats is None:
            stats = lse
        else:
            lane = lax.broadcasted_iota(jnp.int32, lse.shape, 1)
            stats = jnp.where(lane // HEAD_DIM == h, lse, stats)
    out_ref[rows, :] = total.astype(jnp.bfloat16)
    wide_ref[rows, :] = total
    lse_ref[rows, :] = stats


def attend_slot(*args):
    def step(i, _):
        attend_step(i, *args)
        return 0

    lax.fori_loop(0, args[1].shape[0] // args[-1], step, 0)


def turned_back(grad, cos, sin):
    return grad * cos - half_turned(grad) * sin


def attend_back_step(
    i, q_ref, k_ref, v_ref, g_ref, wide_ref, lse_ref, bias, cos, sin, dq_ref, dk_ref, dv_ref, acc_k, acc_v, chunk
):
    seq, width = k_ref.shape
    heads = width // HEAD_DIM
    rows = pl.ds(pl.multiple_of(i * chunk, chunk), chunk)
    query = q_ref[rows, :]
    grad = g_ref[rows, :]
    lse_all = lse_ref[rows, :]
    both = grad.astype(jnp.float32) * wide_ref[rows, :]
    total = None
    for h in range(heads):
        key = head_only(k_ref[...], h)
        lse = lse_all[:, h * HEAD_DIM : h * HEAD_DIM + 1]
        delta = jnp.sum(head_only(both, h), axis=-1, keepdims=True)
        scores = transposed(query * jnp.bfloat16(0.125), key)
        weights = jnp.exp(scores + (bias - lse))
        back = transposed(grad, head_only(v_ref[...], h))
        low = (weights * (back - delta)).astype(jnp.bfloat16)
        part = jnp.dot(low, key, preferred_element_type=jnp.float32)
        total = part if total is None else total + part
        acc_v[...] += leading(weights.astype(jnp.bfloat16), head_only(grad, h))
        acc_k[...] += leading(low, head_only(query, h))
    dq_ref[rows, :] = turned_back(total * 0.125, cos[rows, :], sin[rows, :]).astype(jnp.bfloat16)


def attend_back_end(
    q_ref, k_ref, v_ref, g_ref, wide_ref, lse_ref, bias, cos, sin, dq_ref, dk_ref, dv_ref, acc_k, acc_v, chunk
):
    dk_ref[...] = turned_back(acc_k[...] * 0.125, cos[...], sin[...]).astype(jnp.bfloat16)
    dv_ref[...] = acc_v[...].astype(jnp.bfloat16)


def attend_back_slot(*args):
    acc_k, acc_v, chunk = args[-3:]
    acc_k[...] = jnp.zeros_like(acc_k)
    acc_v[...] = jnp.zeros_like(acc_v)

    def step(i, _):
        attend_back_step(i, *args)
        return 0

    lax.fori_loop(0, args[1].shape[0] // chunk, step, 0)
    attend_back_end(*args)


def attend_kernel(slots, chunk, qkv_ref, bias_ref, out_ref, wide_ref, lse_ref):
    for s in range(slots):
        attend_slot(
            qkv_ref.at[0, s], qkv_ref.at[1, s], qkv_ref.at[2, s], bias_ref[s],
            out_ref.at[s], wide_ref.at[s], lse_ref.at[s], chunk,
        )


def attend_call(qkv, bias):
    _, slots, seq, width = qkv.shape
    chunk = 256
    return pl.pallas_call(
        functools.partial(attend_kernel, slots, chunk),
        out_shape=(
            jax.ShapeDtypeStruct((slots, seq, width), jnp.bfloat16),
            jax.ShapeDtypeStruct((slots, seq, width), jnp.float32),
            jax.ShapeDtypeStruct((slots, seq, width), jnp.float32),
        ),
        compiler_params=pltpu.CompilerParams(vmem_limit_bytes=VMEM_BYTES),
        name="attend",
    )(qkv, bias)


def attend_back_kernel(slots, chunk, qkv_ref, g_ref, wide_ref, lse_ref, bias_ref, cos_ref, sin_ref, out_ref, acc_k, acc_v):
    for s in range(slots):
        attend_back_slot(
            qkv_ref.at[0, s], qkv_ref.at[1, s], qkv_ref.at[2, s], g_ref.at[s],
            wide_ref.at[s], lse_ref.at[s], bias_ref[s], cos_ref, sin_ref,
            out_ref.at[0, s], out_ref.at[1, s], out_ref.at[2, s], acc_k, acc_v, chunk,
        )


def attend_back_call(qkv, grad_heads, wide, lse, bias, cosine, sine):
    _, slots, seq, width = qkv.shape
    chunk = 256
    return pl.pallas_call(
        functools.partial(attend_back_kernel, slots, chunk),
        out_shape=jax.ShapeDtypeStruct(qkv.shape, jnp.bfloat16),
        scratch_shapes=[pltpu.VMEM((seq, width), jnp.float32)] * 2,
        compiler_params=pltpu.CompilerParams(vmem_limit_bytes=VMEM_BYTES),
        name="attend_back",
    )(qkv, grad_heads, wide, lse, bias, cosine, sine)


def adam_kernel(per, unit_ref, a_ref, b_ref, *refs):
    grads = (refs[:per], refs[per : 2 * per])
    master, first, second, new_master, new_first, new_second = refs[2 * per :]
    for j in range(per):
        slot = pl.program_id(0) * per + j
        unit = unit_ref[slot]
        grad = jnp.where(unit == 0, grads[0][j][0], grads[1][j][0]).astype(jnp.float32)
        grad = jnp.where(unit >= 0, grad, 0.0)
        weight, one, two = adam_update(
            master[j], grad, first[j], second[j], rate_matrix, decay_matrix
        )
        new_master[j] = weight
        new_first[j] = one
        new_second[j] = two


def adam_call(kind, at_a, at_b, grads_a, grads_b, master, first, second):
    capacity, rows, width = master.shape
    per = max(p for p in range(1, 8) if capacity % p == 0)

    def unit_spec(j, chunk):
        return pl.BlockSpec(
            (1, rows, width), lambda i, kind, *at: (at[chunk][i * per + j], 0, 0)
        )

    slot_spec = pl.BlockSpec((per, rows, width), lambda i, kind, *at: (i, 0, 0))
    return pl.pallas_call(
        functools.partial(adam_kernel, per),
        grid_spec=pltpu.PrefetchScalarGridSpec(
            num_scalar_prefetch=3,
            grid=(capacity // per,),
            in_specs=[unit_spec(j, c) for c in range(2) for j in range(per)] + [slot_spec] * 3,
            out_specs=[slot_spec] * 3,
        ),
        out_shape=[jax.ShapeDtypeStruct(master.shape, jnp.float32)] * 3,
        compiler_params=pltpu.CompilerParams(vmem_limit_bytes=VMEM_BYTES),
        name="adamw",
    )(kind, at_a, at_b, *([grads_a] * per), *([grads_b] * per), master, first, second)


def pick_kernel(part_ref, master_ref, out_ref, got, sems):
    count, rows = got.shape[:2]

    def at(p):
        return pl.ds(pl.multiple_of(p * rows, rows), rows)

    def copy(p):
        return pltpu.make_async_copy(master_ref.at[part_ref[p]], got.at[p], sems.at[p])

    def start(p, _):
        @pl.when(part_ref[p] >= 0)
        def _():
            copy(p).start()

        return 0

    def end(p, _):
        @pl.when(part_ref[p] >= 0)
        def _():
            copy(p).wait()
            out_ref[at(p), :] = got[p].astype(out_ref.dtype)

        @pl.when(part_ref[p] < 0)
        def _():
            out_ref[at(p), :] = jnp.zeros((rows, out_ref.shape[1]), out_ref.dtype)

        return 0

    lax.fori_loop(0, count, start, 0)
    lax.fori_loop(0, count, end, 0)


def pick_call(part, parts):
    shape = (part.shape[0],) + parts.shape[1:]
    flat = (shape[0] * shape[1], shape[2])
    return pl.pallas_call(
        pick_kernel,
        grid_spec=pltpu.PrefetchScalarGridSpec(
            num_scalar_prefetch=1,
            grid=(1,),
            in_specs=[pl.BlockSpec(memory_space=pl.ANY)],
            out_specs=pl.BlockSpec(flat, lambda i, part: (0, 0)),
            scratch_shapes=[pltpu.VMEM(shape, parts.dtype), DMA((part.shape[0],))],
        ),
        out_shape=jax.ShapeDtypeStruct(flat, jnp.bfloat16),
        compiler_params=pltpu.CompilerParams(vmem_limit_bytes=VMEM_BYTES),
        name="pick",
    )(part, parts)


def place():
    ctx, shard = lax.axis_index("ctx"), lax.axis_index("shard")
    return ctx // 2, ctx % 2, shard // 2, shard % 2


def device_at(z, y, x, core):
    return (z * 2 + y, x * 2 + core)


def piece_at(zb, c, h, a, b):
    return (((zb * 2 + c) * 2 + h) * 2 + a) * 2 + b


def remote(src, dst, send, recv, device):
    return pltpu.make_async_remote_copy(
        src_ref=src, dst_ref=dst, send_sem=send, recv_sem=recv, device_id=device, device_id_type=MESH
    )


def greet(devices):
    barrier = pltpu.get_barrier_semaphore()
    for device in devices:
        pl.semaphore_signal(barrier, inc=1, device_id=device, device_id_type=MESH)
    pl.semaphore_wait(barrier, len(devices))


def line_neighbours():
    z, y, x, core = place()
    return [device_at(z, y, 1 - x, core), device_at(z, 1 - y, x, core), device_at(z, y, x, 1 - core)] + [
        device_at((z + d) % 4, y, x, core) for d in (1, 2, 3)
    ]


def rows_at(ref, piece, count, rows):
    return ref.at[pl.ds(pl.multiple_of(piece * rows, 16), count * rows)]


GATHER_SEMS = [DMA((2,))] + [DMA((2, 4, 2))] * 2 + [DMA((2, 4))] * 2 + [DMA((2, 4, 2))] * 2 + [DMA((4,))] * 2


class Gather:
    def __init__(self, own, buf, rows, sems):
        self.own, self.buf, self.rows = own, buf, rows
        self.lsem, self.zs, self.zr, self.fs, self.fr, self.ts, self.tr, self.ss, self.sr = sems
        self.z, self.y, self.x, self.core = z, y, x, core = place()
        self.xn = device_at(z, y, 1 - x, core)
        self.yn = device_at(z, 1 - y, x, core)
        self.sib = device_at(z, y, x, 1 - core)

    def side(self, h):
        return (self.y, self.x) if h == 0 else (self.x, self.y)

    def near(self, h):
        return (self.xn, self.yn) if h == 0 else (self.yn, self.xn)

    def piece(self, zb, h, a, b):
        return rows_at(self.buf, piece_at(zb, self.core, h, a, b), 1, self.rows)

    def keep(self, h):
        return pltpu.make_async_copy(self.own(h), self.piece(self.z, h, *self.side(h)), self.lsem.at[h])

    def up(self, d, h, step, src=None):
        ref = self.piece(self.z + d, h, *self.side(h))
        k, hop = (0, -d) if step > 0 else (1, d)
        return remote(
            ref if src is None else src,
            ref,
            self.zs.at[k, hop, h],
            self.zr.at[k, hop, h],
            device_at(self.z + step, self.y, self.x, self.core),
        )

    def got(self, d, h):
        ref = self.piece(self.z + d, h, *self.side(h))
        k, hop = (0 if d < 0 else 1), abs(d) - 1
        remote(ref, ref, self.zs.at[k, hop, h], self.zr.at[k, hop, h], self.xn).wait_recv()

    def first(self, zb, h, mine, src=None):
        a, b = self.side(h)
        ref = self.piece(zb, h, a, b if mine else 1 - b)
        return remote(
            ref if src is None else src, ref, self.fs.at[h, zb], self.fr.at[h, zb], self.near(h)[0]
        )

    def second(self, zb, h, j, mine, src=None):
        a, b = self.side(h)
        ref = self.piece(zb, h, a if mine else 1 - a, b if j == 0 else 1 - b)
        return remote(
            ref if src is None else src, ref, self.ts.at[h, zb, j], self.tr.at[h, zb, j], self.near(h)[1]
        )

    def whole(self, zb, c):
        ref = rows_at(self.buf, (zb * 2 + c) * 8, 8, self.rows)
        return remote(ref, ref, self.ss.at[zb], self.sr.at[zb], self.sib)

    def start(self):
        for h in range(2):
            self.keep(h).start()
        for h in range(2):

            @pl.when(self.z < 3)
            def _():
                self.up(0, h, 1, self.own(h)).start()

            @pl.when(self.z > 0)
            def _():
                self.up(0, h, -1, self.own(h)).start()

            self.first(self.z, h, True, self.own(h)).start()
        for h in range(2):
            self.second(self.z, h, 0, True, self.own(h)).start()
        for h in range(2):
            self.keep(h).wait()

    def there(self, d, work):
        if d == 0:
            work()
        else:
            pl.when((self.z + d >= 0) & (self.z + d < 4))(work)

    def line(self, d):
        def work():
            zb = self.z + d
            for h in range(2):
                self.got(d, h)
                if d < 0:

                    @pl.when(self.z < 3)
                    def _():
                        self.up(d, h, 1).start()
                else:

                    @pl.when(self.z > 0)
                    def _():
                        self.up(d, h, -1).start()

                self.first(zb, h, True).start()
            for h in range(2):
                self.second(zb, h, 0, True).start()

        self.there(d, work)

    def cross(self, d):
        def work():
            zb = self.z + d
            for h in range(2):
                self.first(zb, h, False).wait_recv()
                self.second(zb, h, 1, True).start()

        self.there(d, work)

    def close(self, d):
        def work():
            zb = self.z + d
            for h in range(2):
                for j in range(2):
                    self.second(zb, h, j, False).wait_recv()
            self.whole(zb, self.core).start()

        self.there(d, work)

    def finish(self, take=True):
        for h in range(2):
            for d in range(4):

                @pl.when((self.z - d >= 0) & (self.z < 3))
                def _():
                    self.up(-d, h, 1).wait_send()

                @pl.when((self.z + d < 4) & (self.z > 0))
                def _():
                    self.up(d, h, -1).wait_send()

        for zb in range(4):
            for h in range(2):
                self.first(zb, h, True).wait_send()
                for j in range(2):
                    self.second(zb, h, j, True).wait_send()
            self.whole(zb, self.core).wait_send()
            if take:
                self.whole(zb, 1 - self.core).wait_recv()


REDUCE_REFS = 10


def reduce_scratch(rows, width):
    def buf(n):
        return pltpu.VMEM((n * rows, width), jnp.bfloat16)

    return (
        [buf(32), buf(16), buf(8), buf(10)]
        + [DMA((4, 2, 2))] * 2
        + [DMA((4, 2))] * 3
        + [DMA((5, 2))]
    )


class Reduce:
    def __init__(self, rows, refs):
        self.acc, self.got1, self.got2, self.got3 = refs[:4]
        self.s1, self.r1, self.s2, self.r2, self.s3, self.r3 = refs[4:]
        self.rows = rows
        self.z, self.y, self.x, self.core = z, y, x, core = place()
        self.xn = device_at(z, y, 1 - x, core)
        self.yn = device_at(z, 1 - y, x, core)
        self.sib = device_at(z, y, x, 1 - core)

    def zb(self, t):
        s = self.z // 2
        return (3 - 3 * s, 2 - s, 1 - self.z + 4 * s, self.z)[t]

    def base(self, zb):
        return zb * 8

    def side(self, h):
        return (self.y, self.x) if h == 0 else (self.x, self.y)

    def near(self, h):
        return (self.yn, self.xn) if h == 0 else (self.xn, self.yn)

    def send1(self, t, h, q):
        zb = self.zb(t)
        a, b = self.side(h)
        b = 1 - b if q == 0 else b
        return remote(
            rows_at(self.acc, self.base(zb) + h * 4 + (1 - a) * 2 + b, 1, self.rows),
            rows_at(self.got1, zb * 4 + h * 2 + b, 1, self.rows),
            self.s1.at[zb, h, q],
            self.r1.at[zb, h, q],
            self.near(h)[0],
        )

    def send2(self, t, h):
        zb = self.zb(t)
        a, b = self.side(h)
        return remote(
            rows_at(self.acc, self.base(zb) + h * 4 + a * 2 + 1 - b, 1, self.rows),
            rows_at(self.got2, zb * 2 + h, 1, self.rows),
            self.s2.at[zb, h],
            self.r2.at[zb, h],
            self.near(h)[1],
        )

    def send3(self, t, h, up):
        zb = self.zb(t)
        a, b = self.side(h)
        slot = zb if up else zb + (4 - zb) * (1 - (self.z - 1 - zb + 2) // 3)
        return remote(
            rows_at(self.acc, self.base(zb) + h * 4 + a * 2 + b, 1, self.rows),
            rows_at(self.got3, slot * 2 + h, 1, self.rows),
            self.s3.at[t, h],
            self.r3.at[slot, h],
            device_at(self.z + (1 if up else -1), self.y, self.x, self.core),
        )

    def come3(self, slot, h):
        ref = rows_at(self.got3, slot * 2 + h, 1, self.rows)
        remote(ref, ref, self.s3.at[0, h], self.r3.at[slot, h], self.xn).wait_recv()
        a, b = self.side(h)
        zb = self.z if isinstance(slot, int) else slot
        self.add(self.base(zb) + h * 4 + a * 2 + b, self.got3, slot * 2 + h, 1)

    def add(self, at, ref, start, count):
        step = 48

        def body(i, _):
            to = pl.ds(pl.multiple_of(at * self.rows + i * step, 16), step)
            given = pl.ds(pl.multiple_of(start * self.rows + i * step, 16), step)
            self.acc[to, :] = self.acc[to, :] + ref[given, :]
            return 0

        lax.fori_loop(0, count * self.rows // step, body, 0)

    def go1(self, t, q):
        for h in range(2):
            self.send1(t, h, q).start()

    def one(self, t, q):
        zb = self.zb(t)
        for h in range(2):
            a, b = self.side(h)
            b = 1 - b if q == 0 else b
            self.send1(t, h, q).wait_recv()
            self.add(self.base(zb) + h * 4 + a * 2 + b, self.got1, zb * 4 + h * 2 + b, 1)
            if q == 0:
                self.send2(t, h).start()

    def two(self, t):
        zb = self.zb(t)
        for h in range(2):
            a, b = self.side(h)
            self.send2(t, h).wait_recv()
            self.add(self.base(zb) + h * 4 + a * 2 + b, self.got2, zb * 2 + h, 1)

    def tri(self, t):
        zb = self.zb(t)
        z = self.z
        for h in range(2):

            @pl.when(((zb > z) & (z > 0)) | ((zb < z) & (z < 3)))
            def _():
                self.come3(zb, h)

            @pl.when(zb > z)
            def _():
                self.send3(t, h, True).start()

            @pl.when(zb < z)
            def _():
                self.send3(t, h, False).start()

    def three(self):
        for h in range(2):

            @pl.when(self.z > 0)
            def _():
                self.come3(self.z, h)

            @pl.when(self.z < 3)
            def _():
                self.come3(4, h)

    def own(self, h):
        a, b = self.side(h)
        return rows_at(self.acc, self.base(self.z) + h * 4 + a * 2 + b, 1, self.rows)

    def finish(self):
        for t in range(4):
            for h in range(2):
                for q in range(2):
                    self.send1(t, h, q).wait_send()
                self.send2(t, h).wait_send()
                if t < 3:
                    ref = rows_at(self.got3, h, 1, self.rows)
                    remote(ref, ref, self.s3.at[t, h], self.r3.at[0, h], self.xn).wait_send()


def front_kernel(
    given_ref, norm_ref, cos_ref, sin_ref, bias_ref,
    oa_ref, ob_ref, heads, wide_ref, lse_ref, mixed_ref,
    stack, rows, seen, low, mixed, got_a, got_b, new_a, new_b, own_a, own_b, send, recv, csem, ql, qsend, qrecv, ml, msend, mrecv, *sems
):
    n = 8
    z, y, x, core = place()
    ctx, shard = lax.axis_index("ctx"), lax.axis_index("shard")
    m = len(GATHER_SEMS)
    rows_a, rows_b = own_a.shape[0] // 2, own_b.shape[0] // 2
    ga = Gather(lambda h: rows_at(own_a, h, 1, rows_a), stack, rows_a, sems[:m])
    gb = Gather(lambda h: rows_at(own_b, h, 1, rows_b), ob_ref, rows_b, sems[m:])
    _, slots, block_len, width = rows.shape
    seq, my_width = seen.shape[2:]
    greet([ga.xn, ga.sib] + [(lax.rem(ctx + d, n), shard) for d in range(1, n)])
    jobs = ((0, got_a, new_a, own_a), (8 * rows_a, got_b, new_b, own_b))

    def share(i, c, xb):
        start, got, new, own = jobs[i]
        size = own.shape[0]
        at = start + c * 2 * size
        if xb is None:
            return given_ref.at[pl.ds(pl.multiple_of(at, 16), 2 * size)]
        return given_ref[pl.ds(pl.multiple_of(at + xb * size, 16), size), :]

    def held(i, xb):
        size = jobs[i][3].shape[0]
        return pl.ds(pl.multiple_of(xb * size, 16), size)

    def to_core(i):
        return remote(share(i, 1 - core, None), jobs[i][1], send.at[i], recv.at[i], ga.sib)

    def to_x(i):
        start, got, new, own = jobs[i]
        return remote(got.at[held(i, 1 - x)], new, send.at[2 + i], recv.at[2 + i], ga.xn)

    def spread(i):
        start, got, new, own = jobs[i]
        to_core(i).wait_recv()
        got[held(i, 1 - x), :] = got[held(i, 1 - x), :] + share(i, core, 1 - x)
        to_x(i).start()
        own[...] = got[held(i, x), :] + share(i, core, x)

    def cross(i):
        start, got, new, own = jobs[i]
        to_x(i).wait_recv()
        own[...] = own[...] + new[...]

    def peer(d):
        return lax.rem(ctx + d, n)

    def lanes(owner):
        return pl.ds(pl.multiple_of(owner * my_width, my_width), my_width)

    def block(owner):
        return pl.ds(pl.multiple_of(owner * block_len, block_len), block_len)

    def head_copy(j, owner):
        return remote(
            rows.at[j, :, :, lanes(owner)], seen.at[j, :, block(ctx), :], qsend.at[j, owner], qrecv.at[j, ctx], (owner, shard)
        )

    def head_own(j):
        return pltpu.make_async_copy(rows.at[j, :, :, lanes(ctx)], seen.at[j, :, block(ctx), :], ql.at[j])

    def mixed_copy(s, d):
        return remote(
            low.at[s, block(peer(d)), :], mixed.at[s, :, lanes(ctx)], msend.at[s, d], mrecv.at[s, d], (peer(d), shard)
        )

    def mixed_own(s):
        return pltpu.make_async_copy(low.at[s, block(ctx), :], mixed.at[s, :, lanes(ctx)], ml.at[s])

    cols = 256
    tiles = width // cols
    per_z = 16 * rows_a // cols

    def region(i):
        s = z // 2
        t = z % 2
        return (
            z,
            (1 - t) * (1 - s) + s * (1 + t),
            2 * (1 - s) + s * (3 - 2 * t),
            3 * (1 - s),
        )[i]

    def qkv(i):
        zb = region(i)
        ga.whole(zb, 1 - core).wait_recv()

        def tile_step(k, _):
            tile = zb * per_z + k
            j, t = tile // tiles, tile % tiles
            at = pl.ds(pl.multiple_of(t * cols, cols), cols)
            weight = stack[pl.ds(pl.multiple_of(tile * cols, cols), cols), :]
            values = transposed(norm_ref[...], weight)
            turn = (j < 2).astype(jnp.float32)
            cos = cos_ref[...] * turn + (1.0 - turn)
            values = values * cos + half_turned(values) * (sin_ref[...] * turn)
            rows[j, :, :, at] = values.astype(jnp.bfloat16).reshape(slots, block_len, cols)
            for q in range(cols // my_width):
                owner = t * (cols // my_width) + q

                @pl.when(owner == ctx)
                def _():
                    head_own(j).start()

                @pl.when(owner != ctx)
                def _():
                    head_copy(j, owner).start()

            return 0

        lax.fori_loop(0, per_z, tile_step, 0)

    def heads_wait():
        for j in range(3):
            head_own(j).wait()
            for d in range(1, n):
                ref = seen.at[j, :, block(peer(d)), :]
                remote(ref, ref, qsend.at[j, peer(d)], qrecv.at[j, peer(d)], (peer(d), shard)).wait_recv()

    def mixed_wait():
        for s in range(slots):
            mixed_own(s).wait()
            for d in range(1, n):
                mixed_copy(s, d).wait_recv()

    for i in range(2):
        to_core(i).start()
    spread(0)
    spread(1)
    cross(0)
    ga.start()
    ga.line(-1), ga.line(1)
    ga.cross(0)
    ga.line(-2), ga.line(2)
    ga.cross(-1), ga.cross(1)
    ga.close(0)
    cross(1)
    ga.line(-3), ga.line(3)
    ga.cross(-2), ga.cross(2)
    qkv(0)
    ga.close(-1), ga.close(1)
    gb.start()
    ga.cross(-3), ga.cross(3)
    qkv(1)
    ga.close(-2), ga.close(2)
    gb.line(-1), gb.line(1)
    qkv(2)
    ga.close(-3), ga.close(3)
    gb.cross(0)
    qkv(3)
    gb.line(-2), gb.line(2)
    heads_wait()
    keep_a = pltpu.make_async_copy(stack, oa_ref, csem.at[0])
    keep_heads = pltpu.make_async_copy(seen, heads, csem.at[1])
    keep_a.start()
    keep_heads.start()
    chunk = 256
    per_slot = seq // chunk

    def attend_at(i, _):
        s, c = i // per_slot, i % per_slot
        attend_step(
            c, seen.at[0, s], seen.at[1, s], seen.at[2, s], bias_ref[s], low.at[s], wide_ref.at[s], lse_ref.at[s], chunk
        )

        @pl.when(c == per_slot - 1)
        def _():
            mixed_own(s).start()
            for d in range(1, n):
                mixed_copy(s, d).start()

        @pl.when(i == 0)
        def _():
            gb.cross(-1), gb.cross(1)

        @pl.when(i == 3)
        def _():
            gb.close(0)

        @pl.when(i == 5)
        def _():
            gb.line(-3), gb.line(3)

        return 0

    lax.fori_loop(0, slots * per_slot, attend_at, 0)
    gb.cross(-2), gb.cross(2)
    gb.close(-1), gb.close(1)
    gb.cross(-3), gb.cross(3)
    gb.close(-2), gb.close(2)
    gb.close(-3), gb.close(3)
    mixed_wait()
    mixed_ref[...] = mixed[...]
    keep_a.wait()
    keep_heads.wait()
    for i in range(2):
        to_core(i).wait_send()
        to_x(i).wait_send()
    for d in range(1, n):
        for j in range(3):
            head_copy(j, peer(d)).wait_send()
        for s in range(slots):
            mixed_copy(s, d).wait_send()
    ga.finish(False)
    gb.finish()


def front_call(given, rows_a, rows_b, norm_one, cosine, sine, bias, slots, block_len, collective_id):
    vmem = pl.BlockSpec(memory_space=pltpu.VMEM)
    any_ = pl.BlockSpec(memory_space=pl.ANY)
    low = jnp.bfloat16
    width = norm_one.shape[1]
    seq = block_len * 8
    my_width = width // 8
    stack_a, stack_b = (jax.ShapeDtypeStruct((64 * r, width), low) for r in (rows_a, rows_b))
    scratch = [
        pltpu.VMEM(stack_a.shape, low),
        pltpu.VMEM((3, slots, block_len, width), low),
        pltpu.VMEM((3, slots, seq, my_width), low),
        pltpu.VMEM((slots, seq, my_width), low),
        pltpu.VMEM((slots, block_len, width), low),
    ]
    for pieces in (4, 2, 2):
        for r in (rows_a, rows_b):
            scratch.append(pltpu.VMEM((pieces * r, width), low))
    return pl.pallas_call(
        front_kernel,
        out_shape=(
            stack_a,
            stack_b,
            jax.ShapeDtypeStruct((3, slots, seq, my_width), low),
            jax.ShapeDtypeStruct((slots, seq, my_width), jnp.float32),
            jax.ShapeDtypeStruct((slots, seq, my_width), jnp.float32),
            jax.ShapeDtypeStruct((slots, block_len, width), low),
        ),
        in_specs=[vmem] * 5,
        out_specs=(any_, any_, any_, vmem, vmem, vmem),
        scratch_shapes=scratch
        + [DMA((4,)), DMA((4,)), DMA((2,)), DMA((3,)), DMA((3, 8)), DMA((3, 8)), DMA((slots,)), DMA((slots, 8)), DMA((slots, 8))]
        + GATHER_SEMS * 2,
        compiler_params=pltpu.CompilerParams(
            collective_id=collective_id, has_side_effects=True, vmem_limit_bytes=VMEM_BYTES
        ),
        name="spread_and_attend",
    )(given, norm_one, cosine, sine, bias)


GAIN_SEMS = [DMA((6,)), DMA((6,))]


class GainSum:
    def __init__(self, ref, got, line, sems):
        self.ref, self.got, self.all = ref, got, line
        self.send, self.recv = sems
        self.z, self.y, self.x, self.core = place()

    def step(self, i):
        z, y, x, core = self.z, self.y, self.x, self.core
        to = (device_at(z, y, x, 1 - core), device_at(z, y, 1 - x, core), device_at(z, 1 - y, x, core))[i]
        return remote(self.ref, self.got.at[i], self.send.at[i], self.recv.at[i], to)

    def far(self, d):
        to = device_at((self.z + d) % 4, self.y, self.x, self.core)
        return remote(self.ref, self.all.at[self.z], self.send.at[2 + d], self.recv.at[2 + d], to)

    def begin(self, i):
        self.step(i).start()

    def end(self, i):
        self.step(i).wait()
        self.ref[...] = self.ref[...] + self.got[i]

    def begin_far(self):
        for d in (1, 2, 3):
            self.far(d).start()
        self.all[self.z] = self.ref[...]

    def end_far(self, out):
        for d in (1, 2, 3):
            self.far(d).wait()
        total = self.all[0]
        for i in range(1, 4):
            total = total + self.all[i]
        out[...] = total


def back_kernel(
    g_ref, qkv_ref, wide_ref, lse_ref, bias_ref, cos_ref, sin_ref, norm_ref, tokens_ref, gains_ref, middle_ref, gain_ref,
    left_ref, right_ref, w_ref,
    oa_ref, ob_ref, og_ref, tok_ref,
    left_got, right_got, norm_got, rows_got, weight_ref, xsend, xrecv, heads, grad, rows, acc_k, acc_v, dnorm, gain, gain_got, gain_all, wsem, gl, gsend, grecv, dl, dsend, drecv, *refs
):
    n = 8
    slots, block_len, width = g_ref.shape
    seq, my_width = qkv_ref.shape[2:]
    chunk = 256
    per_slot = seq // chunk
    m = len(GATHER_SEMS)
    rows_a, rows_b = oa_ref.shape[0] // 64, ob_ref.shape[0] // 64
    ra = Reduce(rows_a, refs[:REDUCE_REFS])
    rb = Reduce(rows_b, refs[REDUCE_REFS : 2 * REDUCE_REFS])
    refs = refs[2 * REDUCE_REFS :]
    ga = Gather(ra.own, oa_ref, rows_a, refs[:m])
    gb = Gather(rb.own, ob_ref, rows_b, refs[m : 2 * m])
    gs = GainSum(gain, gain_got, gain_all, refs[2 * m :])
    z, y, x, core = place()
    ctx, shard = lax.axis_index("ctx"), lax.axis_index("shard")
    greet([ra.xn, ra.sib] + [(lax.rem(ctx + d, n), shard) for d in range(1, n)])

    def peer(d):
        return lax.rem(ctx + d, n)

    def lanes(owner):
        return pl.ds(pl.multiple_of(owner * my_width, my_width), my_width)

    def block(owner):
        return pl.ds(pl.multiple_of(owner * block_len, block_len), block_len)

    def go_copy(d):
        return remote(
            g_ref.at[:, :, lanes(peer(d))], grad.at[:, block(ctx), :], gsend.at[d], grecv.at[d], (peer(d), shard)
        )

    def back_copy(s, d):
        return remote(
            heads.at[:, s, block(peer(d)), :], rows.at[:, s, :, lanes(ctx)], dsend.at[s, d], drecv.at[s, d], (peer(d), shard)
        )

    def back_own(s):
        return pltpu.make_async_copy(heads.at[:, s, block(ctx), :], rows.at[:, s, :, lanes(ctx)], dl.at[s])

    go_own = pltpu.make_async_copy(g_ref.at[:, :, lanes(ctx)], grad.at[:, block(ctx), :], gl)
    w_copy = pltpu.make_async_copy(w_ref, weight_ref, wsem)
    cut = 128
    rows_all = slots * block_len

    def to_sib(src, dst, i):
        return remote(src, dst, xsend.at[i], xrecv.at[i], ra.sib)

    def left_copy(t, c):
        lane = pl.ds(pl.multiple_of((rb.zb(t) * 2 + c) * 8 * rows_b, cut), 8 * rows_b)
        return to_sib(left_ref.at[:, lane], left_got.at[rb.zb(t)], t)

    right_copy = to_sib(right_ref, right_got, 4)
    norm_copy = to_sib(norm_ref, norm_got, 5)
    rows_copy = to_sib(rows, rows_got, 6)

    def given():
        left_copy(0, 1 - core).start()
        right_copy.start()
        for t in range(1, 4):
            left_copy(t, 1 - core).start()
        norm_copy.start()
        right_copy.wait_recv()

    def fill(t):
        zb = rb.zb(t)
        left_copy(t, core).wait_recv()
        count = 8 * rows_b // cut

        def step(i, _):
            g = (zb * 2 + core) * count + i
            kind = (g >= width // cut).astype(jnp.int32) + (g >= (width + 2 * FF_WIDE) // cut).astype(jnp.int32)
            mine = left_ref[:, pl.ds(pl.multiple_of(g * cut, cut), cut)]
            other = left_got[zb, :, pl.ds(pl.multiple_of(i * cut, cut), cut)]
            total = leading(mine, right_ref[kind]) + leading(other, right_got[kind])
            at = pl.ds(pl.multiple_of(zb * 8 * rows_b + i * cut, cut), cut)
            rb.acc[at, :] = total.astype(jnp.bfloat16)
            return 0

        lax.fori_loop(0, count, step, 0)
    cols = 256
    tiles = width // cols

    def rows_wait():
        for s in range(slots):
            back_own(s).wait()
            for d in range(1, n):
                back_copy(s, d).wait_recv()
        rows_copy.start()
        norm_copy.wait_recv()
        rows_copy.wait_recv()

    def weight(t):
        zb = ra.zb(t)
        count = 8 * rows_a // cut

        def step(i, _):
            g = (zb * 2 + core) * count + i
            j = g * cut // width
            lane = pl.ds(pl.multiple_of(g * cut - j * width, cut), cut)
            total = leading(rows[j, :, :, lane].reshape(rows_all, cut), norm_ref[...])
            total += leading(rows_got[j, :, :, lane].reshape(rows_all, cut), norm_got[...])
            at = pl.ds(pl.multiple_of(zb * 8 * rows_a + i * cut, cut), cut)
            ra.acc[at, :] = total.astype(jnp.bfloat16)
            return 0

        lax.fori_loop(0, count, step, 0)

    def norm_step(t, _):
        at = pl.ds(pl.multiple_of(t * cols, cols), cols)
        total = None
        for j in range(3):
            left = rows[j].reshape(slots * block_len, width)
            right = weight_ref[pl.ds(j * width, width), at]
            part = jnp.dot(left, right, preferred_element_type=jnp.float32)
            total = part if total is None else total + part
        dnorm[:, at] = total
        return 0

    some = 64
    def token_step(i, _):
        at = pl.ds(pl.multiple_of(i * some, some), some)
        values = tokens_ref[at, :].astype(jnp.float32)
        mean = jnp.mean(values, axis=-1, keepdims=True)
        centred = values - mean
        scale = lax.rsqrt(jnp.mean(centred * centred, axis=-1, keepdims=True) + eps_norm)
        unit = centred * scale
        given = dnorm[at, :]
        inner = given * gains_ref[0:1, :]
        inner_mean = jnp.mean(inner, axis=-1, keepdims=True)
        along = jnp.mean(inner * unit, axis=-1, keepdims=True)
        grads = middle_ref[at, :] + scale * (inner - inner_mean - unit * along)
        tok_ref[at, :] = grads.astype(jnp.bfloat16)
        gain[0:1, :] += jnp.sum(given * unit, axis=0, keepdims=True)
        return 0

    def token():
        w_copy.wait()
        lax.fori_loop(0, tiles, norm_step, 0)
        gain[...] = gain_ref[...]
        lax.fori_loop(0, slots * block_len // some, token_step, 0)
        gs.begin(0)

    for d in range(1, n):
        go_copy(d).start()
    go_own.start()
    given()
    fill(0)
    rb.go1(0, 0)
    rb.go1(0, 1)
    fill(1)
    fill(2)
    fill(3)
    w_copy.start()
    go_own.wait()
    for d in range(1, n):
        go_copy(d).wait_recv()

    def attend_step(i, _):
        s, c = i // per_slot, i % per_slot
        slot = (
            qkv_ref.at[0, s], qkv_ref.at[1, s], qkv_ref.at[2, s], grad.at[s], wide_ref.at[s], lse_ref.at[s], bias_ref[s],
            cos_ref, sin_ref, heads.at[0, s], heads.at[1, s], heads.at[2, s], acc_k, acc_v, chunk,
        )

        @pl.when(c == 0)
        def _():
            acc_k[...] = jnp.zeros_like(acc_k)
            acc_v[...] = jnp.zeros_like(acc_v)

        attend_back_step(c, *slot)

        @pl.when(c == per_slot - 1)
        def _():
            attend_back_end(*slot)
            back_own(s).start()
            for d in range(1, n):
                back_copy(s, d).start()

        @pl.when(i == 1)
        def _():
            rb.one(0, 0)
            rb.go1(1, 0)
            rb.one(0, 1)
            rb.go1(1, 1)

        return 0

    lax.fori_loop(0, slots * per_slot, attend_step, 0)
    rb.two(0)
    rb.one(1, 0)
    rb.go1(2, 0)
    rb.one(1, 1)
    rb.go1(2, 1)
    rb.tri(0)
    rb.two(1)
    rb.one(2, 0)
    rb.go1(3, 0)
    rb.one(2, 1)
    rb.go1(3, 1)
    rb.tri(1)
    rb.two(2)
    rb.one(3, 0)
    rb.one(3, 1)
    rb.tri(2)
    rows_wait()
    weight(0)
    ra.go1(0, 0)
    ra.go1(0, 1)
    weight(1)
    ra.go1(1, 0)
    ra.go1(1, 1)
    rb.two(3)
    weight(2)
    ra.go1(2, 0)
    ra.go1(2, 1)
    weight(3)
    ra.go1(3, 0)
    ra.go1(3, 1)
    ra.one(0, 0)
    ra.one(0, 1)
    rb.three()
    gb.start()
    token()
    ra.one(1, 0)
    ra.one(1, 1)
    ra.two(0)
    ra.one(2, 0)
    ra.one(2, 1)
    ra.tri(0)
    ra.two(1)
    gb.line(-1), gb.line(1)
    ra.one(3, 0)
    ra.one(3, 1)
    ra.tri(1)
    ra.two(2)
    gb.cross(0)
    gs.end(0)
    gs.begin(1)
    ra.tri(2)
    ra.two(3)
    gb.line(-2), gb.line(2)
    ra.three()
    ga.start()
    gb.cross(-1), gb.cross(1)
    gs.end(1)
    gs.begin(2)
    gb.close(0)
    gb.line(-3), gb.line(3)
    ga.line(-1), ga.line(1)
    gb.cross(-2), gb.cross(2)
    gs.end(2)
    gs.begin_far()
    ga.cross(0)
    gb.close(-1), gb.close(1)
    ga.line(-2), ga.line(2)
    gb.cross(-3), gb.cross(3)
    ga.cross(-1), ga.cross(1)
    ga.close(0)
    gb.close(-2), gb.close(2)
    ga.line(-3), ga.line(3)
    ga.cross(-2), ga.cross(2)
    ga.close(-1), ga.close(1)
    gb.close(-3), gb.close(3)
    ga.cross(-3), ga.cross(3)
    ga.close(-2), ga.close(2)
    ga.close(-3), ga.close(3)
    gs.end_far(og_ref)
    for d in range(1, n):
        go_copy(d).wait_send()
        for s in range(slots):
            back_copy(s, d).wait_send()
    for t in range(4):
        left_copy(t, 1 - core).wait_send()
    for copy in (right_copy, norm_copy, rows_copy):
        copy.wait_send()
    ra.finish(), rb.finish(), ga.finish(), gb.finish()


def back_call(
    grad_rows, qkv_heads, wide, lse, bias, cosine, sine, norm_one, tokens, gains, grad_middle, gain_part, left, right, w_qkv, collective_id
):
    any_ = pl.BlockSpec(memory_space=pl.ANY)
    vmem = pl.BlockSpec(memory_space=pltpu.VMEM)
    low = jnp.bfloat16
    slots, block_len, width = grad_rows.shape
    seq, my_width = qkv_heads.shape[2:]
    rows_all = slots * block_len
    gain = gain_part.shape
    rows_a, rows_b = w_qkv.shape[0] // 64, left.shape[1] // 64
    return pl.pallas_call(
        back_kernel,
        out_shape=(
            jax.ShapeDtypeStruct(w_qkv.shape, low),
            jax.ShapeDtypeStruct((64 * rows_b, width), low),
            jax.ShapeDtypeStruct(gain, jnp.float32),
            jax.ShapeDtypeStruct((rows_all, width), low),
        ),
        in_specs=[vmem] * 14 + [any_],
        out_specs=(any_, any_, vmem, vmem),
        scratch_shapes=[
            pltpu.VMEM((4, rows_all, 8 * rows_b), low),
            pltpu.VMEM(right.shape, low),
            pltpu.VMEM((rows_all, width), low),
            pltpu.VMEM((3, slots, block_len, width), low),
            pltpu.VMEM(w_qkv.shape, low),
            DMA((7,)),
            DMA((7,)),
            pltpu.VMEM(qkv_heads.shape, low),
            pltpu.VMEM((slots, seq, my_width), low),
            pltpu.VMEM((3, slots, block_len, width), low),
            pltpu.VMEM((seq, my_width), jnp.float32),
            pltpu.VMEM((seq, my_width), jnp.float32),
            pltpu.VMEM((rows_all, width), jnp.float32),
            pltpu.VMEM(gain, jnp.float32),
            pltpu.VMEM((3,) + gain, jnp.float32),
            pltpu.VMEM((4,) + gain, jnp.float32),
            DMA,
            DMA,
            DMA((8,)),
            DMA((8,)),
            DMA((slots,)),
            DMA((slots, 8)),
            DMA((slots, 8)),
        ]
        + reduce_scratch(rows_a, width)
        + reduce_scratch(rows_b, width)
        + GATHER_SEMS * 2
        + GAIN_SEMS,
        compiler_params=pltpu.CompilerParams(
            collective_id=collective_id, has_side_effects=True, vmem_limit_bytes=VMEM_BYTES
        ),
        name="back_and_sum",
    )(grad_rows, qkv_heads, wide, lse, bias, cosine, sine, norm_one, tokens, gains, grad_middle, gain_part, left, right, w_qkv)


def to_heads(values):
    return lax.all_to_all(values, "ctx", split_axis=3, concat_axis=2, tiled=True)


def to_rows(values):
    return lax.all_to_all(values, "ctx", split_axis=2, concat_axis=3, tiled=True)


def shards(
    fast,
    tokens,
    cotangent,
    lengths,
    unit_owner,
    master,
    first_moment,
    second_moment,
    norm_gains,
    gain_first,
    gain_second,
):
    slots, block_len, width = tokens.shape
    groups = lax.axis_size("shard")
    n = lax.axis_size("ctx")
    ctx, shard = lax.axis_index("ctx"), lax.axis_index("shard")
    capacity, unit_rows, _ = master.shape
    units = unit_owner.shape[0]
    rows_all = slots * block_len
    seq = block_len * n
    device_count = n * groups
    my_width = width // n

    low = jnp.bfloat16
    rows_a = 3 * width
    rows_b = width + 3 * FF_WIDE
    split = rows_a // unit_rows
    lead, ff_units, wide_units = (r // unit_rows for r in (width, FF, FF_WIDE))

    def unit_of(block, chunk):
        if chunk == 0:
            return jnp.where(block < split, block, -1)
        inner = block - lead
        third = inner // wide_units
        at = inner - third * wide_units
        there = (block < lead) | ((at < ff_units) & (third < 3))
        return jnp.where(there, split + jnp.where(block < lead, block, lead + third * ff_units + at), -1)

    def block_of(unit):
        inner = unit - split - lead
        third = jnp.maximum(inner, 0) // ff_units
        return unit - split + third * (wide_units - ff_units)

    part_rows = 16
    per_unit = unit_rows // part_rows
    parts = master.reshape(capacity * per_unit, part_rows, width)

    def units_at(chunk, per, wanted):
        at = wanted[..., None] * (per // part_rows) + jnp.arange(per // part_rows, dtype=jnp.int32)
        at = at.reshape(-1)
        return unit_of(at // per_unit, chunk), at % per_unit

    def pick(unit, inner):
        owner, rank = unit_places(unit_owner, unit)
        mine = (owner == shard) & (unit >= 0)
        return pick_call(jnp.where(mine, rank * per_unit + inner, -1), parts)

    def piece_rows(count, pieces):
        return -(-count // (pieces * part_rows)) * part_rows

    positions = ctx * block_len + jnp.arange(block_len, dtype=jnp.int32)
    tile_heads = 256 // HEAD_DIM
    cos_rows, sin_rows = rope_tables(jnp.tile(positions, slots), tile_heads)
    cos_seq, sin_seq = rope_tables(jnp.arange(seq, dtype=jnp.int32), my_width // HEAD_DIM)
    live_rows = (positions[None, :] < lengths[:, None]).astype(jnp.float32)
    bias = jnp.where(
        jnp.arange(seq, dtype=jnp.int32)[None, :] < lengths[:, None], 0.0, mask_fill
    ).astype(jnp.float32)[:, None, :]

    inputs = tokens.astype(jnp.float32).reshape(rows_all, width)
    norm_one = layer_norm(inputs, norm_gains[0]).astype(jnp.bfloat16)
    if fast:
        z, y, x, core = place()
        wanted = jnp.stack(
            [
                jnp.stack([jnp.stack([piece_at(z, c, 0, y, q), piece_at(z, c, 1, q, y)]) for q in range(2)])
                for c in range(2)
            ]
        )
        per_a, per_b = piece_rows(rows_a, 64), piece_rows(rows_b, 64)
        at_pieces = [units_at(0, per_a, wanted), units_at(1, per_b, wanted)]
        given = pick(*(jnp.concatenate(both) for both in zip(*at_pieces)))
        stack_a, stack_b, qkv_heads, wide, lse, mixed_low = front_call(
            given, per_a, per_b, norm_one, cos_rows, sin_rows, bias, slots, block_len, 0
        )
    else:
        wanted = ctx * groups + jnp.arange(groups, dtype=jnp.int32)
        stacks = []
        for chunk, count in enumerate((rows_a, rows_b)):
            share = pick(*units_at(chunk, piece_rows(count, device_count), wanted))
            own = lax.psum_scatter(share, "shard", scatter_dimension=0, tiled=True)
            stacks.append(lax.all_gather(own, BOTH, axis=0, tiled=True))
        stack_a, stack_b = stacks
        qkv = qkv_call(norm_one, stack_a, cos_rows, sin_rows)
        qkv_heads = to_heads(qkv.reshape(3, slots, block_len, width))
        mixed_heads, wide, lse = attend_call(qkv_heads, bias)
        mixed_low = to_rows(mixed_heads[None])
    mixed_low = mixed_low.reshape(rows_all, width)
    w_out = stack_b[:width]
    w_up = stack_b[width : width + 2 * FF_WIDE]
    w_down = stack_b[width + 2 * FF_WIDE : rows_b]

    middle = inputs + transposed(mixed_low, w_out)
    norm_two = layer_norm(middle, norm_gains[1]).astype(jnp.bfloat16)
    upper_proj = transposed(norm_two, w_up)
    hidden_low = gated_gelu(upper_proj).astype(jnp.bfloat16)
    result = middle + jnp.dot(hidden_low, w_down, preferred_element_type=jnp.float32)
    output = result.astype(jnp.bfloat16).reshape(slots, block_len, width)

    grad_result = cotangent.astype(jnp.float32).reshape(rows_all, width) * live_rows.reshape(
        rows_all, 1
    )
    grad_down_low = grad_result.astype(jnp.bfloat16)
    grad_hidden = transposed(grad_down_low, w_down)
    _, gelu_back = jax.vjp(gated_gelu, upper_proj)
    grad_upper_low = gelu_back(grad_hidden)[0].astype(jnp.bfloat16)
    grad_norm_two = jnp.dot(grad_upper_low, w_up, preferred_element_type=jnp.float32)
    _, norm_back_two = jax.vjp(layer_norm, middle, norm_gains[1])
    grad_middle_part, grad_gain_two = norm_back_two(grad_norm_two)
    grad_middle = grad_result + grad_middle_part
    grad_attn_low = grad_middle.astype(jnp.bfloat16)
    grad_heads_rows = jnp.dot(grad_attn_low, w_out, preferred_element_type=jnp.float32).astype(
        jnp.bfloat16
    )
    grad_heads_rows = grad_heads_rows.reshape(slots, block_len, width)

    gain_part = jnp.zeros((8, width), jnp.float32).at[1].set(grad_gain_two)
    if fast:
        left = jnp.concatenate(
            [
                grad_attn_low,
                grad_upper_low,
                hidden_low,
                jnp.zeros((rows_all, stack_b.shape[0] - rows_b), low),
            ],
            axis=1,
        )
        right = jnp.stack([mixed_low, norm_two, grad_down_low])
        all_a, all_b, gain_grad, token_grad = back_call(
            grad_heads_rows, qkv_heads, wide, lse, bias, cos_seq, sin_seq, norm_one, tokens.reshape(rows_all, width),
            norm_gains, grad_middle, gain_part, left, right, stack_a, 1,
        )
    else:
        grads_b = jnp.concatenate(
            [
                leading(grad_attn_low, mixed_low).astype(low),
                leading(grad_upper_low, norm_two).astype(low),
                leading(hidden_low, grad_down_low).astype(low),
                jnp.zeros((stack_b.shape[0] - rows_b, width), low),
            ],
            axis=0,
        )
        grad_heads = to_heads(grad_heads_rows[None])[0]
        grad_qkv_heads = attend_back_call(qkv_heads, grad_heads, wide, lse, bias, cos_seq, sin_seq)
        grad_qkv_low = to_rows(grad_qkv_heads).reshape(3, rows_all, width)
        grad_norm_one = sum(
            jnp.dot(
                grad_qkv_low[i],
                stack_a[i * width : (i + 1) * width],
                preferred_element_type=jnp.float32,
            )
            for i in range(3)
        )
        _, norm_back_one = jax.vjp(layer_norm, inputs, norm_gains[0])
        grad_input_part, grad_gain_one = norm_back_one(grad_norm_one)
        token_grad = (grad_middle + grad_input_part).astype(low)
        grads_a = jnp.concatenate(
            [leading(grad_qkv_low[i], norm_one).astype(low) for i in range(3)]
            + [jnp.zeros((stack_a.shape[0] - rows_a, width), low)],
            axis=0,
        )
        all_a, all_b = (
            lax.all_gather(
                lax.psum_scatter(g, BOTH, scatter_dimension=0, tiled=True), BOTH, axis=0, tiled=True
            )
            for g in (grads_a, grads_b)
        )
        gain_grad = lax.psum(gain_part.at[0].set(grad_gain_one), BOTH)
    token_grad = token_grad.reshape(slots, block_len, width)
    gain_grad = gain_grad[:2]
    all_a = all_a.reshape(-1, unit_rows, width)
    all_b = all_b.reshape(-1, unit_rows, width)

    every = jnp.arange(units, dtype=jnp.int32)
    rank = unit_places(unit_owner, every)[1]
    here = (unit_owner == shard) & (rank == jnp.arange(capacity, dtype=jnp.int32)[:, None])
    unit_of_slot = jnp.sum(jnp.where(here, every + 1, 0), axis=1) - 1
    kind = jnp.where(unit_of_slot < 0, -1, (unit_of_slot >= split).astype(jnp.int32))
    at_a = jnp.maximum(lax.cummax(jnp.where(kind == 0, unit_of_slot, -1)), 0)
    at_b = jnp.maximum(block_of(lax.cummax(jnp.where(kind == 1, unit_of_slot, -1))), 0)
    new_master, new_first, new_second = adam_call(
        kind, at_a, at_b, all_a, all_b, master, first_moment, second_moment
    )
    new_gains, new_gain_first, new_gain_second = adam_update(
        norm_gains, gain_grad, gain_first, gain_second, rate_gain, 0.0
    )
    return (
        output,
        token_grad,
        new_master,
        new_first,
        new_second,
        new_gains,
        new_gain_first,
        new_gain_second,
    )


def solution(mesh):
    fast = dict(mesh.shape) == {"ctx": 8, "shard": 4}
    return jax.shard_map(
        functools.partial(shards, fast),
        mesh=mesh,
        in_specs=(
            P("shard", "ctx", None),
            P("shard", "ctx", None),
            P("shard"),
            P(),
            P("shard", None, None),
            P("shard", None, None),
            P("shard", None, None),
            P(),
            P(),
            P(),
        ),
        out_specs=(
            P("shard", "ctx", None),
            P("shard", "ctx", None),
            P("shard", None, None),
            P("shard", None, None),
            P("shard", None, None),
            P(),
            P(),
            P(),
        ),
        check_vma=False,
    )
```

```python
import functools
import math

import jax
import jax.numpy as jnp
import numpy as np
from jax import lax
from jax.experimental import pallas as pl
from jax.experimental.pallas import tpu as pltpu
from jax.sharding import PartitionSpec as P

HEADS = 16
HEAD_DIM = 64
FF = 2624
FF_WIDE = -(-FF // 128) * 128
STEP = 10
MESH = pl.DeviceIdType.MESH
DMA = pltpu.SemaphoreType.DMA

eps_norm = 1e-05
rope_base = 160000.0
mask_fill = -1e30
beta_one = 0.9
beta_two = 0.98
adam_eps = 1e-06
rate_matrix = 0.03
rate_gain = 0.6
decay_matrix = 0.01
BOTH = ("ctx", "shard")
VMEM_BYTES = 60 * 2**20


def transposed(left, right):
    return lax.dot_general(
        left, right, (((1,), (1,)), ((), ())), preferred_element_type=jnp.float32
    )


def leading(left, right):
    return lax.dot_general(
        left, right, (((0,), (0,)), ((), ())), preferred_element_type=jnp.float32
    )


def layer_norm(values, gain):
    row_mean = jnp.mean(values, axis=-1, keepdims=True)
    centred = values - row_mean
    variance = jnp.mean(centred * centred, axis=-1, keepdims=True)
    return centred * lax.rsqrt(variance + eps_norm) * gain


def rope_tables(seq, heads):
    half_dim = HEAD_DIM // 2
    inverse = rope_base ** (-2.0 * np.arange(half_dim) / HEAD_DIM)
    angles = np.arange(seq)[:, None] * inverse.astype(np.float32).astype(np.float64)[None, :]
    angles = angles.astype(np.float32).astype(np.float64)
    cosine, sine = np.cos(angles), np.sin(angles)
    cosine = np.concatenate([cosine, cosine] * heads, axis=1)
    sine = np.concatenate([-sine, sine] * heads, axis=1)
    return jnp.asarray(cosine, jnp.float32), jnp.asarray(sine, jnp.float32)


def half_turned(values):
    width = values.shape[-1]
    half = HEAD_DIM // 2
    lane = lax.broadcasted_iota(jnp.int32, values.shape, values.ndim - 1)
    if width == HEAD_DIM:
        return jnp.concatenate([values[:, half:], values[:, :half]], axis=1)
    ahead = pltpu.roll(values, width - half, axis=1)
    behind = pltpu.roll(values, half, axis=1)
    return jnp.where(lane % HEAD_DIM < half, ahead, behind)


def unit_places(unit_owner, chosen):
    every = jnp.arange(unit_owner.shape[0], dtype=jnp.int32)
    owner = jnp.sum(jnp.where(every == chosen[:, None], unit_owner, 0), axis=1)
    below = (every < chosen[:, None]) & (unit_owner == owner[:, None])
    return owner, jnp.sum(below.astype(jnp.int32), axis=1)


def adam_update(weight, gradient, first_old, second_old, step_rate, weight_decay):
    first_new = beta_one * first_old + (1.0 - beta_one) * gradient
    second_new = beta_two * second_old + (1.0 - beta_two) * gradient * gradient
    first_fix = 1.0 - beta_one**STEP
    second_fix = 1.0 - beta_two**STEP
    adam_step = first_new / first_fix / (jnp.sqrt(second_new / second_fix) + adam_eps)
    return (weight - step_rate * (adam_step + weight_decay * weight), first_new, second_new)


def qkv_kernel(norm_ref, w_ref, cos_ref, sin_ref, out_ref):
    tile = pl.program_id(0)
    turned_tiles = 2 * pl.num_programs(0) // 3
    values = transposed(norm_ref[...], w_ref[...])

    @pl.when(tile < turned_tiles)
    def _():
        out_ref[0] = (values * cos_ref[...] + half_turned(values) * sin_ref[...]).astype(
            out_ref.dtype
        )

    @pl.when(tile >= turned_tiles)
    def _():
        out_ref[0] = values.astype(out_ref.dtype)


def qkv_call(norm_one, w_qkv, cosine, sine):
    rows, width = norm_one.shape
    cols = 256
    tiles = width // cols
    return pl.pallas_call(
        qkv_kernel,
        grid=(3 * width // cols,),
        in_specs=[
            pl.BlockSpec((rows, width), lambda i: (0, 0)),
            pl.BlockSpec((cols, width), lambda i: (i, 0)),
            pl.BlockSpec((rows, cols), lambda i: (0, 0)),
            pl.BlockSpec((rows, cols), lambda i: (0, 0)),
        ],
        out_specs=pl.BlockSpec((1, rows, cols), lambda i: (i // tiles, 0, i % tiles)),
        out_shape=jax.ShapeDtypeStruct((3, rows, width), jnp.bfloat16),
        name="qkv",
    )(norm_one, w_qkv, cosine, sine)


def head_only(values, head):
    width = values.shape[-1]
    if width == HEAD_DIM:
        return values
    lane = lax.broadcasted_iota(jnp.int32, values.shape, 1)
    return jnp.where(lane // HEAD_DIM == head, values, jnp.zeros_like(values))


def key_bias(length, seq):
    position = lax.broadcasted_iota(jnp.int32, (1, seq), 1)
    return jnp.where(position < length, 0.0, mask_fill).astype(jnp.float32)


def attend_step(i, q_ref, k_ref, v_ref, bias, out_ref, wide_ref, lse_ref, chunk):
    width = k_ref.shape[1]
    heads = width // HEAD_DIM
    rows = pl.ds(pl.multiple_of(i * chunk, chunk), chunk)
    query = q_ref[rows, :] * jnp.bfloat16(0.125)
    total = None
    stats = None
    for h in range(heads):
        scores = transposed(query, head_only(k_ref[...], h)) + bias
        top = jnp.max(scores, axis=-1, keepdims=True)
        weights = jnp.exp(scores - top)
        norm = jnp.sum(weights, axis=-1, keepdims=True)
        low = (weights * (1.0 / norm)).astype(jnp.bfloat16)
        part = jnp.dot(low, head_only(v_ref[...], h), preferred_element_type=jnp.float32)
        lse = jnp.broadcast_to(top + jnp.log(norm), (chunk, width))
        total = part if total is None else total + part
        if stats is None:
            stats = lse
        else:
            lane = lax.broadcasted_iota(jnp.int32, lse.shape, 1)
            stats = jnp.where(lane // HEAD_DIM == h, lse, stats)
    out_ref[rows, :] = total.astype(jnp.bfloat16)
    wide_ref[rows, :] = total
    lse_ref[rows, :] = stats


def attend_slot(*args):
    def step(i, _):
        attend_step(i, *args)
        return 0

    lax.fori_loop(0, args[1].shape[0] // args[-1], step, 0)


def turned_back(grad, cos, sin):
    return grad * cos - half_turned(grad) * sin


def attend_back_step(
    i, q_ref, k_ref, v_ref, g_ref, wide_ref, lse_ref, bias, cos, sin, dq_ref, dk_ref, dv_ref, acc_k, acc_v, chunk
):
    seq, width = k_ref.shape
    heads = width // HEAD_DIM
    rows = pl.ds(pl.multiple_of(i * chunk, chunk), chunk)
    query = q_ref[rows, :]
    grad = g_ref[rows, :]
    lse_all = lse_ref[rows, :]
    both = grad.astype(jnp.float32) * wide_ref[rows, :]
    total = None
    for h in range(heads):
        key = head_only(k_ref[...], h)
        lse = lse_all[:, h * HEAD_DIM : h * HEAD_DIM + 1]
        delta = jnp.sum(head_only(both, h), axis=-1, keepdims=True)
        scores = transposed(query * jnp.bfloat16(0.125), key)
        weights = jnp.exp(scores + (bias - lse))
        back = transposed(grad, head_only(v_ref[...], h))
        low = (weights * (back - delta)).astype(jnp.bfloat16)
        part = jnp.dot(low, key, preferred_element_type=jnp.float32)
        total = part if total is None else total + part
        acc_v[...] += leading(weights.astype(jnp.bfloat16), head_only(grad, h))
        acc_k[...] += leading(low, head_only(query, h))
    dq_ref[rows, :] = turned_back(total * 0.125, cos[rows, :], sin[rows, :]).astype(jnp.bfloat16)


def attend_back_end(
    q_ref, k_ref, v_ref, g_ref, wide_ref, lse_ref, bias, cos, sin, dq_ref, dk_ref, dv_ref, acc_k, acc_v, chunk
):
    dk_ref[...] = turned_back(acc_k[...] * 0.125, cos[...], sin[...]).astype(jnp.bfloat16)
    dv_ref[...] = acc_v[...].astype(jnp.bfloat16)


def attend_back_slot(*args):
    acc_k, acc_v, chunk = args[-3:]
    acc_k[...] = jnp.zeros_like(acc_k)
    acc_v[...] = jnp.zeros_like(acc_v)

    def step(i, _):
        attend_back_step(i, *args)
        return 0

    lax.fori_loop(0, args[1].shape[0] // chunk, step, 0)
    attend_back_end(*args)


def attend_kernel(slots, chunk, qkv_ref, lengths_ref, out_ref, wide_ref, lse_ref):
    for s in range(slots):
        attend_slot(
            qkv_ref.at[0, s], qkv_ref.at[1, s], qkv_ref.at[2, s], key_bias(lengths_ref[s], qkv_ref.shape[2]),
            out_ref.at[s], wide_ref.at[s], lse_ref.at[s], chunk,
        )


def attend_call(qkv, lengths):
    _, slots, seq, width = qkv.shape
    chunk = 256
    return pl.pallas_call(
        functools.partial(attend_kernel, slots, chunk),
        out_shape=(
            jax.ShapeDtypeStruct((slots, seq, width), jnp.bfloat16),
            jax.ShapeDtypeStruct((slots, seq, width), jnp.float32),
            jax.ShapeDtypeStruct((slots, seq, width), jnp.float32),
        ),
        in_specs=[pl.BlockSpec(memory_space=pltpu.VMEM), pl.BlockSpec(memory_space=pltpu.SMEM)],
        compiler_params=pltpu.CompilerParams(vmem_limit_bytes=VMEM_BYTES),
        name="attend",
    )(qkv, lengths)


def attend_back_kernel(slots, chunk, qkv_ref, g_ref, wide_ref, lse_ref, lengths_ref, cos_ref, sin_ref, out_ref, acc_k, acc_v):
    for s in range(slots):
        attend_back_slot(
            qkv_ref.at[0, s], qkv_ref.at[1, s], qkv_ref.at[2, s], g_ref.at[s],
            wide_ref.at[s], lse_ref.at[s], key_bias(lengths_ref[s], qkv_ref.shape[2]), cos_ref, sin_ref,
            out_ref.at[0, s], out_ref.at[1, s], out_ref.at[2, s], acc_k, acc_v, chunk,
        )


def attend_back_call(qkv, grad_heads, wide, lse, lengths, cosine, sine):
    _, slots, seq, width = qkv.shape
    chunk = 256
    return pl.pallas_call(
        functools.partial(attend_back_kernel, slots, chunk),
        out_shape=jax.ShapeDtypeStruct(qkv.shape, jnp.bfloat16),
        in_specs=[pl.BlockSpec(memory_space=pltpu.VMEM)] * 4
        + [pl.BlockSpec(memory_space=pltpu.SMEM)]
        + [pl.BlockSpec(memory_space=pltpu.VMEM)] * 2,
        scratch_shapes=[pltpu.VMEM((seq, width), jnp.float32)] * 2,
        compiler_params=pltpu.CompilerParams(vmem_limit_bytes=VMEM_BYTES),
        name="attend_back",
    )(qkv, grad_heads, wide, lse, lengths, cosine, sine)


def middle_kernel(
    tile, block_len, mixed_ref, tokens_ref, cot_ref, gains_ref, lengths_ref, w_ref,
    out_ref, left_ref, right_ref, go_ref, back_ref, gain_ref,
    w_out, w_one, w_two, w_down, x1, result, dnorm, sems
):
    rows_all, width = tokens_ref.shape
    wide = w_one.shape[0] * tile
    tiles = wide // tile
    cols = 256
    some = 64
    start = lax.axis_index("ctx") * block_len

    def live(i):
        slot, inner = i * some // block_len, i * some % block_len
        position = start + inner + lax.broadcasted_iota(jnp.int32, (some, 1), 0)
        return (position < lengths_ref[slot]).astype(jnp.float32)

    def copies(j):
        rows = [pl.ds(width + k * wide + j * tile, tile) for k in range(3)]
        return [
            pltpu.make_async_copy(w_ref.at[r], to.at[j], sems.at[1 + j * 3 + k])
            for k, (r, to) in enumerate(zip(rows, (w_one, w_two, w_down)))
        ]

    first = pltpu.make_async_copy(w_ref.at[pl.ds(0, width)], w_out, sems.at[0])
    first.start()
    for j in range(tiles):
        for copy in copies(j):
            copy.start()
    right_ref[0] = mixed_ref[...]
    first.wait()

    def out_step(t, _):
        at = pl.ds(pl.multiple_of(t * cols, cols), cols)
        x1[:, at] = tokens_ref[:, at].astype(jnp.float32) + transposed(mixed_ref[...], w_out[at, :])
        return 0

    lax.fori_loop(0, width // cols, out_step, 0)

    def normal(at):
        values = x1[at, :]
        mean = jnp.mean(values, axis=-1, keepdims=True)
        centred = values - mean
        scale = lax.rsqrt(jnp.mean(centred * centred, axis=-1, keepdims=True) + eps_norm)
        return centred * scale, scale

    def norm_step(i, _):
        at = pl.ds(pl.multiple_of(i * some, some), some)
        unit, _ = normal(at)
        right_ref[1, at, :] = (unit * gains_ref[1:2, :]).astype(jnp.bfloat16)
        right_ref[2, at, :] = (cot_ref[at, :].astype(jnp.float32) * live(i)).astype(jnp.bfloat16)
        return 0

    lax.fori_loop(0, rows_all // some, norm_step, 0)
    result[...] = x1[...]
    dnorm[...] = jnp.zeros_like(dnorm)
    for j in range(tiles):
        for copy in copies(j):
            copy.wait()
        norm, grad = right_ref[1], right_ref[2]
        one = transposed(norm, w_one[j])
        two = transposed(norm, w_two[j])
        back = transposed(grad, w_down[j])
        share = 0.5 * (1.0 + lax.erf(one * (0.5**0.5)))
        gelu = one * share
        slope = share + one * (jnp.exp(-0.5 * one * one) * (0.5 / math.pi) ** 0.5)
        low = (gelu * two).astype(jnp.bfloat16)
        d_one = (back * two * slope).astype(jnp.bfloat16)
        d_two = (back * gelu).astype(jnp.bfloat16)
        for k, part in enumerate((d_one, d_two, low)):
            left_ref[:, pl.ds(width + k * wide + j * tile, tile)] = part
        result[...] += jnp.dot(low, w_down[j], preferred_element_type=jnp.float32)
        dnorm[...] += jnp.dot(d_one, w_one[j], preferred_element_type=jnp.float32) + jnp.dot(
            d_two, w_two[j], preferred_element_type=jnp.float32
        )
    end = width + 3 * wide
    if left_ref.shape[1] > end:
        left_ref[:, end:] = jnp.zeros((rows_all, left_ref.shape[1] - end), left_ref.dtype)
    out_ref[...] = result[...].astype(out_ref.dtype)
    gain_ref[...] = jnp.zeros_like(gain_ref)

    def back_step(i, _):
        at = pl.ds(pl.multiple_of(i * some, some), some)
        unit, scale = normal(at)
        given = dnorm[at, :]
        inner = given * gains_ref[1:2, :]
        inner_mean = jnp.mean(inner, axis=-1, keepdims=True)
        along = jnp.mean(inner * unit, axis=-1, keepdims=True)
        grad = cot_ref[at, :].astype(jnp.float32) * live(i)
        grad = grad + scale * (inner - inner_mean - unit * along)
        back_ref[at, :] = grad
        left_ref[at, 0:width] = grad.astype(jnp.bfloat16)
        gain_ref[1:2, :] += jnp.sum(given * unit, axis=0, keepdims=True)
        return 0

    lax.fori_loop(0, rows_all // some, back_step, 0)

    def go_step(t, _):
        at = pl.ds(pl.multiple_of(t * cols, cols), cols)
        go_ref[:, at] = jnp.dot(
            left_ref[:, 0:width], w_out[:, at], preferred_element_type=jnp.float32
        ).astype(jnp.bfloat16)
        return 0

    lax.fori_loop(0, width // cols, go_step, 0)


def middle_call(mixed, tokens, cotangent, gains, lengths, stack_b, left_cols, block_len):
    rows_all, width = tokens.shape
    low = jnp.bfloat16
    tile = 384
    tiles = FF_WIDE // tile
    vmem = pl.BlockSpec(memory_space=pltpu.VMEM)
    return pl.pallas_call(
        functools.partial(middle_kernel, tile, block_len),
        out_shape=(
            jax.ShapeDtypeStruct((rows_all, width), low),
            jax.ShapeDtypeStruct((rows_all, left_cols), low),
            jax.ShapeDtypeStruct((3, rows_all, width), low),
            jax.ShapeDtypeStruct((rows_all, width), low),
            jax.ShapeDtypeStruct((rows_all, width), jnp.float32),
            jax.ShapeDtypeStruct((8, width), jnp.float32),
        ),
        in_specs=[vmem] * 4 + [pl.BlockSpec(memory_space=pltpu.SMEM), pl.BlockSpec(memory_space=pl.ANY)],
        out_specs=(vmem,) * 6,
        scratch_shapes=[pltpu.VMEM((width, width), low)]
        + [pltpu.VMEM((tiles, tile, width), low)] * 3
        + [pltpu.VMEM((rows_all, width), jnp.float32)] * 3
        + [DMA((1 + 3 * tiles,))],
        compiler_params=pltpu.CompilerParams(vmem_limit_bytes=VMEM_BYTES),
        name="middle",
    )(mixed, tokens, cotangent, gains, lengths, stack_b)


def adam_kernel(per, unit_ref, a_ref, b_ref, *refs):
    grads = (refs[:per], refs[per : 2 * per])
    master, first, second, new_master, new_first, new_second = refs[2 * per :]
    for j in range(per):
        slot = pl.program_id(0) * per + j
        unit = unit_ref[slot]
        grad = jnp.where(unit == 0, grads[0][j][0], grads[1][j][0]).astype(jnp.float32)
        grad = jnp.where(unit >= 0, grad, 0.0)
        weight, one, two = adam_update(
            master[j], grad, first[j], second[j], rate_matrix, decay_matrix
        )
        new_master[j] = weight
        new_first[j] = one
        new_second[j] = two


def adam_call(kind, at_a, at_b, grads_a, grads_b, master, first, second):
    capacity, rows, width = master.shape
    per = max(p for p in range(1, 8) if capacity % p == 0)

    def unit_spec(j, chunk):
        return pl.BlockSpec(
            (1, rows, width), lambda i, kind, *at: (at[chunk][i * per + j], 0, 0)
        )

    slot_spec = pl.BlockSpec((per, rows, width), lambda i, kind, *at: (i, 0, 0))
    return pl.pallas_call(
        functools.partial(adam_kernel, per),
        grid_spec=pltpu.PrefetchScalarGridSpec(
            num_scalar_prefetch=3,
            grid=(capacity // per,),
            in_specs=[unit_spec(j, c) for c in range(2) for j in range(per)] + [slot_spec] * 3,
            out_specs=[slot_spec] * 3,
        ),
        out_shape=[jax.ShapeDtypeStruct(master.shape, jnp.float32)] * 3,
        compiler_params=pltpu.CompilerParams(vmem_limit_bytes=VMEM_BYTES),
        name="adamw",
    )(kind, at_a, at_b, *([grads_a] * per), *([grads_b] * per), master, first, second)


def pick_kernel(part_ref, master_ref, out_ref, got, sems):
    count, rows = got.shape[:2]

    def at(p):
        return pl.ds(pl.multiple_of(p * rows, rows), rows)

    def copy(p):
        return pltpu.make_async_copy(master_ref.at[part_ref[p]], got.at[p], sems.at[p])

    def start(p, _):
        @pl.when(part_ref[p] >= 0)
        def _():
            copy(p).start()

        return 0

    def end(p, _):
        @pl.when(part_ref[p] >= 0)
        def _():
            copy(p).wait()
            out_ref[at(p), :] = got[p].astype(out_ref.dtype)

        @pl.when(part_ref[p] < 0)
        def _():
            out_ref[at(p), :] = jnp.zeros((rows, out_ref.shape[1]), out_ref.dtype)

        return 0

    lax.fori_loop(0, count, start, 0)
    lax.fori_loop(0, count, end, 0)


def pick_call(part, parts):
    shape = (part.shape[0],) + parts.shape[1:]
    flat = (shape[0] * shape[1], shape[2])
    return pl.pallas_call(
        pick_kernel,
        grid_spec=pltpu.PrefetchScalarGridSpec(
            num_scalar_prefetch=1,
            grid=(1,),
            in_specs=[pl.BlockSpec(memory_space=pl.ANY)],
            out_specs=pl.BlockSpec(flat, lambda i, part: (0, 0)),
            scratch_shapes=[pltpu.VMEM(shape, parts.dtype), DMA((part.shape[0],))],
        ),
        out_shape=jax.ShapeDtypeStruct(flat, jnp.bfloat16),
        compiler_params=pltpu.CompilerParams(vmem_limit_bytes=VMEM_BYTES),
        name="pick",
    )(part, parts)


def place():
    ctx, shard = lax.axis_index("ctx"), lax.axis_index("shard")
    return ctx // 2, ctx % 2, shard // 2, shard % 2


def device_at(z, y, x, core):
    return (z * 2 + y, x * 2 + core)


def piece_at(zb, c, h, a, b):
    return (((zb * 2 + c) * 2 + h) * 2 + a) * 2 + b


def remote(src, dst, send, recv, device):
    return pltpu.make_async_remote_copy(
        src_ref=src, dst_ref=dst, send_sem=send, recv_sem=recv, device_id=device, device_id_type=MESH
    )


def greet(devices):
    barrier = pltpu.get_barrier_semaphore()
    for device in devices:
        pl.semaphore_signal(barrier, inc=1, device_id=device, device_id_type=MESH)
    pl.semaphore_wait(barrier, len(devices))


def line_neighbours():
    z, y, x, core = place()
    return [device_at(z, y, 1 - x, core), device_at(z, 1 - y, x, core), device_at(z, y, x, 1 - core)] + [
        device_at((z + d) % 4, y, x, core) for d in (1, 2, 3)
    ]


def rows_at(ref, piece, count, rows):
    return ref.at[pl.ds(pl.multiple_of(piece * rows, 16), count * rows)]


GATHER_SEMS = [DMA((2,))] + [DMA((2, 4, 2))] * 2 + [DMA((2, 4))] * 2 + [DMA((2, 4, 2))] * 2 + [DMA((4,))] * 2


class Gather:
    def __init__(self, own, buf, rows, sems):
        self.own, self.buf, self.rows = own, buf, rows
        self.lsem, self.zs, self.zr, self.fs, self.fr, self.ts, self.tr, self.ss, self.sr = sems
        self.z, self.y, self.x, self.core = z, y, x, core = place()
        self.xn = device_at(z, y, 1 - x, core)
        self.yn = device_at(z, 1 - y, x, core)
        self.sib = device_at(z, y, x, 1 - core)

    def side(self, h):
        return (self.y, self.x) if h == 0 else (self.x, self.y)

    def near(self, h):
        return (self.xn, self.yn) if h == 0 else (self.yn, self.xn)

    def piece(self, zb, h, a, b):
        return rows_at(self.buf, piece_at(zb, self.core, h, a, b), 1, self.rows)

    def keep(self, h):
        return pltpu.make_async_copy(self.own(h), self.piece(self.z, h, *self.side(h)), self.lsem.at[h])

    def up(self, d, h, step, src=None):
        ref = self.piece(self.z + d, h, *self.side(h))
        k, hop = (0, -d) if step > 0 else (1, d)
        return remote(
            ref if src is None else src,
            ref,
            self.zs.at[k, hop, h],
            self.zr.at[k, hop, h],
            device_at(self.z + step, self.y, self.x, self.core),
        )

    def got(self, d, h):
        ref = self.piece(self.z + d, h, *self.side(h))
        k, hop = (0 if d < 0 else 1), abs(d) - 1
        remote(ref, ref, self.zs.at[k, hop, h], self.zr.at[k, hop, h], self.xn).wait_recv()

    def first(self, zb, h, mine, src=None):
        a, b = self.side(h)
        ref = self.piece(zb, h, a, b if mine else 1 - b)
        return remote(
            ref if src is None else src, ref, self.fs.at[h, zb], self.fr.at[h, zb], self.near(h)[0]
        )

    def second(self, zb, h, j, mine, src=None):
        a, b = self.side(h)
        ref = self.piece(zb, h, a if mine else 1 - a, b if j == 0 else 1 - b)
        return remote(
            ref if src is None else src, ref, self.ts.at[h, zb, j], self.tr.at[h, zb, j], self.near(h)[1]
        )

    def whole(self, zb, c):
        ref = rows_at(self.buf, (zb * 2 + c) * 8, 8, self.rows)
        return remote(ref, ref, self.ss.at[zb], self.sr.at[zb], self.sib)

    def start(self):
        for h in range(2):
            self.keep(h).start()
        for h in range(2):

            @pl.when(self.z < 3)
            def _():
                self.up(0, h, 1, self.own(h)).start()

            @pl.when(self.z > 0)
            def _():
                self.up(0, h, -1, self.own(h)).start()

            self.first(self.z, h, True, self.own(h)).start()
        for h in range(2):
            self.second(self.z, h, 0, True, self.own(h)).start()
        for h in range(2):
            self.keep(h).wait()

    def there(self, d, work):
        if d == 0:
            work()
        else:
            pl.when((self.z + d >= 0) & (self.z + d < 4))(work)

    def line(self, d):
        def work():
            zb = self.z + d
            for h in range(2):
                self.got(d, h)
                if d < 0:

                    @pl.when(self.z < 3)
                    def _():
                        self.up(d, h, 1).start()
                else:

                    @pl.when(self.z > 0)
                    def _():
                        self.up(d, h, -1).start()

                self.first(zb, h, True).start()
            for h in range(2):
                self.second(zb, h, 0, True).start()

        self.there(d, work)

    def cross(self, d):
        def work():
            zb = self.z + d
            for h in range(2):
                self.first(zb, h, False).wait_recv()
                self.second(zb, h, 1, True).start()

        self.there(d, work)

    def close(self, d):
        def work():
            zb = self.z + d
            for h in range(2):
                for j in range(2):
                    self.second(zb, h, j, False).wait_recv()
            self.whole(zb, self.core).start()

        self.there(d, work)

    def finish(self, take=True):
        for h in range(2):
            for d in range(4):

                @pl.when((self.z - d >= 0) & (self.z < 3))
                def _():
                    self.up(-d, h, 1).wait_send()

                @pl.when((self.z + d < 4) & (self.z > 0))
                def _():
                    self.up(d, h, -1).wait_send()

        for zb in range(4):
            for h in range(2):
                self.first(zb, h, True).wait_send()
                for j in range(2):
                    self.second(zb, h, j, True).wait_send()
            self.whole(zb, self.core).wait_send()
            if take:
                self.whole(zb, 1 - self.core).wait_recv()


REDUCE_REFS = 10


def reduce_scratch(rows, width):
    def buf(n):
        return pltpu.VMEM((n * rows, width), jnp.bfloat16)

    return (
        [buf(32), buf(16), buf(8), buf(10)]
        + [DMA((4, 2, 2))] * 2
        + [DMA((4, 2))] * 3
        + [DMA((5, 2))]
    )


class Reduce:
    def __init__(self, rows, refs):
        self.acc, self.got1, self.got2, self.got3 = refs[:4]
        self.s1, self.r1, self.s2, self.r2, self.s3, self.r3 = refs[4:]
        self.rows = rows
        self.z, self.y, self.x, self.core = z, y, x, core = place()
        self.xn = device_at(z, y, 1 - x, core)
        self.yn = device_at(z, 1 - y, x, core)
        self.sib = device_at(z, y, x, 1 - core)

    def zb(self, t):
        s = self.z // 2
        return (3 - 3 * s, 2 - s, 1 - self.z + 4 * s, self.z)[t]

    def base(self, zb):
        return zb * 8

    def side(self, h):
        return (self.y, self.x) if h == 0 else (self.x, self.y)

    def near(self, h):
        return (self.yn, self.xn) if h == 0 else (self.xn, self.yn)

    def send1(self, t, h, q):
        zb = self.zb(t)
        a, b = self.side(h)
        b = 1 - b if q == 0 else b
        return remote(
            rows_at(self.acc, self.base(zb) + h * 4 + (1 - a) * 2 + b, 1, self.rows),
            rows_at(self.got1, zb * 4 + h * 2 + b, 1, self.rows),
            self.s1.at[zb, h, q],
            self.r1.at[zb, h, q],
            self.near(h)[0],
        )

    def send2(self, t, h):
        zb = self.zb(t)
        a, b = self.side(h)
        return remote(
            rows_at(self.acc, self.base(zb) + h * 4 + a * 2 + 1 - b, 1, self.rows),
            rows_at(self.got2, zb * 2 + h, 1, self.rows),
            self.s2.at[zb, h],
            self.r2.at[zb, h],
            self.near(h)[1],
        )

    def send3(self, t, h, up):
        zb = self.zb(t)
        a, b = self.side(h)
        slot = zb if up else zb + (4 - zb) * (1 - (self.z - 1 - zb + 2) // 3)
        return remote(
            rows_at(self.acc, self.base(zb) + h * 4 + a * 2 + b, 1, self.rows),
            rows_at(self.got3, slot * 2 + h, 1, self.rows),
            self.s3.at[t, h],
            self.r3.at[slot, h],
            device_at(self.z + (1 if up else -1), self.y, self.x, self.core),
        )

    def come3(self, slot, h):
        ref = rows_at(self.got3, slot * 2 + h, 1, self.rows)
        remote(ref, ref, self.s3.at[0, h], self.r3.at[slot, h], self.xn).wait_recv()
        a, b = self.side(h)
        zb = self.z if isinstance(slot, int) else slot
        self.add(self.base(zb) + h * 4 + a * 2 + b, self.got3, slot * 2 + h, 1)

    def add(self, at, ref, start, count):
        step = 48

        def body(i, _):
            to = pl.ds(pl.multiple_of(at * self.rows + i * step, 16), step)
            given = pl.ds(pl.multiple_of(start * self.rows + i * step, 16), step)
            self.acc[to, :] = self.acc[to, :] + ref[given, :]
            return 0

        lax.fori_loop(0, count * self.rows // step, body, 0)

    def go1(self, t, q):
        for h in range(2):
            self.send1(t, h, q).start()

    def one(self, t, q):
        zb = self.zb(t)
        for h in range(2):
            a, b = self.side(h)
            b = 1 - b if q == 0 else b
            self.send1(t, h, q).wait_recv()
            self.add(self.base(zb) + h * 4 + a * 2 + b, self.got1, zb * 4 + h * 2 + b, 1)
            if q == 0:
                self.send2(t, h).start()

    def two(self, t):
        zb = self.zb(t)
        for h in range(2):
            a, b = self.side(h)
            self.send2(t, h).wait_recv()
            self.add(self.base(zb) + h * 4 + a * 2 + b, self.got2, zb * 2 + h, 1)

    def tri(self, t):
        zb = self.zb(t)
        z = self.z
        for h in range(2):

            @pl.when(((zb > z) & (z > 0)) | ((zb < z) & (z < 3)))
            def _():
                self.come3(zb, h)

            @pl.when(zb > z)
            def _():
                self.send3(t, h, True).start()

            @pl.when(zb < z)
            def _():
                self.send3(t, h, False).start()

    def three(self):
        for h in range(2):

            @pl.when(self.z > 0)
            def _():
                self.come3(self.z, h)

            @pl.when(self.z < 3)
            def _():
                self.come3(4, h)

    def own(self, h):
        a, b = self.side(h)
        return rows_at(self.acc, self.base(self.z) + h * 4 + a * 2 + b, 1, self.rows)

    def finish(self):
        for t in range(4):
            for h in range(2):
                for q in range(2):
                    self.send1(t, h, q).wait_send()
                self.send2(t, h).wait_send()
                if t < 3:
                    ref = rows_at(self.got3, h, 1, self.rows)
                    remote(ref, ref, self.s3.at[t, h], self.r3.at[0, h], self.xn).wait_send()


def front_kernel(
    given_ref, tokens_ref, gains_ref, cos_ref, sin_ref, lengths_ref,
    oa_ref, ob_ref, heads, wide_ref, lse_ref, mixed_ref, norm_ref,
    stack, rows, seen, low, mixed, got_a, got_b, new_a, new_b, own_a, own_b, send, recv, csem, ql, qsend, qrecv, ml, msend, mrecv, *sems
):
    n = 8
    z, y, x, core = place()
    ctx, shard = lax.axis_index("ctx"), lax.axis_index("shard")
    m = len(GATHER_SEMS)
    rows_a, rows_b = own_a.shape[0] // 2, own_b.shape[0] // 2
    ga = Gather(lambda h: rows_at(own_a, h, 1, rows_a), stack, rows_a, sems[:m])
    gb = Gather(lambda h: rows_at(own_b, h, 1, rows_b), ob_ref, rows_b, sems[m:])
    _, slots, block_len, width = rows.shape
    seq, my_width = seen.shape[2:]
    greet([ga.xn, ga.sib] + [(lax.rem(ctx + d, n), shard) for d in range(1, n)])
    jobs = ((0, got_a, new_a, own_a), (8 * rows_a, got_b, new_b, own_b))

    def share(i, c, xb):
        start, got, new, own = jobs[i]
        size = own.shape[0]
        at = start + c * 2 * size
        if xb is None:
            return given_ref.at[pl.ds(pl.multiple_of(at, 16), 2 * size)]
        return given_ref[pl.ds(pl.multiple_of(at + xb * size, 16), size), :]

    def held(i, xb):
        size = jobs[i][3].shape[0]
        return pl.ds(pl.multiple_of(xb * size, 16), size)

    def to_core(i):
        return remote(share(i, 1 - core, None), jobs[i][1], send.at[i], recv.at[i], ga.sib)

    def to_x(i):
        start, got, new, own = jobs[i]
        return remote(got.at[held(i, 1 - x)], new, send.at[2 + i], recv.at[2 + i], ga.xn)

    def spread(i):
        start, got, new, own = jobs[i]
        to_core(i).wait_recv()
        got[held(i, 1 - x), :] = got[held(i, 1 - x), :] + share(i, core, 1 - x)
        to_x(i).start()
        own[...] = got[held(i, x), :] + share(i, core, x)

    def cross(i):
        start, got, new, own = jobs[i]
        to_x(i).wait_recv()
        own[...] = own[...] + new[...]

    def peer(d):
        return lax.rem(ctx + d, n)

    def lanes(owner):
        return pl.ds(pl.multiple_of(owner * my_width, my_width), my_width)

    def block(owner):
        return pl.ds(pl.multiple_of(owner * block_len, block_len), block_len)

    def head_copy(j, owner):
        return remote(
            rows.at[j, :, :, lanes(owner)], seen.at[j, :, block(ctx), :], qsend.at[j, owner], qrecv.at[j, ctx], (owner, shard)
        )

    def head_own(j):
        return pltpu.make_async_copy(rows.at[j, :, :, lanes(ctx)], seen.at[j, :, block(ctx), :], ql.at[j])

    def mixed_copy(s, d):
        return remote(
            low.at[s, block(peer(d)), :], mixed.at[s, :, lanes(ctx)], msend.at[s, d], mrecv.at[s, d], (peer(d), shard)
        )

    def mixed_own(s):
        return pltpu.make_async_copy(low.at[s, block(ctx), :], mixed.at[s, :, lanes(ctx)], ml.at[s])

    cols = 256
    tiles = width // cols
    per_z = 16 * rows_a // cols

    def region(i):
        s = z // 2
        t = z % 2
        return (
            z,
            (1 - t) * (1 - s) + s * (1 + t),
            2 * (1 - s) + s * (3 - 2 * t),
            3 * (1 - s),
        )[i]

    def norm():
        def step(i, _):
            at = pl.ds(pl.multiple_of(i * 64, 64), 64)
            values = layer_norm(tokens_ref[at, :].astype(jnp.float32), gains_ref[0:1, :])
            norm_ref[at, :] = values.astype(jnp.bfloat16)
            return 0

        lax.fori_loop(0, slots * block_len // 64, step, 0)

    def table(ref):
        one = ref[block(ctx), :]
        one = jnp.concatenate([one] * (cols // my_width), axis=1)
        return jnp.concatenate([one] * slots, axis=0)

    def qkv(i):
        zb = region(i)
        ga.whole(zb, 1 - core).wait_recv()

        def tile_step(k, _):
            tile = zb * per_z + k
            j, t = tile // tiles, tile % tiles
            at = pl.ds(pl.multiple_of(t * cols, cols), cols)
            weight = stack[pl.ds(pl.multiple_of(tile * cols, cols), cols), :]
            values = transposed(norm_ref[...], weight)
            turn = (j < 2).astype(jnp.float32)
            cos = table(cos_ref) * turn + (1.0 - turn)
            values = values * cos + half_turned(values) * (table(sin_ref) * turn)
            rows[j, :, :, at] = values.astype(jnp.bfloat16).reshape(slots, block_len, cols)
            for q in range(cols // my_width):
                owner = t * (cols // my_width) + q

                @pl.when(owner == ctx)
                def _():
                    head_own(j).start()

                @pl.when(owner != ctx)
                def _():
                    head_copy(j, owner).start()

            return 0

        lax.fori_loop(0, per_z, tile_step, 0)

    def heads_wait(j):
        head_own(j).wait()
        for d in range(1, n):
            ref = seen.at[j, :, block(peer(d)), :]
            remote(ref, ref, qsend.at[j, peer(d)], qrecv.at[j, peer(d)], (peer(d), shard)).wait_recv()

    def mixed_wait():
        for s in range(slots):
            mixed_own(s).wait()
            for d in range(1, n):
                mixed_copy(s, d).wait_recv()

    for i in range(2):
        to_core(i).start()
    spread(0)
    spread(1)
    cross(0)
    ga.start()
    norm()
    ga.line(-1), ga.line(1)
    ga.cross(0)
    ga.line(-2), ga.line(2)
    cross(1)
    gb.start()
    ga.cross(-1), ga.cross(1)
    ga.close(0)
    ga.line(-3), ga.line(3)
    ga.cross(-2), ga.cross(2)
    qkv(0)
    gb.line(-1), gb.line(1)
    ga.close(-1), ga.close(1)
    ga.cross(-3), ga.cross(3)
    qkv(1)
    gb.cross(0)
    ga.close(-2), ga.close(2)
    qkv(2)
    ga.close(-3), ga.close(3)
    gb.line(-2), gb.line(2)
    qkv(3)
    gb.cross(-1), gb.cross(1)
    gb.close(0)
    heads_wait(0)
    gb.line(-3), gb.line(3)
    gb.cross(-2), gb.cross(2)
    gb.close(-1), gb.close(1)
    heads_wait(1)
    heads_wait(2)
    keep_a = pltpu.make_async_copy(stack, oa_ref, csem.at[0])
    keep_heads = pltpu.make_async_copy(seen, heads, csem.at[1])
    keep_a.start()
    keep_heads.start()
    chunk = 256
    per_slot = seq // chunk

    def attend_at(i, _):
        s, c = i // per_slot, i % per_slot
        bias = key_bias(lengths_ref[s], seq)
        attend_step(
            c, seen.at[0, s], seen.at[1, s], seen.at[2, s], bias, low.at[s], wide_ref.at[s], lse_ref.at[s], chunk
        )

        @pl.when(c == per_slot - 1)
        def _():
            mixed_own(s).start()
            for d in range(1, n):
                mixed_copy(s, d).start()

        @pl.when(i == 0)
        def _():
            gb.cross(-3), gb.cross(3)

        @pl.when(i == 4)
        def _():
            gb.close(-2), gb.close(2)

        return 0

    lax.fori_loop(0, slots * per_slot, attend_at, 0)
    gb.close(-3), gb.close(3)
    mixed_wait()
    mixed_ref[...] = mixed[...]
    keep_a.wait()
    keep_heads.wait()
    for i in range(2):
        to_core(i).wait_send()
        to_x(i).wait_send()
    for d in range(1, n):
        for j in range(3):
            head_copy(j, peer(d)).wait_send()
        for s in range(slots):
            mixed_copy(s, d).wait_send()
    ga.finish(False)
    gb.finish()


def front_call(given, rows_a, rows_b, tokens, gains, cosine, sine, lengths, slots, block_len, collective_id):
    vmem = pl.BlockSpec(memory_space=pltpu.VMEM)
    any_ = pl.BlockSpec(memory_space=pl.ANY)
    low = jnp.bfloat16
    width = tokens.shape[1]
    seq = block_len * 8
    my_width = width // 8
    stack_a, stack_b = (jax.ShapeDtypeStruct((64 * r, width), low) for r in (rows_a, rows_b))
    scratch = [
        pltpu.VMEM(stack_a.shape, low),
        pltpu.VMEM((3, slots, block_len, width), low),
        pltpu.VMEM((3, slots, seq, my_width), low),
        pltpu.VMEM((slots, seq, my_width), low),
        pltpu.VMEM((slots, block_len, width), low),
    ]
    for pieces in (4, 2, 2):
        for r in (rows_a, rows_b):
            scratch.append(pltpu.VMEM((pieces * r, width), low))
    return pl.pallas_call(
        front_kernel,
        out_shape=(
            stack_a,
            stack_b,
            jax.ShapeDtypeStruct((3, slots, seq, my_width), low),
            jax.ShapeDtypeStruct((slots, seq, my_width), jnp.float32),
            jax.ShapeDtypeStruct((slots, seq, my_width), jnp.float32),
            jax.ShapeDtypeStruct((slots, block_len, width), low),
            jax.ShapeDtypeStruct((slots * block_len, width), low),
        ),
        in_specs=[vmem] * 5 + [pl.BlockSpec(memory_space=pltpu.SMEM)],
        out_specs=(any_, any_, any_, vmem, vmem, vmem, vmem),
        scratch_shapes=scratch
        + [DMA((4,)), DMA((4,)), DMA((2,)), DMA((3,)), DMA((3, 8)), DMA((3, 8)), DMA((slots,)), DMA((slots, 8)), DMA((slots, 8))]
        + GATHER_SEMS * 2,
        compiler_params=pltpu.CompilerParams(
            collective_id=collective_id, has_side_effects=True, vmem_limit_bytes=VMEM_BYTES
        ),
        name="spread_and_attend",
    )(given, tokens, gains, cosine, sine, lengths)


GAIN_SEMS = [DMA((6,)), DMA((6,))]


class GainSum:
    def __init__(self, ref, got, line, sems):
        self.ref, self.got, self.all = ref, got, line
        self.send, self.recv = sems
        self.z, self.y, self.x, self.core = place()

    def step(self, i):
        z, y, x, core = self.z, self.y, self.x, self.core
        to = (device_at(z, y, x, 1 - core), device_at(z, y, 1 - x, core), device_at(z, 1 - y, x, core))[i]
        return remote(self.ref, self.got.at[i], self.send.at[i], self.recv.at[i], to)

    def far(self, d):
        to = device_at((self.z + d) % 4, self.y, self.x, self.core)
        return remote(self.ref, self.all.at[self.z], self.send.at[2 + d], self.recv.at[2 + d], to)

    def begin(self, i):
        self.step(i).start()

    def end(self, i):
        self.step(i).wait()
        self.ref[...] = self.ref[...] + self.got[i]

    def begin_far(self):
        for d in (1, 2, 3):
            self.far(d).start()
        self.all[self.z] = self.ref[...]

    def end_far(self, out):
        for d in (1, 2, 3):
            self.far(d).wait()
        total = self.all[0]
        for i in range(1, 4):
            total = total + self.all[i]
        out[...] = total


def back_kernel(
    g_ref, qkv_ref, wide_ref, lse_ref, cos_ref, sin_ref, norm_ref, tokens_ref, gains_ref, middle_ref, gain_ref,
    left_ref, right_ref, w_ref, lengths_ref,
    oa_ref, ob_ref, og_ref, tok_ref,
    left_got, right_got, norm_got, rows_got, weight_ref, xsend, xrecv, heads, grad, rows, acc_k, acc_v, dnorm, gain, gain_got, gain_all, wsem, gl, gsend, grecv, dl, dsend, drecv, *refs
):
    n = 8
    slots, block_len, width = g_ref.shape
    seq, my_width = qkv_ref.shape[2:]
    chunk = 256
    per_slot = seq // chunk
    m = len(GATHER_SEMS)
    rows_a, rows_b = oa_ref.shape[0] // 64, ob_ref.shape[0] // 64
    ra = Reduce(rows_a, refs[:REDUCE_REFS])
    rb = Reduce(rows_b, refs[REDUCE_REFS : 2 * REDUCE_REFS])
    refs = refs[2 * REDUCE_REFS :]
    ga = Gather(ra.own, oa_ref, rows_a, refs[:m])
    gb = Gather(rb.own, ob_ref, rows_b, refs[m : 2 * m])
    gs = GainSum(gain, gain_got, gain_all, refs[2 * m :])
    z, y, x, core = place()
    ctx, shard = lax.axis_index("ctx"), lax.axis_index("shard")
    greet([ra.xn, ra.sib] + [(lax.rem(ctx + d, n), shard) for d in range(1, n)])

    def peer(d):
        return lax.rem(ctx + d, n)

    def lanes(owner):
        return pl.ds(pl.multiple_of(owner * my_width, my_width), my_width)

    def block(owner):
        return pl.ds(pl.multiple_of(owner * block_len, block_len), block_len)

    def go_copy(d):
        return remote(
            g_ref.at[:, :, lanes(peer(d))], grad.at[:, block(ctx), :], gsend.at[d], grecv.at[d], (peer(d), shard)
        )

    def back_copy(s, d):
        return remote(
            heads.at[:, s, block(peer(d)), :], rows.at[:, s, :, lanes(ctx)], dsend.at[s, d], drecv.at[s, d], (peer(d), shard)
        )

    def back_own(s):
        return pltpu.make_async_copy(heads.at[:, s, block(ctx), :], rows.at[:, s, :, lanes(ctx)], dl.at[s])

    go_own = pltpu.make_async_copy(g_ref.at[:, :, lanes(ctx)], grad.at[:, block(ctx), :], gl)
    w_copy = pltpu.make_async_copy(w_ref, weight_ref, wsem)
    cut = 128
    rows_all = slots * block_len

    def to_sib(src, dst, i):
        return remote(src, dst, xsend.at[i], xrecv.at[i], ra.sib)

    def left_copy(t, c):
        lane = pl.ds(pl.multiple_of((rb.zb(t) * 2 + c) * 8 * rows_b, cut), 8 * rows_b)
        return to_sib(left_ref.at[:, lane], left_got.at[rb.zb(t)], t)

    right_copy = to_sib(right_ref, right_got, 4)
    norm_copy = to_sib(norm_ref, norm_got, 5)
    def rows_copy(s):
        return to_sib(rows.at[:, s], rows_got.at[:, s], 6 + s)

    def given():
        left_copy(0, 1 - core).start()
        right_copy.start()
        for t in range(1, 4):
            left_copy(t, 1 - core).start()
        norm_copy.start()
        right_copy.wait_recv()

    def fill(t):
        zb = rb.zb(t)
        left_copy(t, core).wait_recv()
        count = 8 * rows_b // cut

        def step(i, _):
            g = (zb * 2 + core) * count + i
            kind = (g >= width // cut).astype(jnp.int32) + (g >= (width + 2 * FF_WIDE) // cut).astype(jnp.int32)
            mine = left_ref[:, pl.ds(pl.multiple_of(g * cut, cut), cut)]
            other = left_got[zb, :, pl.ds(pl.multiple_of(i * cut, cut), cut)]
            total = leading(mine, right_ref[kind]) + leading(other, right_got[kind])
            at = pl.ds(pl.multiple_of(zb * 8 * rows_b + i * cut, cut), cut)
            rb.acc[at, :] = total.astype(jnp.bfloat16)
            return 0

        lax.fori_loop(0, count, step, 0)
    cols = 256
    tiles = width // cols

    def rows_wait(s):
        back_own(s).wait()
        for d in range(1, n):
            back_copy(s, d).wait_recv()
        rows_copy(s).start()

    def both():
        norm_copy.wait_recv()
        for s in range(slots):
            rows_copy(s).wait_recv()

    def weight(t):
        zb = ra.zb(t)
        count = 8 * rows_a // cut

        def step(i, _):
            g = (zb * 2 + core) * count + i
            j = g * cut // width
            lane = pl.ds(pl.multiple_of(g * cut - j * width, cut), cut)
            total = leading(rows[j, :, :, lane].reshape(rows_all, cut), norm_ref[...])
            total += leading(rows_got[j, :, :, lane].reshape(rows_all, cut), norm_got[...])
            at = pl.ds(pl.multiple_of(zb * 8 * rows_a + i * cut, cut), cut)
            ra.acc[at, :] = total.astype(jnp.bfloat16)
            return 0

        lax.fori_loop(0, count, step, 0)

    def norm_step(t, _):
        at = pl.ds(pl.multiple_of(t * cols, cols), cols)
        total = None
        for j in range(3):
            left = rows[j].reshape(slots * block_len, width)
            right = weight_ref[pl.ds(j * width, width), at]
            part = jnp.dot(left, right, preferred_element_type=jnp.float32)
            total = part if total is None else total + part
        dnorm[:, at] = total
        return 0

    some = 64
    def token_step(i, _):
        at = pl.ds(pl.multiple_of(i * some, some), some)
        values = tokens_ref[at, :].astype(jnp.float32)
        mean = jnp.mean(values, axis=-1, keepdims=True)
        centred = values - mean
        scale = lax.rsqrt(jnp.mean(centred * centred, axis=-1, keepdims=True) + eps_norm)
        unit = centred * scale
        given = dnorm[at, :]
        inner = given * gains_ref[0:1, :]
        inner_mean = jnp.mean(inner, axis=-1, keepdims=True)
        along = jnp.mean(inner * unit, axis=-1, keepdims=True)
        grads = middle_ref[at, :] + scale * (inner - inner_mean - unit * along)
        tok_ref[at, :] = grads.astype(jnp.bfloat16)
        gain[0:1, :] += jnp.sum(given * unit, axis=0, keepdims=True)
        return 0

    def token():
        w_copy.wait()
        lax.fori_loop(0, tiles, norm_step, 0)
        gain[...] = gain_ref[...]
        lax.fori_loop(0, slots * block_len // some, token_step, 0)
        gs.begin(0)

    for d in range(1, n):
        go_copy(d).start()
    go_own.start()
    given()
    fill(0)
    rb.go1(0, 0)
    rb.go1(0, 1)
    fill(1)
    fill(2)
    fill(3)
    w_copy.start()
    go_own.wait()
    for d in range(1, n):
        go_copy(d).wait_recv()

    def attend_step(i, _):
        s, c = i // per_slot, i % per_slot
        slot = (
            qkv_ref.at[0, s], qkv_ref.at[1, s], qkv_ref.at[2, s], grad.at[s], wide_ref.at[s], lse_ref.at[s],
            key_bias(lengths_ref[s], seq), cos_ref, sin_ref, heads.at[0, s], heads.at[1, s], heads.at[2, s], acc_k, acc_v, chunk,
        )

        @pl.when(c == 0)
        def _():
            acc_k[...] = jnp.zeros_like(acc_k)
            acc_v[...] = jnp.zeros_like(acc_v)

        attend_back_step(c, *slot)

        @pl.when(c == per_slot - 1)
        def _():
            attend_back_end(*slot)
            back_own(s).start()
            for d in range(1, n):
                back_copy(s, d).start()

        @pl.when(i == 1)
        def _():
            rb.one(0, 0)
            rb.go1(1, 0)
            rb.one(0, 1)
            rb.go1(1, 1)

        return 0

    lax.fori_loop(0, slots * per_slot, attend_step, 0)
    rb.two(0)
    rb.one(1, 0)
    rb.go1(2, 0)
    rb.one(1, 1)
    rb.go1(2, 1)
    rb.tri(0)
    rb.two(1)
    rb.one(2, 0)
    rb.go1(3, 0)
    rb.one(2, 1)
    rb.go1(3, 1)
    rb.tri(1)
    rb.two(2)
    rb.one(3, 0)
    rb.one(3, 1)
    rb.tri(2)
    rows_wait(0)
    rows_wait(1)
    both()
    weight(0)
    ra.go1(0, 0)
    ra.go1(0, 1)
    weight(1)
    ra.go1(1, 0)
    ra.go1(1, 1)
    rb.two(3)
    weight(2)
    ra.go1(2, 0)
    ra.go1(2, 1)
    weight(3)
    ra.go1(3, 0)
    ra.go1(3, 1)
    ra.one(0, 0)
    ra.one(0, 1)
    rb.three()
    gb.start()
    token()
    ra.one(1, 0)
    ra.one(1, 1)
    ra.two(0)
    ra.one(2, 0)
    ra.one(2, 1)
    ra.tri(0)
    ra.two(1)
    gb.line(-1), gb.line(1)
    ra.one(3, 0)
    ra.one(3, 1)
    ra.tri(1)
    ra.two(2)
    gb.cross(0)
    gs.end(0)
    gs.begin(1)
    ra.tri(2)
    ra.two(3)
    gb.line(-2), gb.line(2)
    ra.three()
    ga.start()
    gb.cross(-1), gb.cross(1)
    gs.end(1)
    gs.begin(2)
    gb.close(0)
    gb.line(-3), gb.line(3)
    ga.line(-1), ga.line(1)
    gb.cross(-2), gb.cross(2)
    gs.end(2)
    gs.begin_far()
    ga.cross(0)
    gb.close(-1), gb.close(1)
    ga.line(-2), ga.line(2)
    gb.cross(-3), gb.cross(3)
    ga.cross(-1), ga.cross(1)
    ga.close(0)
    gb.close(-2), gb.close(2)
    ga.line(-3), ga.line(3)
    ga.cross(-2), ga.cross(2)
    ga.close(-1), ga.close(1)
    gb.close(-3), gb.close(3)
    ga.cross(-3), ga.cross(3)
    ga.close(-2), ga.close(2)
    ga.close(-3), ga.close(3)
    gs.end_far(og_ref)
    for d in range(1, n):
        go_copy(d).wait_send()
        for s in range(slots):
            back_copy(s, d).wait_send()
    for t in range(4):
        left_copy(t, 1 - core).wait_send()
    for copy in [right_copy, norm_copy] + [rows_copy(s) for s in range(slots)]:
        copy.wait_send()
    ra.finish(), rb.finish(), ga.finish(), gb.finish()


def back_call(
    grad_rows, qkv_heads, wide, lse, cosine, sine, norm_one, tokens, gains, grad_middle, gain_part, left, right, w_qkv, lengths, collective_id
):
    any_ = pl.BlockSpec(memory_space=pl.ANY)
    vmem = pl.BlockSpec(memory_space=pltpu.VMEM)
    low = jnp.bfloat16
    slots, block_len, width = grad_rows.shape
    seq, my_width = qkv_heads.shape[2:]
    rows_all = slots * block_len
    gain = gain_part.shape
    rows_a, rows_b = w_qkv.shape[0] // 64, left.shape[1] // 64
    return pl.pallas_call(
        back_kernel,
        out_shape=(
            jax.ShapeDtypeStruct(w_qkv.shape, low),
            jax.ShapeDtypeStruct((64 * rows_b, width), low),
            jax.ShapeDtypeStruct(gain, jnp.float32),
            jax.ShapeDtypeStruct((rows_all, width), low),
        ),
        in_specs=[vmem] * 13 + [any_, pl.BlockSpec(memory_space=pltpu.SMEM)],
        out_specs=(any_, any_, vmem, vmem),
        scratch_shapes=[
            pltpu.VMEM((4, rows_all, 8 * rows_b), low),
            pltpu.VMEM(right.shape, low),
            pltpu.VMEM((rows_all, width), low),
            pltpu.VMEM((3, slots, block_len, width), low),
            pltpu.VMEM(w_qkv.shape, low),
            DMA((6 + slots,)),
            DMA((6 + slots,)),
            pltpu.VMEM(qkv_heads.shape, low),
            pltpu.VMEM((slots, seq, my_width), low),
            pltpu.VMEM((3, slots, block_len, width), low),
            pltpu.VMEM((seq, my_width), jnp.float32),
            pltpu.VMEM((seq, my_width), jnp.float32),
            pltpu.VMEM((rows_all, width), jnp.float32),
            pltpu.VMEM(gain, jnp.float32),
            pltpu.VMEM((3,) + gain, jnp.float32),
            pltpu.VMEM((4,) + gain, jnp.float32),
            DMA,
            DMA,
            DMA((8,)),
            DMA((8,)),
            DMA((slots,)),
            DMA((slots, 8)),
            DMA((slots, 8)),
        ]
        + reduce_scratch(rows_a, width)
        + reduce_scratch(rows_b, width)
        + GATHER_SEMS * 2
        + GAIN_SEMS,
        compiler_params=pltpu.CompilerParams(
            collective_id=collective_id, has_side_effects=True, vmem_limit_bytes=VMEM_BYTES
        ),
        name="back_and_sum",
    )(
        grad_rows, qkv_heads, wide, lse, cosine, sine, norm_one, tokens, gains, grad_middle, gain_part, left, right, w_qkv, lengths
    )


def to_heads(values):
    return lax.all_to_all(values, "ctx", split_axis=3, concat_axis=2, tiled=True)


def to_rows(values):
    return lax.all_to_all(values, "ctx", split_axis=2, concat_axis=3, tiled=True)


def shards(
    fast,
    tokens,
    cotangent,
    lengths,
    unit_owner,
    master,
    first_moment,
    second_moment,
    norm_gains,
    gain_first,
    gain_second,
):
    slots, block_len, width = tokens.shape
    groups = lax.axis_size("shard")
    n = lax.axis_size("ctx")
    ctx, shard = lax.axis_index("ctx"), lax.axis_index("shard")
    capacity, unit_rows, _ = master.shape
    units = unit_owner.shape[0]
    rows_all = slots * block_len
    seq = block_len * n
    device_count = n * groups
    my_width = width // n

    low = jnp.bfloat16
    rows_a = 3 * width
    rows_b = width + 3 * FF_WIDE
    split = rows_a // unit_rows
    lead, ff_units, wide_units = (r // unit_rows for r in (width, FF, FF_WIDE))

    def unit_of(block, chunk):
        if chunk == 0:
            return jnp.where(block < split, block, -1)
        inner = block - lead
        third = inner // wide_units
        at = inner - third * wide_units
        there = (block < lead) | ((at < ff_units) & (third < 3))
        return jnp.where(there, split + jnp.where(block < lead, block, lead + third * ff_units + at), -1)

    def block_of(unit):
        inner = unit - split - lead
        third = jnp.maximum(inner, 0) // ff_units
        return unit - split + third * (wide_units - ff_units)

    part_rows = 16
    per_unit = unit_rows // part_rows
    parts = master.reshape(capacity * per_unit, part_rows, width)

    def units_at(chunk, per, wanted):
        at = wanted[..., None] * (per // part_rows) + jnp.arange(per // part_rows, dtype=jnp.int32)
        at = at.reshape(-1)
        return unit_of(at // per_unit, chunk), at % per_unit

    def pick(unit, inner):
        owner, rank = unit_places(unit_owner, unit)
        mine = (owner == shard) & (unit >= 0)
        return pick_call(jnp.where(mine, rank * per_unit + inner, -1), parts)

    def piece_rows(count, pieces):
        return -(-count // (pieces * part_rows)) * part_rows

    cos_seq, sin_seq = rope_tables(seq, my_width // HEAD_DIM)
    flat_tokens = tokens.reshape(rows_all, width)

    if fast:
        z, y, x, core = place()
        wanted = jnp.stack(
            [
                jnp.stack([jnp.stack([piece_at(z, c, 0, y, q), piece_at(z, c, 1, q, y)]) for q in range(2)])
                for c in range(2)
            ]
        )
        per_a, per_b = piece_rows(rows_a, 64), piece_rows(rows_b, 64)
        at_pieces = [units_at(0, per_a, wanted), units_at(1, per_b, wanted)]
        given = pick(*(jnp.concatenate(both) for both in zip(*at_pieces)))
        stack_a, stack_b, qkv_heads, wide, lse, mixed_low, norm_one = front_call(
            given, per_a, per_b, flat_tokens, norm_gains, cos_seq, sin_seq, lengths, slots, block_len, 0
        )
    else:
        wanted = ctx * groups + jnp.arange(groups, dtype=jnp.int32)
        stacks = []
        for chunk, count in enumerate((rows_a, rows_b)):
            share = pick(*units_at(chunk, piece_rows(count, device_count), wanted))
            own = lax.psum_scatter(share, "shard", scatter_dimension=0, tiled=True)
            stacks.append(lax.all_gather(own, BOTH, axis=0, tiled=True))
        stack_a, stack_b = stacks
        inputs = flat_tokens.astype(jnp.float32)
        norm_one = layer_norm(inputs, norm_gains[0]).astype(low)
        cos_rows, sin_rows = (
            jnp.tile(lax.dynamic_slice_in_dim(table, ctx * block_len, block_len, 0), (slots, 256 // my_width))
            for table in (cos_seq, sin_seq)
        )
        qkv = qkv_call(norm_one, stack_a, cos_rows, sin_rows)
        qkv_heads = to_heads(qkv.reshape(3, slots, block_len, width))
        mixed_heads, wide, lse = attend_call(qkv_heads, lengths)
        mixed_low = to_rows(mixed_heads[None])
    mixed_low = mixed_low.reshape(rows_all, width)
    left_cols = 64 * piece_rows(rows_b, 64)
    output, left, right, grad_heads_rows, grad_middle, gain_part = middle_call(
        mixed_low, flat_tokens, cotangent.reshape(rows_all, width), norm_gains, lengths, stack_b, left_cols, block_len
    )
    output = output.reshape(slots, block_len, width)
    grad_heads_rows = grad_heads_rows.reshape(slots, block_len, width)

    if fast:
        all_a, all_b, gain_grad, token_grad = back_call(
            grad_heads_rows, qkv_heads, wide, lse, cos_seq, sin_seq, norm_one, flat_tokens,
            norm_gains, grad_middle, gain_part, left, right, stack_a, lengths, 1,
        )
    else:
        cuts = (0, width, width + 2 * FF_WIDE, rows_b)
        grads_b = jnp.concatenate(
            [leading(left[:, cuts[i] : cuts[i + 1]], right[i]).astype(low) for i in range(3)]
            + [jnp.zeros((stack_b.shape[0] - rows_b, width), low)],
            axis=0,
        )
        grad_heads = to_heads(grad_heads_rows[None])[0]
        grad_qkv_heads = attend_back_call(qkv_heads, grad_heads, wide, lse, lengths, cos_seq, sin_seq)
        grad_qkv_low = to_rows(grad_qkv_heads).reshape(3, rows_all, width)
        grad_norm_one = sum(
            jnp.dot(
                grad_qkv_low[i],
                stack_a[i * width : (i + 1) * width],
                preferred_element_type=jnp.float32,
            )
            for i in range(3)
        )
        _, norm_back_one = jax.vjp(layer_norm, inputs, norm_gains[0])
        grad_input_part, grad_gain_one = norm_back_one(grad_norm_one)
        token_grad = (grad_middle + grad_input_part).astype(low)
        grads_a = jnp.concatenate(
            [leading(grad_qkv_low[i], norm_one).astype(low) for i in range(3)]
            + [jnp.zeros((stack_a.shape[0] - rows_a, width), low)],
            axis=0,
        )
        all_a, all_b = (
            lax.all_gather(
                lax.psum_scatter(g, BOTH, scatter_dimension=0, tiled=True), BOTH, axis=0, tiled=True
            )
            for g in (grads_a, grads_b)
        )
        gain_grad = lax.psum(gain_part.at[0].set(grad_gain_one), BOTH)
    token_grad = token_grad.reshape(slots, block_len, width)
    gain_grad = gain_grad[:2]
    all_a = all_a.reshape(-1, unit_rows, width)
    all_b = all_b.reshape(-1, unit_rows, width)

    every = jnp.arange(units, dtype=jnp.int32)
    rank = unit_places(unit_owner, every)[1]
    here = (unit_owner == shard) & (rank == jnp.arange(capacity, dtype=jnp.int32)[:, None])
    unit_of_slot = jnp.sum(jnp.where(here, every + 1, 0), axis=1) - 1
    kind = jnp.where(unit_of_slot < 0, -1, (unit_of_slot >= split).astype(jnp.int32))
    at_a = jnp.where(kind == 0, unit_of_slot, 0)
    at_b = jnp.where(kind == 1, block_of(unit_of_slot), 0)
    new_master, new_first, new_second = adam_call(
        kind, at_a, at_b, all_a, all_b, master, first_moment, second_moment
    )
    new_gains, new_gain_first, new_gain_second = adam_update(
        norm_gains, gain_grad, gain_first, gain_second, rate_gain, 0.0
    )
    return (
        output,
        token_grad,
        new_master,
        new_first,
        new_second,
        new_gains,
        new_gain_first,
        new_gain_second,
    )


def solution(mesh):
    fast = dict(mesh.shape) == {"ctx": 8, "shard": 4}
    return jax.shard_map(
        functools.partial(shards, fast),
        mesh=mesh,
        in_specs=(
            P("shard", "ctx", None),
            P("shard", "ctx", None),
            P("shard"),
            P(),
            P("shard", None, None),
            P("shard", None, None),
            P("shard", None, None),
            P(),
            P(),
            P(),
        ),
        out_specs=(
            P("shard", "ctx", None),
            P("shard", "ctx", None),
            P("shard", None, None),
            P("shard", None, None),
            P("shard", None, None),
            P(),
            P(),
            P(),
        ),
        check_vma=False,
    )
```

```python
import functools
import math

import jax
import jax.numpy as jnp
import numpy as np
from jax import lax
from jax.experimental import pallas as pl
from jax.experimental.pallas import tpu as pltpu
from jax.sharding import PartitionSpec as P

HEADS = 16
HEAD_DIM = 64
FF = 2624
FF_WIDE = -(-FF // 128) * 128
STEP = 10
MESH = pl.DeviceIdType.MESH
DMA = pltpu.SemaphoreType.DMA

eps_norm = 1e-05
rope_base = 160000.0
mask_fill = -1e30
beta_one = 0.9
beta_two = 0.98
adam_eps = 1e-06
rate_matrix = 0.03
rate_gain = 0.6
decay_matrix = 0.01
BOTH = ("ctx", "shard")
VMEM_BYTES = 60 * 2**20


def transposed(left, right):
    return lax.dot_general(
        left, right, (((1,), (1,)), ((), ())), preferred_element_type=jnp.float32
    )


def leading(left, right):
    return lax.dot_general(
        left, right, (((0,), (0,)), ((), ())), preferred_element_type=jnp.float32
    )


def layer_norm(values, gain):
    row_mean = jnp.mean(values, axis=-1, keepdims=True)
    centred = values - row_mean
    variance = jnp.mean(centred * centred, axis=-1, keepdims=True)
    return centred * lax.rsqrt(variance + eps_norm) * gain


def rope_tables(seq, heads):
    half_dim = HEAD_DIM // 2
    inverse = rope_base ** (-2.0 * np.arange(half_dim) / HEAD_DIM)
    angles = np.arange(seq)[:, None] * inverse.astype(np.float32).astype(np.float64)[None, :]
    angles = angles.astype(np.float32).astype(np.float64)
    cosine, sine = np.cos(angles), np.sin(angles)
    cosine = np.concatenate([cosine, cosine] * heads, axis=1)
    sine = np.concatenate([-sine, sine] * heads, axis=1)
    return jnp.asarray(cosine, jnp.float32), jnp.asarray(sine, jnp.float32)


def half_turned(values):
    width = values.shape[-1]
    half = HEAD_DIM // 2
    lane = lax.broadcasted_iota(jnp.int32, values.shape, values.ndim - 1)
    if width == HEAD_DIM:
        return jnp.concatenate([values[:, half:], values[:, :half]], axis=1)
    ahead = pltpu.roll(values, width - half, axis=1)
    behind = pltpu.roll(values, half, axis=1)
    return jnp.where(lane % HEAD_DIM < half, ahead, behind)


def own_places(unit_owner, owner, chosen):
    every = jnp.arange(unit_owner.shape[0], dtype=jnp.int32)
    held = unit_owner == owner
    mine = jnp.any((every == chosen[:, None]) & held, axis=1)
    return mine, jnp.sum(((every < chosen[:, None]) & held).astype(jnp.int32), axis=1)


def adam_update(weight, gradient, first_old, second_old, step_rate, weight_decay):
    first_new = beta_one * first_old + (1.0 - beta_one) * gradient
    second_new = beta_two * second_old + (1.0 - beta_two) * gradient * gradient
    first_fix = 1.0 - beta_one**STEP
    second_fix = 1.0 - beta_two**STEP
    adam_step = first_new / first_fix / (jnp.sqrt(second_new / second_fix) + adam_eps)
    return (weight - step_rate * (adam_step + weight_decay * weight), first_new, second_new)


def qkv_kernel(norm_ref, w_ref, cos_ref, sin_ref, out_ref):
    tile = pl.program_id(0)
    turned_tiles = 2 * pl.num_programs(0) // 3
    values = transposed(norm_ref[...], w_ref[...])

    @pl.when(tile < turned_tiles)
    def _():
        out_ref[0] = (values * cos_ref[...] + half_turned(values) * sin_ref[...]).astype(
            out_ref.dtype
        )

    @pl.when(tile >= turned_tiles)
    def _():
        out_ref[0] = values.astype(out_ref.dtype)


def qkv_call(norm_one, w_qkv, cosine, sine):
    rows, width = norm_one.shape
    cols = 256
    tiles = width // cols
    return pl.pallas_call(
        qkv_kernel,
        grid=(3 * width // cols,),
        in_specs=[
            pl.BlockSpec((rows, width), lambda i: (0, 0)),
            pl.BlockSpec((cols, width), lambda i: (i, 0)),
            pl.BlockSpec((rows, cols), lambda i: (0, 0)),
            pl.BlockSpec((rows, cols), lambda i: (0, 0)),
        ],
        out_specs=pl.BlockSpec((1, rows, cols), lambda i: (i // tiles, 0, i % tiles)),
        out_shape=jax.ShapeDtypeStruct((3, rows, width), jnp.bfloat16),
        name="qkv",
    )(norm_one, w_qkv, cosine, sine)


def head_only(values, head):
    width = values.shape[-1]
    if width == HEAD_DIM:
        return values
    lane = lax.broadcasted_iota(jnp.int32, values.shape, 1)
    return jnp.where(lane // HEAD_DIM == head, values, jnp.zeros_like(values))


def key_bias(length, seq):
    position = lax.broadcasted_iota(jnp.int32, (1, seq), 1)
    return jnp.where(position < length, 0.0, mask_fill).astype(jnp.float32)


def attend_step(i, q_ref, k_ref, v_ref, bias, out_ref, wide_ref, lse_ref, chunk):
    width = k_ref.shape[1]
    heads = width // HEAD_DIM
    rows = pl.ds(pl.multiple_of(i * chunk, chunk), chunk)
    query = q_ref[rows, :] * jnp.bfloat16(0.125)
    total = None
    stats = None
    for h in range(heads):
        scores = transposed(query, head_only(k_ref[...], h)) + bias
        top = jnp.max(scores, axis=-1, keepdims=True)
        weights = jnp.exp(scores - top)
        norm = jnp.sum(weights, axis=-1, keepdims=True)
        low = (weights * (1.0 / norm)).astype(jnp.bfloat16)
        part = jnp.dot(low, head_only(v_ref[...], h), preferred_element_type=jnp.float32)
        lse = jnp.broadcast_to(top + jnp.log(norm), (chunk, width))
        total = part if total is None else total + part
        if stats is None:
            stats = lse
        else:
            lane = lax.broadcasted_iota(jnp.int32, lse.shape, 1)
            stats = jnp.where(lane // HEAD_DIM == h, lse, stats)
    out_ref[rows, :] = total.astype(jnp.bfloat16)
    wide_ref[rows, :] = total
    lse_ref[rows, :] = stats


def attend_slot(*args):
    def step(i, _):
        attend_step(i, *args)
        return 0

    lax.fori_loop(0, args[1].shape[0] // args[-1], step, 0)


def turned_back(grad, cos, sin):
    return grad * cos - half_turned(grad) * sin


def attend_back_step(
    i, q_ref, k_ref, v_ref, g_ref, wide_ref, lse_ref, bias, cos, sin, dq_ref, dk_ref, dv_ref, acc_k, acc_v, chunk
):
    seq, width = k_ref.shape
    heads = width // HEAD_DIM
    rows = pl.ds(pl.multiple_of(i * chunk, chunk), chunk)
    query = q_ref[rows, :]
    grad = g_ref[rows, :]
    lse_all = lse_ref[rows, :]
    both = grad.astype(jnp.float32) * wide_ref[rows, :]
    total = None
    for h in range(heads):
        key = head_only(k_ref[...], h)
        lse = lse_all[:, h * HEAD_DIM : h * HEAD_DIM + 1]
        delta = jnp.sum(head_only(both, h), axis=-1, keepdims=True)
        scores = transposed(query * jnp.bfloat16(0.125), key)
        weights = jnp.exp(scores + (bias - lse))
        back = transposed(grad, head_only(v_ref[...], h))
        low = (weights * (back - delta)).astype(jnp.bfloat16)
        part = jnp.dot(low, key, preferred_element_type=jnp.float32)
        total = part if total is None else total + part
        acc_v[...] += leading(weights.astype(jnp.bfloat16), head_only(grad, h))
        acc_k[...] += leading(low, head_only(query, h))
    dq_ref[rows, :] = turned_back(total * 0.125, cos[rows, :], sin[rows, :]).astype(jnp.bfloat16)


def attend_back_end(
    q_ref, k_ref, v_ref, g_ref, wide_ref, lse_ref, bias, cos, sin, dq_ref, dk_ref, dv_ref, acc_k, acc_v, chunk
):
    dk_ref[...] = turned_back(acc_k[...] * 0.125, cos[...], sin[...]).astype(jnp.bfloat16)
    dv_ref[...] = acc_v[...].astype(jnp.bfloat16)


def attend_back_slot(*args):
    acc_k, acc_v, chunk = args[-3:]
    acc_k[...] = jnp.zeros_like(acc_k)
    acc_v[...] = jnp.zeros_like(acc_v)

    def step(i, _):
        attend_back_step(i, *args)
        return 0

    lax.fori_loop(0, args[1].shape[0] // chunk, step, 0)
    attend_back_end(*args)


def attend_kernel(slots, chunk, qkv_ref, lengths_ref, out_ref, wide_ref, lse_ref):
    for s in range(slots):
        attend_slot(
            qkv_ref.at[0, s], qkv_ref.at[1, s], qkv_ref.at[2, s], key_bias(lengths_ref[s], qkv_ref.shape[2]),
            out_ref.at[s], wide_ref.at[s], lse_ref.at[s], chunk,
        )


def attend_call(qkv, lengths):
    _, slots, seq, width = qkv.shape
    chunk = 256
    return pl.pallas_call(
        functools.partial(attend_kernel, slots, chunk),
        out_shape=(
            jax.ShapeDtypeStruct((slots, seq, width), jnp.bfloat16),
            jax.ShapeDtypeStruct((slots, seq, width), jnp.float32),
            jax.ShapeDtypeStruct((slots, seq, width), jnp.float32),
        ),
        in_specs=[pl.BlockSpec(memory_space=pltpu.VMEM), pl.BlockSpec(memory_space=pltpu.SMEM)],
        compiler_params=pltpu.CompilerParams(vmem_limit_bytes=VMEM_BYTES),
        name="attend",
    )(qkv, lengths)


def attend_back_kernel(slots, chunk, qkv_ref, g_ref, wide_ref, lse_ref, lengths_ref, cos_ref, sin_ref, out_ref, acc_k, acc_v):
    for s in range(slots):
        attend_back_slot(
            qkv_ref.at[0, s], qkv_ref.at[1, s], qkv_ref.at[2, s], g_ref.at[s],
            wide_ref.at[s], lse_ref.at[s], key_bias(lengths_ref[s], qkv_ref.shape[2]), cos_ref, sin_ref,
            out_ref.at[0, s], out_ref.at[1, s], out_ref.at[2, s], acc_k, acc_v, chunk,
        )


def attend_back_call(qkv, grad_heads, wide, lse, lengths, cosine, sine):
    _, slots, seq, width = qkv.shape
    chunk = 256
    return pl.pallas_call(
        functools.partial(attend_back_kernel, slots, chunk),
        out_shape=jax.ShapeDtypeStruct(qkv.shape, jnp.bfloat16),
        in_specs=[pl.BlockSpec(memory_space=pltpu.VMEM)] * 4
        + [pl.BlockSpec(memory_space=pltpu.SMEM)]
        + [pl.BlockSpec(memory_space=pltpu.VMEM)] * 2,
        scratch_shapes=[pltpu.VMEM((seq, width), jnp.float32)] * 2,
        compiler_params=pltpu.CompilerParams(vmem_limit_bytes=VMEM_BYTES),
        name="attend_back",
    )(qkv, grad_heads, wide, lse, lengths, cosine, sine)


def middle_kernel(
    tile, block_len, mixed_ref, tokens_ref, cot_ref, gains_ref, lengths_ref, w_ref,
    out_ref, left_ref, right_ref, go_ref, back_ref, gain_ref,
    w_out, w_one, w_two, w_down, x1, result, dnorm, sems
):
    rows_all, width = tokens_ref.shape
    wide = w_one.shape[0] * tile
    tiles = wide // tile
    cols = 256
    some = 64
    start = lax.axis_index("ctx") * block_len

    def live(i):
        slot, inner = i * some // block_len, i * some % block_len
        position = start + inner + lax.broadcasted_iota(jnp.int32, (some, 1), 0)
        return (position < lengths_ref[slot]).astype(jnp.float32)

    def copies(j):
        rows = [pl.ds(width + k * wide + j * tile, tile) for k in range(3)]
        return [
            pltpu.make_async_copy(w_ref.at[r], to.at[j], sems.at[1 + j * 3 + k])
            for k, (r, to) in enumerate(zip(rows, (w_one, w_two, w_down)))
        ]

    first = pltpu.make_async_copy(w_ref.at[pl.ds(0, width)], w_out, sems.at[0])
    first.start()
    for j in range(tiles):
        for copy in copies(j):
            copy.start()
    right_ref[0] = mixed_ref[...]
    first.wait()

    def out_step(t, _):
        at = pl.ds(pl.multiple_of(t * cols, cols), cols)
        x1[:, at] = tokens_ref[:, at].astype(jnp.float32) + transposed(mixed_ref[...], w_out[at, :])
        return 0

    lax.fori_loop(0, width // cols, out_step, 0)

    def normal(at):
        values = x1[at, :]
        mean = jnp.mean(values, axis=-1, keepdims=True)
        centred = values - mean
        scale = lax.rsqrt(jnp.mean(centred * centred, axis=-1, keepdims=True) + eps_norm)
        return centred * scale, scale

    def norm_step(i, _):
        at = pl.ds(pl.multiple_of(i * some, some), some)
        unit, _ = normal(at)
        right_ref[1, at, :] = (unit * gains_ref[1:2, :]).astype(jnp.bfloat16)
        right_ref[2, at, :] = (cot_ref[at, :].astype(jnp.float32) * live(i)).astype(jnp.bfloat16)
        return 0

    lax.fori_loop(0, rows_all // some, norm_step, 0)
    result[...] = x1[...]
    dnorm[...] = jnp.zeros_like(dnorm)
    for j in range(tiles):
        for copy in copies(j):
            copy.wait()
        norm, grad = right_ref[1], right_ref[2]
        one = transposed(norm, w_one[j])
        two = transposed(norm, w_two[j])
        back = transposed(grad, w_down[j])
        share = 0.5 * (1.0 + lax.erf(one * (0.5**0.5)))
        gelu = one * share
        slope = share + one * (jnp.exp(-0.5 * one * one) * (0.5 / math.pi) ** 0.5)
        low = (gelu * two).astype(jnp.bfloat16)
        d_one = (back * two * slope).astype(jnp.bfloat16)
        d_two = (back * gelu).astype(jnp.bfloat16)
        for k, part in enumerate((d_one, d_two, low)):
            left_ref[:, pl.ds(width + k * wide + j * tile, tile)] = part
        result[...] += jnp.dot(low, w_down[j], preferred_element_type=jnp.float32)
        dnorm[...] += jnp.dot(d_one, w_one[j], preferred_element_type=jnp.float32) + jnp.dot(
            d_two, w_two[j], preferred_element_type=jnp.float32
        )
    end = width + 3 * wide
    if left_ref.shape[1] > end:
        left_ref[:, end:] = jnp.zeros((rows_all, left_ref.shape[1] - end), left_ref.dtype)
    out_ref[...] = result[...].astype(out_ref.dtype)
    gain_ref[...] = jnp.zeros_like(gain_ref)

    def back_step(i, _):
        at = pl.ds(pl.multiple_of(i * some, some), some)
        unit, scale = normal(at)
        given = dnorm[at, :]
        inner = given * gains_ref[1:2, :]
        inner_mean = jnp.mean(inner, axis=-1, keepdims=True)
        along = jnp.mean(inner * unit, axis=-1, keepdims=True)
        grad = cot_ref[at, :].astype(jnp.float32) * live(i)
        grad = grad + scale * (inner - inner_mean - unit * along)
        back_ref[at, :] = grad
        left_ref[at, 0:width] = grad.astype(jnp.bfloat16)
        gain_ref[1:2, :] += jnp.sum(given * unit, axis=0, keepdims=True)
        return 0

    lax.fori_loop(0, rows_all // some, back_step, 0)

    def go_step(t, _):
        at = pl.ds(pl.multiple_of(t * cols, cols), cols)
        go_ref[:, at] = jnp.dot(
            left_ref[:, 0:width], w_out[:, at], preferred_element_type=jnp.float32
        ).astype(jnp.bfloat16)
        return 0

    lax.fori_loop(0, width // cols, go_step, 0)


def middle_call(mixed, tokens, cotangent, gains, lengths, stack_b, left_cols, block_len):
    rows_all, width = tokens.shape
    low = jnp.bfloat16
    tile = 896 if FF_WIDE % 896 == 0 else 128
    tiles = FF_WIDE // tile
    vmem = pl.BlockSpec(memory_space=pltpu.VMEM)
    return pl.pallas_call(
        functools.partial(middle_kernel, tile, block_len),
        out_shape=(
            jax.ShapeDtypeStruct((rows_all, width), low),
            jax.ShapeDtypeStruct((rows_all, left_cols), low),
            jax.ShapeDtypeStruct((3, rows_all, width), low),
            jax.ShapeDtypeStruct((rows_all, width), low),
            jax.ShapeDtypeStruct((rows_all, width), jnp.float32),
            jax.ShapeDtypeStruct((8, width), jnp.float32),
        ),
        in_specs=[vmem] * 4 + [pl.BlockSpec(memory_space=pltpu.SMEM), pl.BlockSpec(memory_space=pl.ANY)],
        out_specs=(vmem,) * 6,
        scratch_shapes=[pltpu.VMEM((width, width), low)]
        + [pltpu.VMEM((tiles, tile, width), low)] * 3
        + [pltpu.VMEM((rows_all, width), jnp.float32)] * 3
        + [DMA((1 + 3 * tiles,))],
        compiler_params=pltpu.CompilerParams(vmem_limit_bytes=VMEM_BYTES),
        name="middle",
    )(mixed, tokens, cotangent, gains, lengths, stack_b)


def adam_kernel(per, unit_ref, a_ref, b_ref, *refs):
    grads = (refs[:per], refs[per : 2 * per])
    gain_grad, *gains = refs[2 * per : 2 * per + 4]
    master, first, second, new_master, new_first, new_second, *new_gains = refs[2 * per + 4 :]

    @pl.when(pl.program_id(0) == 0)
    def _():
        rows = gains[0].shape[0]
        updated = adam_update(
            gains[0][...], gain_grad[0:rows, :], gains[1][...], gains[2][...], rate_gain, 0.0
        )
        for ref, value in zip(new_gains, updated):
            ref[...] = value

    for j in range(per):
        slot = pl.program_id(0) * per + j
        unit = unit_ref[slot]
        grad = jnp.where(unit == 0, grads[0][j][0], grads[1][j][0]).astype(jnp.float32)
        grad = jnp.where(unit >= 0, grad, 0.0)
        weight, one, two = adam_update(
            master[j], grad, first[j], second[j], rate_matrix, decay_matrix
        )
        new_master[j] = weight
        new_first[j] = one
        new_second[j] = two


def adam_call(kind, at_a, at_b, grads_a, grads_b, gain_grad, gains, master, first, second):
    capacity, rows, width = master.shape
    per = max(p for p in range(1, 8) if capacity % p == 0)

    def unit_spec(j, chunk):
        return pl.BlockSpec(
            (1, rows, width), lambda i, kind, *at: (at[chunk][i * per + j], 0, 0)
        )

    def whole(array):
        return pl.BlockSpec(array.shape, lambda i, kind, *at: (0, 0))

    slot_spec = pl.BlockSpec((per, rows, width), lambda i, kind, *at: (i, 0, 0))
    return pl.pallas_call(
        functools.partial(adam_kernel, per),
        grid_spec=pltpu.PrefetchScalarGridSpec(
            num_scalar_prefetch=3,
            grid=(capacity // per,),
            in_specs=[unit_spec(j, c) for c in range(2) for j in range(per)]
            + [whole(a) for a in (gain_grad, *gains)]
            + [slot_spec] * 3,
            out_specs=[slot_spec] * 3 + [whole(a) for a in gains],
        ),
        out_shape=[jax.ShapeDtypeStruct(a.shape, jnp.float32) for a in (master, first, second, *gains)],
        compiler_params=pltpu.CompilerParams(vmem_limit_bytes=VMEM_BYTES),
        name="adamw",
    )(kind, at_a, at_b, *([grads_a] * per), *([grads_b] * per), gain_grad, *gains, master, first, second)


def pick_kernel(part_ref, master_ref, out_ref, got, sems):
    count, rows = got.shape[:2]

    def at(p):
        return pl.ds(pl.multiple_of(p * rows, rows), rows)

    def copy(p):
        return pltpu.make_async_copy(master_ref.at[part_ref[p]], got.at[p], sems.at[p])

    def start(p, _):
        @pl.when(part_ref[p] >= 0)
        def _():
            copy(p).start()

        return 0

    def end(p, _):
        @pl.when(part_ref[p] >= 0)
        def _():
            copy(p).wait()
            out_ref[at(p), :] = got[p].astype(out_ref.dtype)

        @pl.when(part_ref[p] < 0)
        def _():
            out_ref[at(p), :] = jnp.zeros((rows, out_ref.shape[1]), out_ref.dtype)

        return 0

    lax.fori_loop(0, count, start, 0)
    lax.fori_loop(0, count, end, 0)


def pick_call(part, parts):
    shape = (part.shape[0],) + parts.shape[1:]
    flat = (shape[0] * shape[1], shape[2])
    return pl.pallas_call(
        pick_kernel,
        grid_spec=pltpu.PrefetchScalarGridSpec(
            num_scalar_prefetch=1,
            grid=(1,),
            in_specs=[pl.BlockSpec(memory_space=pl.ANY)],
            out_specs=pl.BlockSpec(flat, lambda i, part: (0, 0)),
            scratch_shapes=[pltpu.VMEM(shape, parts.dtype), DMA((part.shape[0],))],
        ),
        out_shape=jax.ShapeDtypeStruct(flat, jnp.bfloat16),
        compiler_params=pltpu.CompilerParams(vmem_limit_bytes=VMEM_BYTES),
        name="pick",
    )(part, parts)


def place():
    ctx, shard = lax.axis_index("ctx"), lax.axis_index("shard")
    return ctx // 2, ctx % 2, shard // 2, shard % 2


def device_at(z, y, x, core):
    return (z * 2 + y, x * 2 + core)


def piece_at(zb, c, h, a, b):
    return (((zb * 2 + c) * 2 + h) * 2 + a) * 2 + b


def remote(src, dst, send, recv, device):
    return pltpu.make_async_remote_copy(
        src_ref=src, dst_ref=dst, send_sem=send, recv_sem=recv, device_id=device, device_id_type=MESH
    )


def greet(devices):
    barrier = pltpu.get_barrier_semaphore()
    for device in devices:
        pl.semaphore_signal(barrier, inc=1, device_id=device, device_id_type=MESH)
    pl.semaphore_wait(barrier, len(devices))


def line_neighbours():
    z, y, x, core = place()
    return [device_at(z, y, 1 - x, core), device_at(z, 1 - y, x, core), device_at(z, y, x, 1 - core)] + [
        device_at((z + d) % 4, y, x, core) for d in (1, 2, 3)
    ]


def rows_at(ref, piece, count, rows):
    return ref.at[pl.ds(pl.multiple_of(piece * rows, 16), count * rows)]


GATHER_SEMS = [DMA((2,))] + [DMA((2, 4, 2))] * 2 + [DMA((2, 4))] * 2 + [DMA((2, 4, 2))] * 2 + [DMA((4,))] * 2


class Gather:
    def __init__(self, own, buf, rows, sems):
        self.own, self.buf, self.rows = own, buf, rows
        self.lsem, self.zs, self.zr, self.fs, self.fr, self.ts, self.tr, self.ss, self.sr = sems
        self.z, self.y, self.x, self.core = z, y, x, core = place()
        self.xn = device_at(z, y, 1 - x, core)
        self.yn = device_at(z, 1 - y, x, core)
        self.sib = device_at(z, y, x, 1 - core)

    def side(self, h):
        return (self.y, self.x) if h == 0 else (self.x, self.y)

    def near(self, h):
        return (self.xn, self.yn) if h == 0 else (self.yn, self.xn)

    def piece(self, zb, h, a, b):
        return rows_at(self.buf, piece_at(zb, self.core, h, a, b), 1, self.rows)

    def keep(self, h):
        return pltpu.make_async_copy(self.own(h), self.piece(self.z, h, *self.side(h)), self.lsem.at[h])

    def up(self, d, h, step, src=None):
        ref = self.piece(self.z + d, h, *self.side(h))
        k, hop = (0, -d) if step > 0 else (1, d)
        return remote(
            ref if src is None else src,
            ref,
            self.zs.at[k, hop, h],
            self.zr.at[k, hop, h],
            device_at(self.z + step, self.y, self.x, self.core),
        )

    def got(self, d, h):
        ref = self.piece(self.z + d, h, *self.side(h))
        k, hop = (0 if d < 0 else 1), abs(d) - 1
        remote(ref, ref, self.zs.at[k, hop, h], self.zr.at[k, hop, h], self.xn).wait_recv()

    def first(self, zb, h, mine, src=None):
        a, b = self.side(h)
        ref = self.piece(zb, h, a, b if mine else 1 - b)
        return remote(
            ref if src is None else src, ref, self.fs.at[h, zb], self.fr.at[h, zb], self.near(h)[0]
        )

    def second(self, zb, h, j, mine, src=None):
        a, b = self.side(h)
        ref = self.piece(zb, h, a if mine else 1 - a, b if j == 0 else 1 - b)
        return remote(
            ref if src is None else src, ref, self.ts.at[h, zb, j], self.tr.at[h, zb, j], self.near(h)[1]
        )

    def whole(self, zb, c):
        ref = rows_at(self.buf, (zb * 2 + c) * 8, 8, self.rows)
        return remote(ref, ref, self.ss.at[zb], self.sr.at[zb], self.sib)

    def start(self):
        for h in range(2):
            self.keep(h).start()
        for h in range(2):

            @pl.when(self.z < 3)
            def _():
                self.up(0, h, 1, self.own(h)).start()

            @pl.when(self.z > 0)
            def _():
                self.up(0, h, -1, self.own(h)).start()

            self.first(self.z, h, True, self.own(h)).start()
        for h in range(2):
            self.second(self.z, h, 0, True, self.own(h)).start()
        for h in range(2):
            self.keep(h).wait()

    def there(self, d, work):
        if d == 0:
            work()
        else:
            pl.when((self.z + d >= 0) & (self.z + d < 4))(work)

    def line(self, d):
        def work():
            zb = self.z + d
            for h in range(2):
                self.got(d, h)
                if d < 0:

                    @pl.when(self.z < 3)
                    def _():
                        self.up(d, h, 1).start()
                else:

                    @pl.when(self.z > 0)
                    def _():
                        self.up(d, h, -1).start()

                self.first(zb, h, True).start()
            for h in range(2):
                self.second(zb, h, 0, True).start()

        self.there(d, work)

    def cross(self, d):
        def work():
            zb = self.z + d
            for h in range(2):
                self.first(zb, h, False).wait_recv()
                self.second(zb, h, 1, True).start()

        self.there(d, work)

    def close(self, d):
        def work():
            zb = self.z + d
            for h in range(2):
                for j in range(2):
                    self.second(zb, h, j, False).wait_recv()
            self.whole(zb, self.core).start()

        self.there(d, work)

    def finish(self, take=True):
        for h in range(2):
            for d in range(4):

                @pl.when((self.z - d >= 0) & (self.z < 3))
                def _():
                    self.up(-d, h, 1).wait_send()

                @pl.when((self.z + d < 4) & (self.z > 0))
                def _():
                    self.up(d, h, -1).wait_send()

        for zb in range(4):
            for h in range(2):
                self.first(zb, h, True).wait_send()
                for j in range(2):
                    self.second(zb, h, j, True).wait_send()
            self.whole(zb, self.core).wait_send()
            if take:
                self.whole(zb, 1 - self.core).wait_recv()


REDUCE_REFS = 10


def reduce_scratch(rows, width):
    def buf(n):
        return pltpu.VMEM((n * rows, width), jnp.bfloat16)

    return (
        [buf(32), buf(16), buf(8), buf(10)]
        + [DMA((4, 2, 2))] * 2
        + [DMA((4, 2))] * 3
        + [DMA((5, 2))]
    )


class Reduce:
    def __init__(self, rows, refs):
        self.acc, self.got1, self.got2, self.got3 = refs[:4]
        self.s1, self.r1, self.s2, self.r2, self.s3, self.r3 = refs[4:]
        self.rows = rows
        self.z, self.y, self.x, self.core = z, y, x, core = place()
        self.xn = device_at(z, y, 1 - x, core)
        self.yn = device_at(z, 1 - y, x, core)
        self.sib = device_at(z, y, x, 1 - core)

    def zb(self, t):
        s = self.z // 2
        return (3 - 3 * s, 2 - s, 1 - self.z + 4 * s, self.z)[t]

    def base(self, zb):
        return zb * 8

    def side(self, h):
        return (self.y, self.x) if h == 0 else (self.x, self.y)

    def near(self, h):
        return (self.yn, self.xn) if h == 0 else (self.xn, self.yn)

    def send1(self, t, h, q):
        zb = self.zb(t)
        a, b = self.side(h)
        b = 1 - b if q == 0 else b
        return remote(
            rows_at(self.acc, self.base(zb) + h * 4 + (1 - a) * 2 + b, 1, self.rows),
            rows_at(self.got1, zb * 4 + h * 2 + b, 1, self.rows),
            self.s1.at[zb, h, q],
            self.r1.at[zb, h, q],
            self.near(h)[0],
        )

    def send2(self, t, h):
        zb = self.zb(t)
        a, b = self.side(h)
        return remote(
            rows_at(self.acc, self.base(zb) + h * 4 + a * 2 + 1 - b, 1, self.rows),
            rows_at(self.got2, zb * 2 + h, 1, self.rows),
            self.s2.at[zb, h],
            self.r2.at[zb, h],
            self.near(h)[1],
        )

    def send3(self, t, h, up):
        zb = self.zb(t)
        a, b = self.side(h)
        slot = zb if up else zb + (4 - zb) * (1 - (self.z - 1 - zb + 2) // 3)
        return remote(
            rows_at(self.acc, self.base(zb) + h * 4 + a * 2 + b, 1, self.rows),
            rows_at(self.got3, slot * 2 + h, 1, self.rows),
            self.s3.at[t, h],
            self.r3.at[slot, h],
            device_at(self.z + (1 if up else -1), self.y, self.x, self.core),
        )

    def come3(self, slot, h):
        ref = rows_at(self.got3, slot * 2 + h, 1, self.rows)
        remote(ref, ref, self.s3.at[0, h], self.r3.at[slot, h], self.xn).wait_recv()
        a, b = self.side(h)
        zb = self.z if isinstance(slot, int) else slot
        self.add(self.base(zb) + h * 4 + a * 2 + b, self.got3, slot * 2 + h, 1)

    def add(self, at, ref, start, count):
        def body(i, _):
            to = pl.ds(pl.multiple_of((at + i) * self.rows, 16), self.rows)
            given = pl.ds(pl.multiple_of((start + i) * self.rows, 16), self.rows)
            self.acc[to, :] = self.acc[to, :] + ref[given, :]
            return 0

        lax.fori_loop(0, count, body, 0)

    def go1(self, t, q):
        for h in range(2):
            self.send1(t, h, q).start()

    def one(self, t, q):
        zb = self.zb(t)
        for h in range(2):
            a, b = self.side(h)
            b = 1 - b if q == 0 else b
            self.send1(t, h, q).wait_recv()
            self.add(self.base(zb) + h * 4 + a * 2 + b, self.got1, zb * 4 + h * 2 + b, 1)
            if q == 0:
                self.send2(t, h).start()

    def two(self, t):
        zb = self.zb(t)
        for h in range(2):
            a, b = self.side(h)
            self.send2(t, h).wait_recv()
            self.add(self.base(zb) + h * 4 + a * 2 + b, self.got2, zb * 2 + h, 1)

    def tri(self, t, first):
        zb = self.zb(t)
        z = self.z
        inner = ((zb > z) & (z > 0)) | ((zb < z) & (z < 3))
        for h in range(2):
            if not first:

                @pl.when(inner)
                def _():
                    self.come3(zb, h)

            now = jnp.logical_not(inner) if first else inner

            @pl.when((zb > z) & now)
            def _():
                self.send3(t, h, True).start()

            @pl.when((zb < z) & now)
            def _():
                self.send3(t, h, False).start()

    def three(self):
        for h in range(2):

            @pl.when(self.z > 0)
            def _():
                self.come3(self.z, h)

            @pl.when(self.z < 3)
            def _():
                self.come3(4, h)

    def own(self, h):
        a, b = self.side(h)
        return rows_at(self.acc, self.base(self.z) + h * 4 + a * 2 + b, 1, self.rows)

    def finish(self):
        for t in range(4):
            for h in range(2):
                for q in range(2):
                    self.send1(t, h, q).wait_send()
                self.send2(t, h).wait_send()
                if t < 3:
                    ref = rows_at(self.got3, h, 1, self.rows)
                    remote(ref, ref, self.s3.at[t, h], self.r3.at[0, h], self.xn).wait_send()


LATE_GATHER_SEMS = [DMA] + [DMA((3, 4))] * 2 + [DMA((3,))] * 2 + [DMA((4,))] * 2


class LateGather:
    def __init__(self, own, buf, rows, sems):
        self.own, self.buf, self.rows = own, buf, rows
        self.lsem, self.zs, self.zr, self.fs, self.fr, self.ss, self.sr = sems
        self.meet()

    def meet(self):
        self.z, self.y, self.x, self.core = z, y, x, core = place()
        self.xn = device_at(z, y, 1 - x, core)
        self.yn = device_at(z, 1 - y, x, core)
        self.sib = device_at(z, y, x, 1 - core)

    def one_of(self, y, x):
        return rows_at(self.buf, ((self.z * 2 + self.core) * 2 + y) * 2 + x, 1, self.rows)

    def block(self, zb, c):
        return rows_at(self.buf, (zb * 2 + c) * 4, 4, self.rows)

    def hand(self, i, mine):
        y, x = self.y, self.x
        at = ((y, x) if mine else (1 - y, x), (y, x) if mine else (y, 1 - x), (1 - y, x if mine else 1 - x))[i]
        ref = self.one_of(*at)
        src = self.own() if mine and i < 2 else ref
        return remote(src, ref, self.fs.at[i], self.fr.at[i], self.yn if i == 0 else self.xn)

    def keep(self):
        return pltpu.make_async_copy(self.own(), self.one_of(self.y, self.x), self.lsem)

    def start(self):
        self.keep().start()
        self.hand(0, True).start()
        self.hand(1, True).start()
        self.keep().wait()

    def pass_on(self):
        self.hand(0, False).wait_recv()
        self.hand(2, True).start()

    def far_copy(self, d, i, zb):
        ref = rows_at(self.buf, (zb * 2 + self.core) * 4 + i, 1, self.rows)
        to = device_at((self.z + d) % 4, self.y, self.x, self.core)
        return remote(ref, ref, self.zs.at[d - 1, i], self.zr.at[d - 1, i], to)

    def far(self, d, i):
        self.far_copy(d, i, self.z).start()

    def whole(self, zb, c):
        ref = self.block(zb, c)
        return remote(ref, ref, self.ss.at[zb], self.sr.at[zb], self.sib)

    def ready(self):
        self.hand(1, False).wait_recv()
        self.hand(2, False).wait_recv()
        self.whole(self.z, self.core).start()

    def come(self, d):
        zb = (self.z - d) % 4
        for i in range(4):
            self.far_copy(d, i, zb).wait_recv()
        self.whole(zb, self.core).start()

    def finish(self):
        for i in range(3):
            self.hand(i, True).wait_send()
            for k in range(4):
                self.far_copy(i + 1, k, self.z).wait_send()
        for zb in range(4):
            self.whole(zb, self.core).wait_send()
            self.whole(zb, 1 - self.core).wait_recv()


LATE_REDUCE_REFS = 8
ROWS_C = 32


def late_reduce_scratch(rows, width):
    def buf(n):
        return pltpu.VMEM((n * rows, width), jnp.bfloat16)

    return [buf(16), buf(2), buf(1), buf(12), DMA((3,)), DMA((3,)), DMA((3, 4)), DMA((3, 4))]


class LateReduce:
    def __init__(self, rows, refs):
        self.acc, self.got1, self.got2, self.got3 = refs[:4]
        self.s1, self.r1, self.s3, self.r3 = refs[4:]
        self.rows = rows
        self.meet()

    def meet(self):
        self.z, self.y, self.x, self.core = z, y, x, core = place()
        self.xn = device_at(z, y, 1 - x, core)
        self.yn = device_at(z, 1 - y, x, core)
        self.sib = device_at(z, y, x, 1 - core)
    def add(self, to, given):
        rows = self.rows

        def body(i, _):
            at = pl.ds(pl.multiple_of(i * rows, 16), rows)
            to[at, :] = to[at, :] + given[at, :]
            return 0

        lax.fori_loop(0, to.shape[0] // rows, body, 0)

    def part(self, zb, at, count=1):
        return rows_at(self.acc, zb * 4 + at, count, self.rows)

    def far_copy(self, d, i):
        zb = (self.z + d) % 4
        return remote(
            self.part(zb, i),
            rows_at(self.got3, (d - 1) * 4 + i, 1, self.rows),
            self.s3.at[d - 1, i],
            self.r3.at[d - 1, i],
            device_at(zb, self.y, self.x, self.core),
        )

    def far(self, d, i):
        self.far_copy(d, i).start()

    def to_x(self, yb):
        src = self.part(self.z, yb * 2 + 1 - self.x)
        return remote(src, rows_at(self.got1, yb, 1, self.rows), self.s1.at[yb], self.r1.at[yb], self.xn)

    def to_y(self):
        src = self.part(self.z, (1 - self.y) * 2 + self.x)
        return remote(src, self.got2, self.s1.at[2], self.r1.at[2], self.yn)

    def three(self):
        for d in (1, 2, 3):
            for i in range(4):
                self.far_copy(d, i).wait_recv()
            self.add(self.part(self.z, 0, 4), rows_at(self.got3, (d - 1) * 4, 4, self.rows))
        for yb in range(2):
            self.to_x(yb).start()

    def one(self):
        for yb in range(2):
            self.to_x(yb).wait_recv()
            self.add(self.part(self.z, yb * 2 + self.x), rows_at(self.got1, yb, 1, self.rows))
        self.to_y().start()

    def two(self):
        self.to_y().wait_recv()
        self.add(self.own(), self.got2)

    def own(self):
        return self.part(self.z, self.y * 2 + self.x)

    def finish(self):
        for yb in range(2):
            self.to_x(yb).wait_send()
        self.to_y().wait_send()
        for d in (1, 2, 3):
            for i in range(4):
                self.far_copy(d, i).wait_send()


def front_kernel(
    given_ref, tokens_ref, gains_ref, cos_ref, sin_ref, lengths_ref,
    oa_ref, ob_ref, heads, wide_ref, lse_ref, mixed_ref, norm_ref,
    stack, rows, seen, low, mixed, got_a, got_b, new_a, new_b, own_a, own_b, got_c, new_c, own_c, send, recv, csem, ql, qsend, qrecv, ml, msend, mrecv, *sems
):
    n = 8
    z, y, x, core = place()
    ctx, shard = lax.axis_index("ctx"), lax.axis_index("shard")
    m = len(GATHER_SEMS)
    rows_a, rows_b = own_a.shape[0] // 2, own_b.shape[0] // 2
    ga = Gather(lambda h: rows_at(own_a, h, 1, rows_a), stack, rows_a, sems[:m])
    rows_c = own_c.shape[0]
    start_c = 64 * rows_b
    gb = Gather(lambda h: rows_at(own_b, h, 1, rows_b), ob_ref.at[pl.ds(0, start_c)], rows_b, sems[m : 2 * m])
    gc = LateGather(lambda: own_c, ob_ref.at[pl.ds(start_c, 32 * rows_c)], rows_c, sems[2 * m :])
    _, slots, block_len, width = rows.shape
    seq, my_width = seen.shape[2:]
    greet([ga.xn, ga.sib] + [(lax.rem(ctx + d, n), shard) for d in range(1, n)])
    jobs = (
        (0, got_a, new_a, own_a),
        (8 * rows_a, got_b, new_b, own_b),
        (8 * (rows_a + rows_b), got_c, new_c, own_c),
    )

    def share(i, c, xb):
        start, got, new, own = jobs[i]
        size = own.shape[0]
        at = start + c * 2 * size
        if xb is None:
            return given_ref.at[pl.ds(pl.multiple_of(at, 16), 2 * size)]
        return given_ref[pl.ds(pl.multiple_of(at + xb * size, 16), size), :]

    def held(i, xb):
        size = jobs[i][3].shape[0]
        return pl.ds(pl.multiple_of(xb * size, 16), size)

    def to_core(i):
        return remote(share(i, 1 - core, None), jobs[i][1], send.at[i], recv.at[i], ga.sib)

    def to_x(i):
        start, got, new, own = jobs[i]
        return remote(got.at[held(i, 1 - x)], new, send.at[3 + i], recv.at[3 + i], ga.xn)

    def spread(i):
        start, got, new, own = jobs[i]
        to_core(i).wait_recv()
        got[held(i, 1 - x), :] = got[held(i, 1 - x), :] + share(i, core, 1 - x)
        to_x(i).start()
        own[...] = got[held(i, x), :] + share(i, core, x)

    def cross(i):
        start, got, new, own = jobs[i]
        to_x(i).wait_recv()
        own[...] = own[...] + new[...]

    def peer(d):
        return lax.rem(ctx + d, n)

    def lanes(owner):
        return pl.ds(pl.multiple_of(owner * my_width, my_width), my_width)

    def block(owner):
        return pl.ds(pl.multiple_of(owner * block_len, block_len), block_len)

    def head_copy(j, owner):
        return remote(
            rows.at[j, :, :, lanes(owner)], seen.at[j, :, block(ctx), :], qsend.at[j, owner], qrecv.at[j, ctx], (owner, shard)
        )

    def head_own(j):
        return pltpu.make_async_copy(rows.at[j, :, :, lanes(ctx)], seen.at[j, :, block(ctx), :], ql.at[j])

    def mixed_copy(s, d):
        return remote(
            low.at[s, block(peer(d)), :], mixed.at[s, :, lanes(ctx)], msend.at[s, d], mrecv.at[s, d], (peer(d), shard)
        )

    def mixed_own(s):
        return pltpu.make_async_copy(low.at[s, block(ctx), :], mixed.at[s, :, lanes(ctx)], ml.at[s])

    cols = 256
    tiles = width // cols
    per_z = 16 * rows_a // cols

    def region(i):
        s = z // 2
        t = z % 2
        return (
            z,
            (1 - t) * (1 - s) + s * (1 + t),
            2 * (1 - s) + s * (3 - 2 * t),
            3 * (1 - s),
        )[i]

    def norm():
        def step(i, _):
            at = pl.ds(pl.multiple_of(i * 64, 64), 64)
            values = layer_norm(tokens_ref[at, :].astype(jnp.float32), gains_ref[0:1, :])
            norm_ref[at, :] = values.astype(jnp.bfloat16)
            return 0

        lax.fori_loop(0, slots * block_len // 64, step, 0)

    def table(ref):
        one = ref[block(ctx), :]
        one = jnp.concatenate([one] * (cols // my_width), axis=1)
        return jnp.concatenate([one] * slots, axis=0)

    def qkv(i):
        zb = region(i)
        ga.whole(zb, 1 - core).wait_recv()

        def tile_step(k, _):
            tile = zb * per_z + k
            j, t = tile // tiles, tile % tiles
            at = pl.ds(pl.multiple_of(t * cols, cols), cols)
            weight = stack[pl.ds(pl.multiple_of(tile * cols, cols), cols), :]
            values = transposed(norm_ref[...], weight)
            turn = (j < 2).astype(jnp.float32)
            cos = table(cos_ref) * turn + (1.0 - turn)
            values = values * cos + half_turned(values) * (table(sin_ref) * turn)
            rows[j, :, :, at] = values.astype(jnp.bfloat16).reshape(slots, block_len, cols)
            for q in range(cols // my_width):
                owner = t * (cols // my_width) + q

                @pl.when(owner == ctx)
                def _():
                    head_own(j).start()

                @pl.when(owner != ctx)
                def _():
                    head_copy(j, owner).start()

            return 0

        lax.fori_loop(0, per_z, tile_step, 0)

    def heads_wait(j):
        head_own(j).wait()
        for d in range(1, n):
            ref = seen.at[j, :, block(peer(d)), :]
            remote(ref, ref, qsend.at[j, peer(d)], qrecv.at[j, peer(d)], (peer(d), shard)).wait_recv()

    def mixed_wait():
        for s in range(slots):
            mixed_own(s).wait()
            for d in range(1, n):
                mixed_copy(s, d).wait_recv()

    for i in range(3):
        to_core(i).start()
    spread(0)
    spread(1)
    spread(2)
    cross(0)
    ga.start()
    norm()
    ga.line(-1), ga.line(1)
    ga.cross(0)
    cross(2)
    gc.start()
    ga.line(-2), ga.line(2)
    cross(1)
    gb.start()
    ga.cross(-1), ga.cross(1)
    gc.pass_on()
    ga.close(0)
    ga.line(-3), ga.line(3)
    ga.cross(-2), ga.cross(2)
    qkv(0)
    gb.line(-1), gb.line(1)
    ga.close(-1), ga.close(1)
    ga.cross(-3), ga.cross(3)
    qkv(1)
    gc.ready()
    gc.far(2, 0)
    gc.far(1, 0)
    gb.cross(0)
    gc.far(3, 0)
    gc.far(2, 1)
    ga.close(-2), ga.close(2)
    qkv(2)
    ga.close(-3), ga.close(3)
    gb.line(-2), gb.line(2)
    gc.far(1, 1)
    gc.far(3, 1)
    qkv(3)
    gb.cross(-1), gb.cross(1)
    gc.far(2, 2)
    gc.far(1, 2)
    gb.close(0)
    gc.far(3, 2)
    gc.far(2, 3)
    heads_wait(0)
    gb.line(-3), gb.line(3)
    gc.far(1, 3)
    gc.far(3, 3)
    gb.cross(-2), gb.cross(2)
    gb.close(-1), gb.close(1)
    heads_wait(1)
    heads_wait(2)
    keep_a = pltpu.make_async_copy(stack, oa_ref, csem.at[0])
    keep_heads = pltpu.make_async_copy(seen, heads, csem.at[1])
    keep_a.start()
    keep_heads.start()
    chunk = 256
    per_slot = seq // chunk

    def attend_at(i, _):
        s, c = i // per_slot, i % per_slot
        bias = key_bias(lengths_ref[s], seq)
        attend_step(
            c, seen.at[0, s], seen.at[1, s], seen.at[2, s], bias, low.at[s], wide_ref.at[s], lse_ref.at[s], chunk
        )

        @pl.when(c == per_slot - 1)
        def _():
            mixed_own(s).start()
            for d in range(1, n):
                mixed_copy(s, d).start()

        @pl.when(i == 0)
        def _():
            gb.cross(-3), gb.cross(3)
            gc.come(1)

        @pl.when(i == 4)
        def _():
            gb.close(-2), gb.close(2)
            gc.come(3)

        return 0

    lax.fori_loop(0, slots * per_slot, attend_at, 0)
    gb.close(-3), gb.close(3)
    gc.come(2)
    mixed_wait()
    mixed_ref[...] = mixed[...]
    keep_a.wait()
    keep_heads.wait()
    for i in range(3):
        to_core(i).wait_send()
        to_x(i).wait_send()
    for d in range(1, n):
        for j in range(3):
            head_copy(j, peer(d)).wait_send()
        for s in range(slots):
            mixed_copy(s, d).wait_send()
    ga.finish(False)
    gb.finish()
    gc.finish()


def front_call(given, rows_a, rows_b, rows_c, tokens, gains, cosine, sine, lengths, slots, block_len, collective_id):
    vmem = pl.BlockSpec(memory_space=pltpu.VMEM)
    any_ = pl.BlockSpec(memory_space=pl.ANY)
    low = jnp.bfloat16
    width = tokens.shape[1]
    seq = block_len * 8
    my_width = width // 8
    stack_a, stack_b = (
        jax.ShapeDtypeStruct((r, width), low) for r in (64 * rows_a, 64 * rows_b + 32 * rows_c)
    )
    scratch = [
        pltpu.VMEM(stack_a.shape, low),
        pltpu.VMEM((3, slots, block_len, width), low),
        pltpu.VMEM((3, slots, seq, my_width), low),
        pltpu.VMEM((slots, seq, my_width), low),
        pltpu.VMEM((slots, block_len, width), low),
    ]
    for pieces in (4, 2, 2):
        for r in (rows_a, rows_b):
            scratch.append(pltpu.VMEM((pieces * r, width), low))
    scratch += [pltpu.VMEM((pieces * rows_c, width), low) for pieces in (2, 1, 1)]
    return pl.pallas_call(
        front_kernel,
        out_shape=(
            stack_a,
            stack_b,
            jax.ShapeDtypeStruct((3, slots, seq, my_width), low),
            jax.ShapeDtypeStruct((slots, seq, my_width), jnp.float32),
            jax.ShapeDtypeStruct((slots, seq, my_width), jnp.float32),
            jax.ShapeDtypeStruct((slots, block_len, width), low),
            jax.ShapeDtypeStruct((slots * block_len, width), low),
        ),
        in_specs=[vmem] * 5 + [pl.BlockSpec(memory_space=pltpu.SMEM)],
        out_specs=(any_, any_, any_, vmem, vmem, vmem, vmem),
        scratch_shapes=scratch
        + [DMA((6,)), DMA((6,)), DMA((2,)), DMA((3,)), DMA((3, 8)), DMA((3, 8)), DMA((slots,)), DMA((slots, 8)), DMA((slots, 8))]
        + GATHER_SEMS * 2
        + LATE_GATHER_SEMS,
        compiler_params=pltpu.CompilerParams(
            collective_id=collective_id, has_side_effects=True, vmem_limit_bytes=VMEM_BYTES
        ),
        name="spread_and_attend",
    )(given, tokens, gains, cosine, sine, lengths)


GAIN_SEMS = [DMA((6,)), DMA((6,))]


class GainSum:
    def __init__(self, ref, got, line, sems):
        self.ref, self.got, self.all = ref, got, line
        self.send, self.recv = sems
        self.z, self.y, self.x, self.core = place()

    def step(self, i):
        z, y, x, core = self.z, self.y, self.x, self.core
        to = (device_at(z, y, x, 1 - core), device_at(z, y, 1 - x, core), device_at(z, 1 - y, x, core))[i]
        return remote(self.ref, self.got.at[i], self.send.at[i], self.recv.at[i], to)

    def far(self, d):
        to = device_at((self.z + d) % 4, self.y, self.x, self.core)
        return remote(self.ref, self.all.at[self.z], self.send.at[2 + d], self.recv.at[2 + d], to)

    def begin(self, i):
        self.step(i).start()

    def end(self, i):
        self.step(i).wait()
        self.ref[...] = self.ref[...] + self.got[i]

    def begin_far(self):
        for d in (1, 2, 3):
            self.far(d).start()
        self.all[self.z] = self.ref[...]

    def end_far(self, out):
        for d in (1, 2, 3):
            self.far(d).wait()
        total = self.all[0]
        for i in range(1, 4):
            total = total + self.all[i]
        out[...] = total


def back_kernel(
    g_ref, qkv_ref, wide_ref, lse_ref, cos_ref, sin_ref, norm_ref, tokens_ref, gains_ref, middle_ref, gain_ref,
    left_ref, right_ref, w_ref, lengths_ref,
    oa_ref, ob_ref, og_ref, tok_ref,
    left_got, late_got, right_got, norm_got, rows_got, weight_ref, xsend, xrecv, heads, grad, rows, acc_k, acc_v, dnorm, gain, gain_got, gain_all, wsem, gl, gsend, grecv, dl, dsend, drecv, *refs
):
    n = 8
    slots, block_len, width = g_ref.shape
    seq, my_width = qkv_ref.shape[2:]
    chunk = 256
    per_slot = seq // chunk
    m = len(GATHER_SEMS)
    rows_a, rows_b, rows_c = oa_ref.shape[0] // 64, left_got.shape[2] // 8, late_got.shape[2] // 4
    start_c = 64 * rows_b
    ra = Reduce(rows_a, refs[:REDUCE_REFS])
    rb = Reduce(rows_b, refs[REDUCE_REFS : 2 * REDUCE_REFS])
    refs = refs[2 * REDUCE_REFS :]
    rc = LateReduce(rows_c, refs[:LATE_REDUCE_REFS])
    refs = refs[LATE_REDUCE_REFS:]
    ga = Gather(ra.own, oa_ref, rows_a, refs[:m])
    gb = Gather(rb.own, ob_ref.at[pl.ds(0, start_c)], rows_b, refs[m : 2 * m])
    refs = refs[2 * m :]
    gc = LateGather(rc.own, ob_ref.at[pl.ds(start_c, 32 * rows_c)], rows_c, refs[: len(LATE_GATHER_SEMS)])
    gs = GainSum(gain, gain_got, gain_all, refs[len(LATE_GATHER_SEMS) :])
    z, y, x, core = place()
    ctx, shard = lax.axis_index("ctx"), lax.axis_index("shard")
    greet([ra.xn, ra.sib] + [(lax.rem(ctx + d, n), shard) for d in range(1, n)])

    def peer(d):
        return lax.rem(ctx + d, n)

    def lanes(owner):
        return pl.ds(pl.multiple_of(owner * my_width, my_width), my_width)

    def block(owner):
        return pl.ds(pl.multiple_of(owner * block_len, block_len), block_len)

    def go_copy(d):
        return remote(
            g_ref.at[:, :, lanes(peer(d))], grad.at[:, block(ctx), :], gsend.at[d], grecv.at[d], (peer(d), shard)
        )

    def back_copy(s, d):
        return remote(
            heads.at[:, s, block(peer(d)), :], rows.at[:, s, :, lanes(ctx)], dsend.at[s, d], drecv.at[s, d], (peer(d), shard)
        )

    def back_own(s):
        return pltpu.make_async_copy(heads.at[:, s, block(ctx), :], rows.at[:, s, :, lanes(ctx)], dl.at[s])

    go_own = pltpu.make_async_copy(g_ref.at[:, :, lanes(ctx)], grad.at[:, block(ctx), :], gl)
    w_copy = pltpu.make_async_copy(w_ref, weight_ref, wsem)
    cut = 128
    rows_all = slots * block_len

    def to_sib(src, dst, i):
        return remote(src, dst, xsend.at[i], xrecv.at[i], ra.sib)

    region_b, region_c = 8 * rows_b, 4 * rows_c

    def left_copy(t, c):
        lane = pl.ds(pl.multiple_of((rb.zb(t) * 2 + c) * region_b, cut), region_b)
        return to_sib(left_ref.at[:, lane], left_got.at[rb.zb(t)], t)

    def late_copy(zb, c):
        lane = pl.ds(pl.multiple_of(start_c + (zb * 2 + c) * region_c, cut), region_c)
        return to_sib(left_ref.at[:, lane], late_got.at[zb], 6 + slots + zb)

    right_copy = to_sib(right_ref, right_got, 4)
    norm_copy = to_sib(norm_ref, norm_got, 5)
    def rows_copy(s):
        return to_sib(rows.at[:, s], rows_got.at[:, s], 6 + s)

    def given():
        right_copy.start()
        left_copy(0, 1 - core).start()
        for t in range(4):
            late_copy(t, 1 - core).start()
        for t in range(1, 4):
            left_copy(t, 1 - core).start()
        norm_copy.start()
        right_copy.wait_recv()

    def product(zb, start, region, got, acc):
        count = region // cut

        def step(i, _):
            g = start // cut + (zb * 2 + core) * count + i
            kind = (g >= width // cut).astype(jnp.int32) + (g >= (width + 2 * FF_WIDE) // cut).astype(jnp.int32)
            mine = left_ref[:, pl.ds(pl.multiple_of(g * cut, cut), cut)]
            other = got[zb, :, pl.ds(pl.multiple_of(i * cut, cut), cut)]
            total = leading(mine, right_ref[kind]) + leading(other, right_got[kind])
            at = pl.ds(pl.multiple_of((zb * count + i) * cut, cut), cut)
            acc[at, :] = total.astype(jnp.bfloat16)
            return 0

        lax.fori_loop(0, count, step, 0)

    def fill(t):
        left_copy(t, core).wait_recv()
        product(rb.zb(t), 0, region_b, left_got, rb.acc)

    def late():
        for zb in range(4):
            late_copy(zb, core).wait_recv()

        def step(zb, _):
            product(zb, start_c, region_c, late_got, rc.acc)
            return 0

        lax.fori_loop(0, 4, step, 0)

    cols = 256
    tiles = width // cols

    def rows_wait(s):
        back_own(s).wait()
        for d in range(1, n):
            back_copy(s, d).wait_recv()
        rows_copy(s).start()

    def both():
        norm_copy.wait_recv()
        for s in range(slots):
            rows_copy(s).wait_recv()

    def weight(t):
        zb = ra.zb(t)
        count = 8 * rows_a // cut

        def step(i, _):
            g = (zb * 2 + core) * count + i
            j = g * cut // width
            lane = pl.ds(pl.multiple_of(g * cut - j * width, cut), cut)
            total = leading(rows[j, :, :, lane].reshape(rows_all, cut), norm_ref[...])
            total += leading(rows_got[j, :, :, lane].reshape(rows_all, cut), norm_got[...])
            at = pl.ds(pl.multiple_of(zb * 8 * rows_a + i * cut, cut), cut)
            ra.acc[at, :] = total.astype(jnp.bfloat16)
            return 0

        lax.fori_loop(0, count, step, 0)

    def norm_step(t, _):
        at = pl.ds(pl.multiple_of(t * cols, cols), cols)
        total = None
        for j in range(3):
            left = rows[j].reshape(slots * block_len, width)
            right = weight_ref[pl.ds(j * width, width), at]
            part = jnp.dot(left, right, preferred_element_type=jnp.float32)
            total = part if total is None else total + part
        dnorm[:, at] = total
        return 0

    some = 64
    def token_step(i, _):
        at = pl.ds(pl.multiple_of(i * some, some), some)
        values = tokens_ref[at, :].astype(jnp.float32)
        mean = jnp.mean(values, axis=-1, keepdims=True)
        centred = values - mean
        scale = lax.rsqrt(jnp.mean(centred * centred, axis=-1, keepdims=True) + eps_norm)
        unit = centred * scale
        given = dnorm[at, :]
        inner = given * gains_ref[0:1, :]
        inner_mean = jnp.mean(inner, axis=-1, keepdims=True)
        along = jnp.mean(inner * unit, axis=-1, keepdims=True)
        grads = middle_ref[at, :] + scale * (inner - inner_mean - unit * along)
        tok_ref[at, :] = grads.astype(jnp.bfloat16)
        gain[0:1, :] += jnp.sum(given * unit, axis=0, keepdims=True)
        return 0

    def token():
        w_copy.wait()
        lax.fori_loop(0, tiles, norm_step, 0)
        gain[...] = gain_ref[...]
        lax.fori_loop(0, slots * block_len // some, token_step, 0)
        gs.begin(0)

    for d in range(1, n):
        go_copy(d).start()
    go_own.start()
    given()
    fill(0)
    rb.go1(0, 0)
    rb.go1(0, 1)
    fill(1)
    fill(2)
    fill(3)
    late()
    w_copy.start()
    go_own.wait()
    for d in range(1, n):
        go_copy(d).wait_recv()

    def attend_step(i, _):
        s, c = i // per_slot, i % per_slot
        slot = (
            qkv_ref.at[0, s], qkv_ref.at[1, s], qkv_ref.at[2, s], grad.at[s], wide_ref.at[s], lse_ref.at[s],
            key_bias(lengths_ref[s], seq), cos_ref, sin_ref, heads.at[0, s], heads.at[1, s], heads.at[2, s], acc_k, acc_v, chunk,
        )

        @pl.when(c == 0)
        def _():
            acc_k[...] = jnp.zeros_like(acc_k)
            acc_v[...] = jnp.zeros_like(acc_v)

        attend_back_step(c, *slot)

        @pl.when(c == per_slot - 1)
        def _():
            attend_back_end(*slot)
            back_own(s).start()
            for d in range(1, n):
                back_copy(s, d).start()

        @pl.when(i == 1)
        def _():
            rb.one(0, 0)
            rb.go1(1, 0)
            rb.one(0, 1)
            rb.go1(1, 1)

        return 0

    lax.fori_loop(0, slots * per_slot, attend_step, 0)
    rb.two(0)
    rb.one(1, 0)
    rb.go1(2, 0)
    rb.one(1, 1)
    rb.go1(2, 1)
    rc.far(2, 0)
    rc.far(1, 0)
    rb.tri(0, 1)
    rb.tri(0, 0)
    rb.two(1)
    rb.one(2, 0)
    rb.go1(3, 0)
    rb.one(2, 1)
    rb.go1(3, 1)
    rc.far(3, 0)
    rc.far(2, 1)
    rb.tri(1, 1)
    rb.tri(1, 0)
    rb.two(2)
    rb.one(3, 0)
    rb.one(3, 1)
    rc.far(1, 1)
    rc.far(3, 1)
    rb.tri(2, 1)
    rb.tri(2, 0)
    rows_wait(0)
    rows_wait(1)
    both()
    weight(0)
    ra.go1(0, 0)
    ra.go1(0, 1)
    weight(1)
    ra.go1(1, 0)
    ra.go1(1, 1)
    rc.far(2, 2)
    rc.far(1, 2)
    rc.far(3, 2)
    rb.two(3)
    weight(2)
    ra.go1(2, 0)
    ra.go1(2, 1)
    weight(3)
    ra.go1(3, 0)
    ra.go1(3, 1)
    rc.far(2, 3)
    rc.far(1, 3)
    rc.far(3, 3)
    ra.one(0, 0)
    ra.one(0, 1)
    rb.three()
    gb.start()
    token()
    ra.one(1, 0)
    ra.one(1, 1)
    ra.two(0)
    rc.three()
    ra.one(2, 0)
    ra.one(2, 1)
    ra.tri(0, 1)
    ra.tri(0, 0)
    ra.two(1)
    rc.one()
    gb.line(-1), gb.line(1)
    ra.one(3, 0)
    ra.one(3, 1)
    ra.tri(1, 1)
    ra.tri(1, 0)
    ra.two(2)
    gb.cross(0)
    rc.two()
    gc.start()
    gs.end(0)
    gs.begin(1)
    ra.tri(2, 1)
    ra.tri(2, 0)
    ra.two(3)
    gb.line(-2), gb.line(2)
    gc.pass_on()
    ra.three()
    ga.start()
    gc.ready()
    gc.far(2, 0)
    gc.far(1, 0)
    gc.far(3, 0)
    gb.cross(-1), gb.cross(1)
    gs.end(1)
    gs.begin(2)
    gb.close(0)
    gc.far(2, 1)
    gc.far(1, 1)
    gc.far(3, 1)
    gb.line(-3), gb.line(3)
    gc.far(2, 2)
    gc.far(1, 2)
    gc.far(3, 2)
    ga.line(-1), ga.line(1)
    gb.cross(-2), gb.cross(2)
    gc.far(2, 3)
    gc.far(1, 3)
    gc.far(3, 3)
    gs.end(2)
    gs.begin_far()
    ga.cross(0)
    gb.close(-1), gb.close(1)
    ga.line(-2), ga.line(2)
    gb.cross(-3), gb.cross(3)
    gc.come(1)
    ga.cross(-1), ga.cross(1)
    ga.close(0)
    gb.close(-2), gb.close(2)
    gc.come(3)
    ga.line(-3), ga.line(3)
    ga.cross(-2), ga.cross(2)
    ga.close(-1), ga.close(1)
    gb.close(-3), gb.close(3)
    ga.cross(-3), ga.cross(3)
    ga.close(-2), ga.close(2)
    ga.close(-3), ga.close(3)
    gc.come(2)
    gs.end_far(og_ref)
    for d in range(1, n):
        go_copy(d).wait_send()
        for s in range(slots):
            back_copy(s, d).wait_send()
    for t in range(4):
        left_copy(t, 1 - core).wait_send()
        late_copy(t, 1 - core).wait_send()
    for copy in [right_copy, norm_copy] + [rows_copy(s) for s in range(slots)]:
        copy.wait_send()
    ra.finish(), rb.finish(), rc.finish()
    ga.finish(), gb.finish(), gc.finish()


def back_call(
    grad_rows, qkv_heads, wide, lse, cosine, sine, norm_one, tokens, gains, grad_middle, gain_part, left, right, w_qkv, lengths, collective_id
):
    any_ = pl.BlockSpec(memory_space=pl.ANY)
    vmem = pl.BlockSpec(memory_space=pltpu.VMEM)
    low = jnp.bfloat16
    slots, block_len, width = grad_rows.shape
    seq, my_width = qkv_heads.shape[2:]
    rows_all = slots * block_len
    gain = gain_part.shape
    rows_a, rows_c = w_qkv.shape[0] // 64, ROWS_C
    rows_b = left.shape[1] // 64 - rows_c // 2
    return pl.pallas_call(
        back_kernel,
        out_shape=(
            jax.ShapeDtypeStruct(w_qkv.shape, low),
            jax.ShapeDtypeStruct((left.shape[1], width), low),
            jax.ShapeDtypeStruct(gain, jnp.float32),
            jax.ShapeDtypeStruct((rows_all, width), low),
        ),
        in_specs=[vmem] * 13 + [any_, pl.BlockSpec(memory_space=pltpu.SMEM)],
        out_specs=(any_, any_, vmem, vmem),
        scratch_shapes=[
            pltpu.VMEM((4, rows_all, 8 * rows_b), low),
            pltpu.VMEM((4, rows_all, 4 * rows_c), low),
            pltpu.VMEM(right.shape, low),
            pltpu.VMEM((rows_all, width), low),
            pltpu.VMEM((3, slots, block_len, width), low),
            pltpu.VMEM(w_qkv.shape, low),
            DMA((10 + slots,)),
            DMA((10 + slots,)),
            pltpu.VMEM(qkv_heads.shape, low),
            pltpu.VMEM((slots, seq, my_width), low),
            pltpu.VMEM((3, slots, block_len, width), low),
            pltpu.VMEM((seq, my_width), jnp.float32),
            pltpu.VMEM((seq, my_width), jnp.float32),
            pltpu.VMEM((rows_all, width), jnp.float32),
            pltpu.VMEM(gain, jnp.float32),
            pltpu.VMEM((3,) + gain, jnp.float32),
            pltpu.VMEM((4,) + gain, jnp.float32),
            DMA,
            DMA,
            DMA((8,)),
            DMA((8,)),
            DMA((slots,)),
            DMA((slots, 8)),
            DMA((slots, 8)),
        ]
        + reduce_scratch(rows_a, width)
        + reduce_scratch(rows_b, width)
        + late_reduce_scratch(rows_c, width)
        + GATHER_SEMS * 2
        + LATE_GATHER_SEMS
        + GAIN_SEMS,
        compiler_params=pltpu.CompilerParams(
            collective_id=collective_id, has_side_effects=True, vmem_limit_bytes=VMEM_BYTES
        ),
        name="back_and_sum",
    )(
        grad_rows, qkv_heads, wide, lse, cosine, sine, norm_one, tokens, gains, grad_middle, gain_part, left, right, w_qkv, lengths
    )


def to_heads(values):
    return lax.all_to_all(values, "ctx", split_axis=3, concat_axis=2, tiled=True)


def to_rows(values):
    return lax.all_to_all(values, "ctx", split_axis=2, concat_axis=3, tiled=True)


def shards(
    fast,
    tokens,
    cotangent,
    lengths,
    unit_owner,
    master,
    first_moment,
    second_moment,
    norm_gains,
    gain_first,
    gain_second,
):
    slots, block_len, width = tokens.shape
    groups = lax.axis_size("shard")
    n = lax.axis_size("ctx")
    ctx, shard = lax.axis_index("ctx"), lax.axis_index("shard")
    capacity, unit_rows, _ = master.shape
    units = unit_owner.shape[0]
    rows_all = slots * block_len
    seq = block_len * n
    device_count = n * groups
    my_width = width // n

    low = jnp.bfloat16
    rows_a = 3 * width
    rows_b = width + 3 * FF_WIDE
    split = rows_a // unit_rows
    lead, ff_units, wide_units = (r // unit_rows for r in (width, FF, FF_WIDE))

    def unit_of(block, chunk):
        if chunk == 0:
            return jnp.where(block < split, block, -1)
        inner = block - lead
        third = inner // wide_units
        at = inner - third * wide_units
        there = (block < lead) | ((at < ff_units) & (third < 3))
        return jnp.where(there, split + jnp.where(block < lead, block, lead + third * ff_units + at), -1)

    def block_of(unit):
        inner = unit - split - lead
        third = jnp.maximum(inner, 0) // ff_units
        return unit - split + third * (wide_units - ff_units)

    part_rows = 16
    per_unit = unit_rows // part_rows
    parts = master.reshape(capacity * per_unit, part_rows, width)

    def units_at(chunk, per, wanted, start=0):
        at = wanted[..., None] * (per // part_rows) + jnp.arange(per // part_rows, dtype=jnp.int32)
        at = at + start // part_rows
        at = at.reshape(-1)
        return unit_of(at // per_unit, chunk), at % per_unit

    def pick(unit, inner):
        mine, rank = own_places(unit_owner, shard, unit)
        return pick_call(jnp.where(mine, rank * per_unit + inner, -1), parts)

    def piece_rows(count, pieces):
        return -(-count // (pieces * part_rows)) * part_rows

    cos_seq, sin_seq = rope_tables(seq, my_width // HEAD_DIM)
    flat_tokens = tokens.reshape(rows_all, width)

    if fast:
        z, y, x, core = place()
        wanted = jnp.stack(
            [
                jnp.stack([jnp.stack([piece_at(z, c, 0, y, q), piece_at(z, c, 1, q, y)]) for q in range(2)])
                for c in range(2)
            ]
        )
        late = jnp.stack([jnp.stack([((z * 2 + c) * 2 + y) * 2 + q for q in range(2)]) for c in range(2)])
        per_a, per_b = piece_rows(rows_a, 64), piece_rows(rows_b, 64) - ROWS_C // 2
        at_pieces = [
            units_at(0, per_a, wanted),
            units_at(1, per_b, wanted),
            units_at(1, ROWS_C, late, 64 * per_b),
        ]
        given = pick(*(jnp.concatenate(both) for both in zip(*at_pieces)))
        stack_a, stack_b, qkv_heads, wide, lse, mixed_low, norm_one = front_call(
            given, per_a, per_b, ROWS_C, flat_tokens, norm_gains, cos_seq, sin_seq, lengths, slots, block_len, 0
        )
    else:
        wanted = ctx * groups + jnp.arange(groups, dtype=jnp.int32)
        stacks = []
        for chunk, count in enumerate((rows_a, rows_b)):
            share = pick(*units_at(chunk, piece_rows(count, device_count), wanted))
            own = lax.psum_scatter(share, "shard", scatter_dimension=0, tiled=True)
            stacks.append(lax.all_gather(own, BOTH, axis=0, tiled=True))
        stack_a, stack_b = stacks
        inputs = flat_tokens.astype(jnp.float32)
        norm_one = layer_norm(inputs, norm_gains[0]).astype(low)
        cos_rows, sin_rows = (
            jnp.tile(lax.dynamic_slice_in_dim(table, ctx * block_len, block_len, 0), (slots, 256 // my_width))
            for table in (cos_seq, sin_seq)
        )
        qkv = qkv_call(norm_one, stack_a, cos_rows, sin_rows)
        qkv_heads = to_heads(qkv.reshape(3, slots, block_len, width))
        mixed_heads, wide, lse = attend_call(qkv_heads, lengths)
        mixed_low = to_rows(mixed_heads[None])
    mixed_low = mixed_low.reshape(rows_all, width)
    left_cols = 64 * piece_rows(rows_b, 64)
    output, left, right, grad_heads_rows, grad_middle, gain_part = middle_call(
        mixed_low, flat_tokens, cotangent.reshape(rows_all, width), norm_gains, lengths, stack_b, left_cols, block_len
    )
    output = output.reshape(slots, block_len, width)
    grad_heads_rows = grad_heads_rows.reshape(slots, block_len, width)

    if fast:
        all_a, all_b, gain_grad, token_grad = back_call(
            grad_heads_rows, qkv_heads, wide, lse, cos_seq, sin_seq, norm_one, flat_tokens,
            norm_gains, grad_middle, gain_part, left, right, stack_a, lengths, 1,
        )
    else:
        cuts = (0, width, width + 2 * FF_WIDE, rows_b)
        grads_b = jnp.concatenate(
            [leading(left[:, cuts[i] : cuts[i + 1]], right[i]).astype(low) for i in range(3)]
            + [jnp.zeros((stack_b.shape[0] - rows_b, width), low)],
            axis=0,
        )
        grad_heads = to_heads(grad_heads_rows[None])[0]
        grad_qkv_heads = attend_back_call(qkv_heads, grad_heads, wide, lse, lengths, cos_seq, sin_seq)
        grad_qkv_low = to_rows(grad_qkv_heads).reshape(3, rows_all, width)
        grad_norm_one = sum(
            jnp.dot(
                grad_qkv_low[i],
                stack_a[i * width : (i + 1) * width],
                preferred_element_type=jnp.float32,
            )
            for i in range(3)
        )
        _, norm_back_one = jax.vjp(layer_norm, inputs, norm_gains[0])
        grad_input_part, grad_gain_one = norm_back_one(grad_norm_one)
        token_grad = (grad_middle + grad_input_part).astype(low)
        grads_a = jnp.concatenate(
            [leading(grad_qkv_low[i], norm_one).astype(low) for i in range(3)]
            + [jnp.zeros((stack_a.shape[0] - rows_a, width), low)],
            axis=0,
        )
        all_a, all_b = (
            lax.all_gather(
                lax.psum_scatter(g, BOTH, scatter_dimension=0, tiled=True), BOTH, axis=0, tiled=True
            )
            for g in (grads_a, grads_b)
        )
        gain_grad = lax.psum(gain_part.at[0].set(grad_gain_one), BOTH)
    token_grad = token_grad.reshape(slots, block_len, width)
    all_a = all_a.reshape(-1, unit_rows, width)
    all_b = all_b.reshape(-1, unit_rows, width)

    every = jnp.arange(units, dtype=jnp.int32)
    rank = own_places(unit_owner, shard, every)[1]
    here = (unit_owner == shard) & (rank == jnp.arange(capacity, dtype=jnp.int32)[:, None])
    unit_of_slot = jnp.sum(jnp.where(here, every + 1, 0), axis=1) - 1
    kind = jnp.where(unit_of_slot < 0, -1, (unit_of_slot >= split).astype(jnp.int32))
    at_a = jnp.where(kind == 0, unit_of_slot, 0)
    at_b = jnp.where(kind == 1, block_of(unit_of_slot), 0)
    new_master, new_first, new_second, new_gains, new_gain_first, new_gain_second = adam_call(
        kind, at_a, at_b, all_a, all_b, gain_grad, (norm_gains, gain_first, gain_second), master, first_moment, second_moment
    )
    return (
        output,
        token_grad,
        new_master,
        new_first,
        new_second,
        new_gains,
        new_gain_first,
        new_gain_second,
    )


def solution(mesh):
    fast = dict(mesh.shape) == {"ctx": 8, "shard": 4}
    return jax.shard_map(
        functools.partial(shards, fast),
        mesh=mesh,
        in_specs=(
            P("shard", "ctx", None),
            P("shard", "ctx", None),
            P("shard"),
            P(),
            P("shard", None, None),
            P("shard", None, None),
            P("shard", None, None),
            P(),
            P(),
            P(),
        ),
        out_specs=(
            P("shard", "ctx", None),
            P("shard", "ctx", None),
            P("shard", None, None),
            P("shard", None, None),
            P("shard", None, None),
            P(),
            P(),
            P(),
        ),
        check_vma=False,
    )
```

```python
import functools
import math

import jax
import jax.numpy as jnp
import numpy as np
from jax import lax
from jax.experimental import pallas as pl
from jax.experimental.pallas import tpu as pltpu
from jax.sharding import PartitionSpec as P

HEADS = 16
HEAD_DIM = 64
FF = 2624
FF_WIDE = -(-FF // 128) * 128
STEP = 10
MESH = pl.DeviceIdType.MESH
DMA = pltpu.SemaphoreType.DMA

eps_norm = 1e-05
rope_base = 160000.0
mask_fill = -1e30
beta_one = 0.9
beta_two = 0.98
adam_eps = 1e-06
rate_matrix = 0.03
rate_gain = 0.6
decay_matrix = 0.01
BOTH = ("ctx", "shard")
VMEM_BYTES = 60 * 2**20


def transposed(left, right):
    return lax.dot_general(
        left, right, (((1,), (1,)), ((), ())), preferred_element_type=jnp.float32
    )


def leading(left, right):
    return lax.dot_general(
        left, right, (((0,), (0,)), ((), ())), preferred_element_type=jnp.float32
    )


def layer_norm(values, gain):
    row_mean = jnp.mean(values, axis=-1, keepdims=True)
    centred = values - row_mean
    variance = jnp.mean(centred * centred, axis=-1, keepdims=True)
    return centred * lax.rsqrt(variance + eps_norm) * gain


def rope_tables(seq, heads):
    half_dim = HEAD_DIM // 2
    inverse = rope_base ** (-2.0 * np.arange(half_dim) / HEAD_DIM)
    angles = np.arange(seq)[:, None] * inverse.astype(np.float32).astype(np.float64)[None, :]
    angles = angles.astype(np.float32).astype(np.float64)
    cosine, sine = np.cos(angles), np.sin(angles)
    cosine = np.concatenate([cosine, cosine] * heads, axis=1)
    sine = np.concatenate([-sine, sine] * heads, axis=1)
    return jnp.asarray(cosine, jnp.float32), jnp.asarray(sine, jnp.float32)


def half_turned(values):
    width = values.shape[-1]
    half = HEAD_DIM // 2
    lane = lax.broadcasted_iota(jnp.int32, values.shape, values.ndim - 1)
    if width == HEAD_DIM:
        return jnp.concatenate([values[:, half:], values[:, :half]], axis=1)
    ahead = pltpu.roll(values, width - half, axis=1)
    behind = pltpu.roll(values, half, axis=1)
    return jnp.where(lane % HEAD_DIM < half, ahead, behind)


def own_places(unit_owner, owner, chosen):
    every = jnp.arange(unit_owner.shape[0], dtype=jnp.int32)
    held = unit_owner == owner
    mine = jnp.any((every == chosen[:, None]) & held, axis=1)
    return mine, jnp.sum(((every < chosen[:, None]) & held).astype(jnp.int32), axis=1)


def adam_update(weight, gradient, first_old, second_old, step_rate, weight_decay):
    first_new = beta_one * first_old + (1.0 - beta_one) * gradient
    second_new = beta_two * second_old + (1.0 - beta_two) * gradient * gradient
    first_fix = 1.0 - beta_one**STEP
    second_fix = 1.0 - beta_two**STEP
    adam_step = first_new / first_fix / (jnp.sqrt(second_new / second_fix) + adam_eps)
    return (weight - step_rate * (adam_step + weight_decay * weight), first_new, second_new)


def qkv_kernel(norm_ref, w_ref, cos_ref, sin_ref, out_ref):
    tile = pl.program_id(0)
    turned_tiles = 2 * pl.num_programs(0) // 3
    values = transposed(norm_ref[...], w_ref[...])

    @pl.when(tile < turned_tiles)
    def _():
        out_ref[0] = (values * cos_ref[...] + half_turned(values) * sin_ref[...]).astype(
            out_ref.dtype
        )

    @pl.when(tile >= turned_tiles)
    def _():
        out_ref[0] = values.astype(out_ref.dtype)


def qkv_call(norm_one, w_qkv, cosine, sine):
    rows, width = norm_one.shape
    cols = 256
    tiles = width // cols
    return pl.pallas_call(
        qkv_kernel,
        grid=(3 * width // cols,),
        in_specs=[
            pl.BlockSpec((rows, width), lambda i: (0, 0)),
            pl.BlockSpec((cols, width), lambda i: (i, 0)),
            pl.BlockSpec((rows, cols), lambda i: (0, 0)),
            pl.BlockSpec((rows, cols), lambda i: (0, 0)),
        ],
        out_specs=pl.BlockSpec((1, rows, cols), lambda i: (i // tiles, 0, i % tiles)),
        out_shape=jax.ShapeDtypeStruct((3, rows, width), jnp.bfloat16),
        name="qkv",
    )(norm_one, w_qkv, cosine, sine)


def head_only(values, head):
    width = values.shape[-1]
    if width == HEAD_DIM:
        return values
    lane = lax.broadcasted_iota(jnp.int32, values.shape, 1)
    return jnp.where(lane // HEAD_DIM == head, values, jnp.zeros_like(values))


def key_bias(length, seq):
    position = lax.broadcasted_iota(jnp.int32, (1, seq), 1)
    return jnp.where(position < length, 0.0, mask_fill).astype(jnp.float32)


def attend_step(i, q_ref, k_ref, v_ref, bias, out_ref, wide_ref, lse_ref, chunk):
    width = k_ref.shape[1]
    heads = width // HEAD_DIM
    rows = pl.ds(pl.multiple_of(i * chunk, chunk), chunk)
    query = q_ref[rows, :] * jnp.bfloat16(0.125)
    total = None
    stats = None
    for h in range(heads):
        scores = transposed(query, head_only(k_ref[...], h)) + bias
        top = jnp.max(scores, axis=-1, keepdims=True)
        weights = jnp.exp(scores - top)
        norm = jnp.sum(weights, axis=-1, keepdims=True)
        low = (weights * (1.0 / norm)).astype(jnp.bfloat16)
        part = jnp.dot(low, head_only(v_ref[...], h), preferred_element_type=jnp.float32)
        lse = jnp.broadcast_to(top + jnp.log(norm), (chunk, width))
        total = part if total is None else total + part
        if stats is None:
            stats = lse
        else:
            lane = lax.broadcasted_iota(jnp.int32, lse.shape, 1)
            stats = jnp.where(lane // HEAD_DIM == h, lse, stats)
    out_ref[rows, :] = total.astype(jnp.bfloat16)
    wide_ref[rows, :] = total
    lse_ref[rows, :] = stats


def attend_slot(*args):
    def step(i, _):
        attend_step(i, *args)
        return 0

    lax.fori_loop(0, args[1].shape[0] // args[-1], step, 0)


def turned_back(grad, cos, sin):
    return grad * cos - half_turned(grad) * sin


def attend_back_step(
    i, q_ref, k_ref, v_ref, g_ref, wide_ref, lse_ref, bias, cos, sin, dq_ref, dk_ref, dv_ref, acc_k, acc_v, chunk
):
    seq, width = k_ref.shape
    heads = width // HEAD_DIM
    rows = pl.ds(pl.multiple_of(i * chunk, chunk), chunk)
    query = q_ref[rows, :]
    grad = g_ref[rows, :]
    lse_all = lse_ref[rows, :]
    both = grad.astype(jnp.float32) * wide_ref[rows, :]
    total = None
    for h in range(heads):
        key = head_only(k_ref[...], h)
        lse = lse_all[:, h * HEAD_DIM : h * HEAD_DIM + 1]
        delta = jnp.sum(head_only(both, h), axis=-1, keepdims=True)
        scores = transposed(query * jnp.bfloat16(0.125), key)
        weights = jnp.exp(scores + (bias - lse))
        back = transposed(grad, head_only(v_ref[...], h))
        low = (weights * (back - delta)).astype(jnp.bfloat16)
        part = jnp.dot(low, key, preferred_element_type=jnp.float32)
        total = part if total is None else total + part
        acc_v[...] += leading(weights.astype(jnp.bfloat16), head_only(grad, h))
        acc_k[...] += leading(low, head_only(query, h))
    dq_ref[rows, :] = turned_back(total * 0.125, cos[rows, :], sin[rows, :]).astype(jnp.bfloat16)


def attend_back_end(
    q_ref, k_ref, v_ref, g_ref, wide_ref, lse_ref, bias, cos, sin, dq_ref, dk_ref, dv_ref, acc_k, acc_v, chunk
):
    dk_ref[...] = turned_back(acc_k[...] * 0.125, cos[...], sin[...]).astype(jnp.bfloat16)
    dv_ref[...] = acc_v[...].astype(jnp.bfloat16)


def attend_back_slot(*args):
    acc_k, acc_v, chunk = args[-3:]
    acc_k[...] = jnp.zeros_like(acc_k)
    acc_v[...] = jnp.zeros_like(acc_v)

    def step(i, _):
        attend_back_step(i, *args)
        return 0

    lax.fori_loop(0, args[1].shape[0] // chunk, step, 0)
    attend_back_end(*args)


def attend_kernel(slots, chunk, qkv_ref, lengths_ref, out_ref, wide_ref, lse_ref):
    for s in range(slots):
        attend_slot(
            qkv_ref.at[0, s], qkv_ref.at[1, s], qkv_ref.at[2, s], key_bias(lengths_ref[s], qkv_ref.shape[2]),
            out_ref.at[s], wide_ref.at[s], lse_ref.at[s], chunk,
        )


def attend_call(qkv, lengths):
    _, slots, seq, width = qkv.shape
    chunk = 256
    return pl.pallas_call(
        functools.partial(attend_kernel, slots, chunk),
        out_shape=(
            jax.ShapeDtypeStruct((slots, seq, width), jnp.bfloat16),
            jax.ShapeDtypeStruct((slots, seq, width), jnp.float32),
            jax.ShapeDtypeStruct((slots, seq, width), jnp.float32),
        ),
        in_specs=[pl.BlockSpec(memory_space=pltpu.VMEM), pl.BlockSpec(memory_space=pltpu.SMEM)],
        compiler_params=pltpu.CompilerParams(vmem_limit_bytes=VMEM_BYTES),
        name="attend",
    )(qkv, lengths)


def attend_back_kernel(slots, chunk, qkv_ref, g_ref, wide_ref, lse_ref, lengths_ref, cos_ref, sin_ref, out_ref, acc_k, acc_v):
    for s in range(slots):
        attend_back_slot(
            qkv_ref.at[0, s], qkv_ref.at[1, s], qkv_ref.at[2, s], g_ref.at[s],
            wide_ref.at[s], lse_ref.at[s], key_bias(lengths_ref[s], qkv_ref.shape[2]), cos_ref, sin_ref,
            out_ref.at[0, s], out_ref.at[1, s], out_ref.at[2, s], acc_k, acc_v, chunk,
        )


def attend_back_call(qkv, grad_heads, wide, lse, lengths, cosine, sine):
    _, slots, seq, width = qkv.shape
    chunk = 256
    return pl.pallas_call(
        functools.partial(attend_back_kernel, slots, chunk),
        out_shape=jax.ShapeDtypeStruct(qkv.shape, jnp.bfloat16),
        in_specs=[pl.BlockSpec(memory_space=pltpu.VMEM)] * 4
        + [pl.BlockSpec(memory_space=pltpu.SMEM)]
        + [pl.BlockSpec(memory_space=pltpu.VMEM)] * 2,
        scratch_shapes=[pltpu.VMEM((seq, width), jnp.float32)] * 2,
        compiler_params=pltpu.CompilerParams(vmem_limit_bytes=VMEM_BYTES),
        name="attend_back",
    )(qkv, grad_heads, wide, lse, lengths, cosine, sine)


def middle_kernel(
    tile, block_len, mixed_ref, tokens_ref, cot_ref, gains_ref, lengths_ref, w_ref,
    out_ref, left_ref, right_ref, go_ref, back_ref, gain_ref,
    w_out, w_one, w_two, w_down, x1, result, dnorm, sems
):
    rows_all, width = tokens_ref.shape
    wide = w_one.shape[0] * tile
    tiles = wide // tile
    cols = 256
    some = 64
    start = lax.axis_index("ctx") * block_len

    def live(i):
        slot, inner = i * some // block_len, i * some % block_len
        position = start + inner + lax.broadcasted_iota(jnp.int32, (some, 1), 0)
        return (position < lengths_ref[slot]).astype(jnp.float32)

    def copies(j):
        rows = [pl.ds(width + k * wide + j * tile, tile) for k in range(3)]
        return [
            pltpu.make_async_copy(w_ref.at[r], to.at[j], sems.at[1 + j * 3 + k])
            for k, (r, to) in enumerate(zip(rows, (w_one, w_two, w_down)))
        ]

    first = pltpu.make_async_copy(w_ref.at[pl.ds(0, width)], w_out, sems.at[0])
    first.start()
    for j in range(tiles):
        for copy in copies(j):
            copy.start()
    right_ref[0] = mixed_ref[...]
    first.wait()

    def out_step(t, _):
        at = pl.ds(pl.multiple_of(t * cols, cols), cols)
        x1[:, at] = tokens_ref[:, at].astype(jnp.float32) + transposed(mixed_ref[...], w_out[at, :])
        return 0

    lax.fori_loop(0, width // cols, out_step, 0)

    def normal(at):
        values = x1[at, :]
        mean = jnp.mean(values, axis=-1, keepdims=True)
        centred = values - mean
        scale = lax.rsqrt(jnp.mean(centred * centred, axis=-1, keepdims=True) + eps_norm)
        return centred * scale, scale

    def norm_step(i, _):
        at = pl.ds(pl.multiple_of(i * some, some), some)
        unit, _ = normal(at)
        right_ref[1, at, :] = (unit * gains_ref[1:2, :]).astype(jnp.bfloat16)
        right_ref[2, at, :] = (cot_ref[at, :].astype(jnp.float32) * live(i)).astype(jnp.bfloat16)
        return 0

    lax.fori_loop(0, rows_all // some, norm_step, 0)
    result[...] = x1[...]
    dnorm[...] = jnp.zeros_like(dnorm)
    for j in range(tiles):
        for copy in copies(j):
            copy.wait()
        norm, grad = right_ref[1], right_ref[2]
        one = transposed(norm, w_one[j])
        two = transposed(norm, w_two[j])
        back = transposed(grad, w_down[j])
        share = 0.5 * (1.0 + lax.erf(one * (0.5**0.5)))
        gelu = one * share
        slope = share + one * (jnp.exp(-0.5 * one * one) * (0.5 / math.pi) ** 0.5)
        low = (gelu * two).astype(jnp.bfloat16)
        d_one = (back * two * slope).astype(jnp.bfloat16)
        d_two = (back * gelu).astype(jnp.bfloat16)
        for k, part in enumerate((d_one, d_two, low)):
            left_ref[:, pl.ds(width + k * wide + j * tile, tile)] = part
        result[...] += jnp.dot(low, w_down[j], preferred_element_type=jnp.float32)
        dnorm[...] += jnp.dot(d_one, w_one[j], preferred_element_type=jnp.float32) + jnp.dot(
            d_two, w_two[j], preferred_element_type=jnp.float32
        )
    end = width + 3 * wide
    if left_ref.shape[1] > end:
        left_ref[:, end:] = jnp.zeros((rows_all, left_ref.shape[1] - end), left_ref.dtype)
    out_ref[...] = result[...].astype(out_ref.dtype)
    gain_ref[...] = jnp.zeros_like(gain_ref)

    def back_step(i, _):
        at = pl.ds(pl.multiple_of(i * some, some), some)
        unit, scale = normal(at)
        given = dnorm[at, :]
        inner = given * gains_ref[1:2, :]
        inner_mean = jnp.mean(inner, axis=-1, keepdims=True)
        along = jnp.mean(inner * unit, axis=-1, keepdims=True)
        grad = cot_ref[at, :].astype(jnp.float32) * live(i)
        grad = grad + scale * (inner - inner_mean - unit * along)
        back_ref[at, :] = grad
        left_ref[at, 0:width] = grad.astype(jnp.bfloat16)
        gain_ref[1:2, :] += jnp.sum(given * unit, axis=0, keepdims=True)
        return 0

    lax.fori_loop(0, rows_all // some, back_step, 0)

    def go_step(t, _):
        at = pl.ds(pl.multiple_of(t * cols, cols), cols)
        go_ref[:, at] = jnp.dot(
            left_ref[:, 0:width], w_out[:, at], preferred_element_type=jnp.float32
        ).astype(jnp.bfloat16)
        return 0

    lax.fori_loop(0, width // cols, go_step, 0)


def middle_call(mixed, tokens, cotangent, gains, lengths, stack_b, left_cols, block_len):
    rows_all, width = tokens.shape
    low = jnp.bfloat16
    tile = 896 if FF_WIDE % 896 == 0 else 128
    tiles = FF_WIDE // tile
    vmem = pl.BlockSpec(memory_space=pltpu.VMEM)
    return pl.pallas_call(
        functools.partial(middle_kernel, tile, block_len),
        out_shape=(
            jax.ShapeDtypeStruct((rows_all, width), low),
            jax.ShapeDtypeStruct((rows_all, left_cols), low),
            jax.ShapeDtypeStruct((3, rows_all, width), low),
            jax.ShapeDtypeStruct((rows_all, width), low),
            jax.ShapeDtypeStruct((rows_all, width), jnp.float32),
            jax.ShapeDtypeStruct((8, width), jnp.float32),
        ),
        in_specs=[vmem] * 4 + [pl.BlockSpec(memory_space=pltpu.SMEM), pl.BlockSpec(memory_space=pl.ANY)],
        out_specs=(vmem,) * 6,
        scratch_shapes=[pltpu.VMEM((width, width), low)]
        + [pltpu.VMEM((tiles, tile, width), low)] * 3
        + [pltpu.VMEM((rows_all, width), jnp.float32)] * 3
        + [DMA((1 + 3 * tiles,))],
        compiler_params=pltpu.CompilerParams(vmem_limit_bytes=VMEM_BYTES),
        name="middle",
    )(mixed, tokens, cotangent, gains, lengths, stack_b)


def adam_kernel(per, unit_ref, a_ref, b_ref, *refs):
    grads = (refs[:per], refs[per : 2 * per])
    gain_grad, *gains = refs[2 * per : 2 * per + 4]
    master, first, second, new_master, new_first, new_second, *new_gains = refs[2 * per + 4 :]

    @pl.when(pl.program_id(0) == 0)
    def _():
        rows = gains[0].shape[0]
        updated = adam_update(
            gains[0][...], gain_grad[0:rows, :], gains[1][...], gains[2][...], rate_gain, 0.0
        )
        for ref, value in zip(new_gains, updated):
            ref[...] = value

    for j in range(per):
        slot = pl.program_id(0) * per + j
        unit = unit_ref[slot]
        grad = jnp.where(unit == 0, grads[0][j][0], grads[1][j][0]).astype(jnp.float32)
        grad = jnp.where(unit >= 0, grad, 0.0)
        weight, one, two = adam_update(
            master[j], grad, first[j], second[j], rate_matrix, decay_matrix
        )
        new_master[j] = weight
        new_first[j] = one
        new_second[j] = two


def adam_call(kind, at_a, at_b, grads_a, grads_b, gain_grad, gains, master, first, second):
    capacity, rows, width = master.shape
    per = max(p for p in range(1, 8) if capacity % p == 0)

    def unit_spec(j, chunk):
        return pl.BlockSpec(
            (1, rows, width), lambda i, kind, *at: (at[chunk][i * per + j], 0, 0)
        )

    def whole(array):
        return pl.BlockSpec(array.shape, lambda i, kind, *at: (0, 0))

    slot_spec = pl.BlockSpec((per, rows, width), lambda i, kind, *at: (i, 0, 0))
    return pl.pallas_call(
        functools.partial(adam_kernel, per),
        grid_spec=pltpu.PrefetchScalarGridSpec(
            num_scalar_prefetch=3,
            grid=(capacity // per,),
            in_specs=[unit_spec(j, c) for c in range(2) for j in range(per)]
            + [whole(a) for a in (gain_grad, *gains)]
            + [slot_spec] * 3,
            out_specs=[slot_spec] * 3 + [whole(a) for a in gains],
        ),
        out_shape=[jax.ShapeDtypeStruct(a.shape, jnp.float32) for a in (master, first, second, *gains)],
        compiler_params=pltpu.CompilerParams(vmem_limit_bytes=VMEM_BYTES),
        name="adamw",
    )(kind, at_a, at_b, *([grads_a] * per), *([grads_b] * per), gain_grad, *gains, master, first, second)


def pick_kernel(part_ref, master_ref, out_ref, got, sems):
    count, rows = got.shape[:2]

    def at(p):
        return pl.ds(pl.multiple_of(p * rows, rows), rows)

    def copy(p):
        return pltpu.make_async_copy(master_ref.at[part_ref[p]], got.at[p], sems.at[p])

    def start(p, _):
        @pl.when(part_ref[p] >= 0)
        def _():
            copy(p).start()

        return 0

    def end(p, _):
        @pl.when(part_ref[p] >= 0)
        def _():
            copy(p).wait()
            out_ref[at(p), :] = got[p].astype(out_ref.dtype)

        return 0

    unroll = max(u for u in (1, 2, 4, 8) if count % u == 0)
    lax.fori_loop(0, count, start, 0, unroll=unroll)
    out_ref[...] = jnp.zeros_like(out_ref)
    lax.fori_loop(0, count, end, 0, unroll=unroll)


def pick_call(part, parts):
    shape = (part.shape[0],) + parts.shape[1:]
    flat = (shape[0] * shape[1], shape[2])
    return pl.pallas_call(
        pick_kernel,
        grid_spec=pltpu.PrefetchScalarGridSpec(
            num_scalar_prefetch=1,
            grid=(1,),
            in_specs=[pl.BlockSpec(memory_space=pl.ANY)],
            out_specs=pl.BlockSpec(flat, lambda i, part: (0, 0)),
            scratch_shapes=[pltpu.VMEM(shape, parts.dtype), DMA((part.shape[0],))],
        ),
        out_shape=jax.ShapeDtypeStruct(flat, jnp.bfloat16),
        compiler_params=pltpu.CompilerParams(vmem_limit_bytes=VMEM_BYTES),
        name="pick",
    )(part, parts)


def place():
    ctx, shard = lax.axis_index("ctx"), lax.axis_index("shard")
    return ctx // 2, ctx % 2, shard // 2, shard % 2


def device_at(z, y, x, core):
    return (z * 2 + y, x * 2 + core)


def piece_at(zb, c, h, a, b):
    return (((zb * 2 + c) * 2 + h) * 2 + a) * 2 + b


def remote(src, dst, send, recv, device):
    return pltpu.make_async_remote_copy(
        src_ref=src, dst_ref=dst, send_sem=send, recv_sem=recv, device_id=device, device_id_type=MESH
    )


def greet(devices):
    barrier = pltpu.get_barrier_semaphore()
    for device in devices:
        pl.semaphore_signal(barrier, inc=1, device_id=device, device_id_type=MESH)
    pl.semaphore_wait(barrier, len(devices))


def line_neighbours():
    z, y, x, core = place()
    return [device_at(z, y, 1 - x, core), device_at(z, 1 - y, x, core), device_at(z, y, x, 1 - core)] + [
        device_at((z + d) % 4, y, x, core) for d in (1, 2, 3)
    ]


def rows_at(ref, piece, count, rows):
    return ref.at[pl.ds(pl.multiple_of(piece * rows, 16), count * rows)]


GATHER_SEMS = [DMA((2,))] + [DMA((2, 4, 2))] * 2 + [DMA((2, 4))] * 2 + [DMA((2, 4, 2))] * 2 + [DMA((4,))] * 2


class Gather:
    def __init__(self, own, buf, rows, sems):
        self.own, self.buf, self.rows = own, buf, rows
        self.lsem, self.zs, self.zr, self.fs, self.fr, self.ts, self.tr, self.ss, self.sr = sems
        self.z, self.y, self.x, self.core = z, y, x, core = place()
        self.xn = device_at(z, y, 1 - x, core)
        self.yn = device_at(z, 1 - y, x, core)
        self.sib = device_at(z, y, x, 1 - core)

    def side(self, h):
        return (self.y, self.x) if h == 0 else (self.x, self.y)

    def near(self, h):
        return (self.xn, self.yn) if h == 0 else (self.yn, self.xn)

    def piece(self, zb, h, a, b):
        return rows_at(self.buf, piece_at(zb, self.core, h, a, b), 1, self.rows)

    def keep(self, h):
        return pltpu.make_async_copy(self.own(h), self.piece(self.z, h, *self.side(h)), self.lsem.at[h])

    def up(self, d, h, step, src=None):
        ref = self.piece(self.z + d, h, *self.side(h))
        k, hop = (0, -d) if step > 0 else (1, d)
        return remote(
            ref if src is None else src,
            ref,
            self.zs.at[k, hop, h],
            self.zr.at[k, hop, h],
            device_at(self.z + step, self.y, self.x, self.core),
        )

    def got(self, d, h):
        ref = self.piece(self.z + d, h, *self.side(h))
        k, hop = (0 if d < 0 else 1), abs(d) - 1
        remote(ref, ref, self.zs.at[k, hop, h], self.zr.at[k, hop, h], self.xn).wait_recv()

    def first(self, zb, h, mine, src=None):
        a, b = self.side(h)
        ref = self.piece(zb, h, a, b if mine else 1 - b)
        return remote(
            ref if src is None else src, ref, self.fs.at[h, zb], self.fr.at[h, zb], self.near(h)[0]
        )

    def second(self, zb, h, j, mine, src=None):
        a, b = self.side(h)
        ref = self.piece(zb, h, a if mine else 1 - a, b if j == 0 else 1 - b)
        return remote(
            ref if src is None else src, ref, self.ts.at[h, zb, j], self.tr.at[h, zb, j], self.near(h)[1]
        )

    def whole(self, zb, c):
        ref = rows_at(self.buf, (zb * 2 + c) * 8, 8, self.rows)
        return remote(ref, ref, self.ss.at[zb], self.sr.at[zb], self.sib)

    def start(self):
        for h in range(2):
            self.keep(h).start()
        for h in range(2):

            @pl.when(self.z < 3)
            def _():
                self.up(0, h, 1, self.own(h)).start()

            @pl.when(self.z > 0)
            def _():
                self.up(0, h, -1, self.own(h)).start()

            self.first(self.z, h, True, self.own(h)).start()
        for h in range(2):
            self.second(self.z, h, 0, True, self.own(h)).start()
        for h in range(2):
            self.keep(h).wait()

    def there(self, d, work):
        if d == 0:
            work()
        else:
            pl.when((self.z + d >= 0) & (self.z + d < 4))(work)

    def line(self, d):
        def work():
            zb = self.z + d
            for h in range(2):
                self.got(d, h)
                if d < 0:

                    @pl.when(self.z < 3)
                    def _():
                        self.up(d, h, 1).start()
                else:

                    @pl.when(self.z > 0)
                    def _():
                        self.up(d, h, -1).start()

                self.first(zb, h, True).start()
            for h in range(2):
                self.second(zb, h, 0, True).start()

        self.there(d, work)

    def cross(self, d):
        def work():
            zb = self.z + d
            for h in range(2):
                self.first(zb, h, False).wait_recv()
                self.second(zb, h, 1, True).start()

        self.there(d, work)

    def close(self, d):
        def work():
            zb = self.z + d
            for h in range(2):
                for j in range(2):
                    self.second(zb, h, j, False).wait_recv()
            self.whole(zb, self.core).start()

        self.there(d, work)

    def finish(self, take=True):
        for h in range(2):
            for d in range(4):

                @pl.when((self.z - d >= 0) & (self.z < 3))
                def _():
                    self.up(-d, h, 1).wait_send()

                @pl.when((self.z + d < 4) & (self.z > 0))
                def _():
                    self.up(d, h, -1).wait_send()

        for zb in range(4):
            for h in range(2):
                self.first(zb, h, True).wait_send()
                for j in range(2):
                    self.second(zb, h, j, True).wait_send()
            self.whole(zb, self.core).wait_send()
            if take:
                self.whole(zb, 1 - self.core).wait_recv()


REDUCE_REFS = 10


def reduce_scratch(rows, width):
    def buf(n):
        return pltpu.VMEM((n * rows, width), jnp.bfloat16)

    return (
        [buf(32), buf(16), buf(8), buf(10)]
        + [DMA((4, 2, 2))] * 2
        + [DMA((4, 2))] * 3
        + [DMA((5, 2))]
    )


class Reduce:
    def __init__(self, rows, refs):
        self.acc, self.got1, self.got2, self.got3 = refs[:4]
        self.s1, self.r1, self.s2, self.r2, self.s3, self.r3 = refs[4:]
        self.rows = rows
        self.z, self.y, self.x, self.core = z, y, x, core = place()
        self.xn = device_at(z, y, 1 - x, core)
        self.yn = device_at(z, 1 - y, x, core)
        self.sib = device_at(z, y, x, 1 - core)

    def zb(self, t):
        s = self.z // 2
        return (3 - 3 * s, 2 - s, 1 - self.z + 4 * s, self.z)[t]

    def base(self, zb):
        return zb * 8

    def side(self, h):
        return (self.y, self.x) if h == 0 else (self.x, self.y)

    def near(self, h):
        return (self.yn, self.xn) if h == 0 else (self.xn, self.yn)

    def send1(self, t, h, q):
        zb = self.zb(t)
        a, b = self.side(h)
        b = 1 - b if q == 0 else b
        return remote(
            rows_at(self.acc, self.base(zb) + h * 4 + (1 - a) * 2 + b, 1, self.rows),
            rows_at(self.got1, zb * 4 + h * 2 + b, 1, self.rows),
            self.s1.at[zb, h, q],
            self.r1.at[zb, h, q],
            self.near(h)[0],
        )

    def send2(self, t, h):
        zb = self.zb(t)
        a, b = self.side(h)
        return remote(
            rows_at(self.acc, self.base(zb) + h * 4 + a * 2 + 1 - b, 1, self.rows),
            rows_at(self.got2, zb * 2 + h, 1, self.rows),
            self.s2.at[zb, h],
            self.r2.at[zb, h],
            self.near(h)[1],
        )

    def send3(self, t, h, up):
        zb = self.zb(t)
        a, b = self.side(h)
        slot = zb if up else zb + (4 - zb) * (1 - (self.z - 1 - zb + 2) // 3)
        return remote(
            rows_at(self.acc, self.base(zb) + h * 4 + a * 2 + b, 1, self.rows),
            rows_at(self.got3, slot * 2 + h, 1, self.rows),
            self.s3.at[t, h],
            self.r3.at[slot, h],
            device_at(self.z + (1 if up else -1), self.y, self.x, self.core),
        )

    def come3(self, slot, h):
        ref = rows_at(self.got3, slot * 2 + h, 1, self.rows)
        remote(ref, ref, self.s3.at[0, h], self.r3.at[slot, h], self.xn).wait_recv()
        a, b = self.side(h)
        zb = self.z if isinstance(slot, int) else slot
        self.add(self.base(zb) + h * 4 + a * 2 + b, self.got3, slot * 2 + h, 1)

    def add(self, at, ref, start, count):
        def body(i, _):
            to = pl.ds(pl.multiple_of((at + i) * self.rows, 16), self.rows)
            given = pl.ds(pl.multiple_of((start + i) * self.rows, 16), self.rows)
            self.acc[to, :] = self.acc[to, :] + ref[given, :]
            return 0

        lax.fori_loop(0, count, body, 0)

    def go1(self, t, q):
        for h in range(2):
            self.send1(t, h, q).start()

    def one(self, t, q):
        zb = self.zb(t)
        for h in range(2):
            a, b = self.side(h)
            b = 1 - b if q == 0 else b
            self.send1(t, h, q).wait_recv()
            self.add(self.base(zb) + h * 4 + a * 2 + b, self.got1, zb * 4 + h * 2 + b, 1)
            if q == 0:
                self.send2(t, h).start()

    def two(self, t):
        zb = self.zb(t)
        for h in range(2):
            a, b = self.side(h)
            self.send2(t, h).wait_recv()
            self.add(self.base(zb) + h * 4 + a * 2 + b, self.got2, zb * 2 + h, 1)

    def tri(self, t, first):
        zb = self.zb(t)
        z = self.z
        inner = ((zb > z) & (z > 0)) | ((zb < z) & (z < 3))
        for h in range(2):
            if not first:

                @pl.when(inner)
                def _():
                    self.come3(zb, h)

            now = jnp.logical_not(inner) if first else inner

            @pl.when((zb > z) & now)
            def _():
                self.send3(t, h, True).start()

            @pl.when((zb < z) & now)
            def _():
                self.send3(t, h, False).start()

    def three(self):
        for h in range(2):

            @pl.when(self.z > 0)
            def _():
                self.come3(self.z, h)

            @pl.when(self.z < 3)
            def _():
                self.come3(4, h)

    def own(self, h):
        a, b = self.side(h)
        return rows_at(self.acc, self.base(self.z) + h * 4 + a * 2 + b, 1, self.rows)

    def finish(self):
        for t in range(4):
            for h in range(2):
                for q in range(2):
                    self.send1(t, h, q).wait_send()
                self.send2(t, h).wait_send()
                if t < 3:
                    ref = rows_at(self.got3, h, 1, self.rows)
                    remote(ref, ref, self.s3.at[t, h], self.r3.at[0, h], self.xn).wait_send()


LATE_GATHER_SEMS = [DMA] + [DMA((3, 4))] * 2 + [DMA((3,))] * 2 + [DMA((4,))] * 2


class LateGather:
    def __init__(self, own, buf, rows, sems):
        self.own, self.buf, self.rows = own, buf, rows
        self.lsem, self.zs, self.zr, self.fs, self.fr, self.ss, self.sr = sems
        self.meet()

    def meet(self):
        self.z, self.y, self.x, self.core = z, y, x, core = place()
        self.xn = device_at(z, y, 1 - x, core)
        self.yn = device_at(z, 1 - y, x, core)
        self.sib = device_at(z, y, x, 1 - core)

    def one_of(self, y, x):
        return rows_at(self.buf, ((self.z * 2 + self.core) * 2 + y) * 2 + x, 1, self.rows)

    def block(self, zb, c):
        return rows_at(self.buf, (zb * 2 + c) * 4, 4, self.rows)

    def hand(self, i, mine):
        y, x = self.y, self.x
        at = ((y, x) if mine else (1 - y, x), (y, x) if mine else (y, 1 - x), (1 - y, x if mine else 1 - x))[i]
        ref = self.one_of(*at)
        src = self.own() if mine and i < 2 else ref
        return remote(src, ref, self.fs.at[i], self.fr.at[i], self.yn if i == 0 else self.xn)

    def keep(self):
        return pltpu.make_async_copy(self.own(), self.one_of(self.y, self.x), self.lsem)

    def start(self):
        self.keep().start()
        self.hand(0, True).start()
        self.hand(1, True).start()
        self.keep().wait()

    def pass_on(self):
        self.hand(0, False).wait_recv()
        self.hand(2, True).start()

    def far_copy(self, d, i, zb):
        ref = rows_at(self.buf, (zb * 2 + self.core) * 4 + i, 1, self.rows)
        to = device_at((self.z + d) % 4, self.y, self.x, self.core)
        return remote(ref, ref, self.zs.at[d - 1, i], self.zr.at[d - 1, i], to)

    def far(self, d, i):
        self.far_copy(d, i, self.z).start()

    def whole(self, zb, c):
        ref = self.block(zb, c)
        return remote(ref, ref, self.ss.at[zb], self.sr.at[zb], self.sib)

    def ready(self):
        self.hand(1, False).wait_recv()
        self.hand(2, False).wait_recv()
        self.whole(self.z, self.core).start()

    def come(self, d):
        zb = (self.z - d) % 4
        for i in range(4):
            self.far_copy(d, i, zb).wait_recv()
        self.whole(zb, self.core).start()

    def finish(self):
        for i in range(3):
            self.hand(i, True).wait_send()
            for k in range(4):
                self.far_copy(i + 1, k, self.z).wait_send()
        for zb in range(4):
            self.whole(zb, self.core).wait_send()
            self.whole(zb, 1 - self.core).wait_recv()


LATE_REDUCE_REFS = 8
ROWS_C = 32


def late_reduce_scratch(rows, width):
    def buf(n):
        return pltpu.VMEM((n * rows, width), jnp.bfloat16)

    return [buf(16), buf(2), buf(1), buf(12), DMA((3,)), DMA((3,)), DMA((3, 4)), DMA((3, 4))]


class LateReduce:
    def __init__(self, rows, refs):
        self.acc, self.got1, self.got2, self.got3 = refs[:4]
        self.s1, self.r1, self.s3, self.r3 = refs[4:]
        self.rows = rows
        self.meet()

    def meet(self):
        self.z, self.y, self.x, self.core = z, y, x, core = place()
        self.xn = device_at(z, y, 1 - x, core)
        self.yn = device_at(z, 1 - y, x, core)
        self.sib = device_at(z, y, x, 1 - core)
    def add(self, to, given):
        rows = self.rows

        def body(i, _):
            at = pl.ds(pl.multiple_of(i * rows, 16), rows)
            to[at, :] = to[at, :] + given[at, :]
            return 0

        lax.fori_loop(0, to.shape[0] // rows, body, 0)

    def part(self, zb, at, count=1):
        return rows_at(self.acc, zb * 4 + at, count, self.rows)

    def far_copy(self, d, i):
        zb = (self.z + d) % 4
        return remote(
            self.part(zb, i),
            rows_at(self.got3, (d - 1) * 4 + i, 1, self.rows),
            self.s3.at[d - 1, i],
            self.r3.at[d - 1, i],
            device_at(zb, self.y, self.x, self.core),
        )

    def far(self, d, i):
        self.far_copy(d, i).start()

    def to_x(self, yb):
        src = self.part(self.z, yb * 2 + 1 - self.x)
        return remote(src, rows_at(self.got1, yb, 1, self.rows), self.s1.at[yb], self.r1.at[yb], self.xn)

    def to_y(self):
        src = self.part(self.z, (1 - self.y) * 2 + self.x)
        return remote(src, self.got2, self.s1.at[2], self.r1.at[2], self.yn)

    def three(self):
        for d in (1, 2, 3):
            for i in range(4):
                self.far_copy(d, i).wait_recv()
            self.add(self.part(self.z, 0, 4), rows_at(self.got3, (d - 1) * 4, 4, self.rows))
        for yb in range(2):
            self.to_x(yb).start()

    def one(self):
        for yb in range(2):
            self.to_x(yb).wait_recv()
            self.add(self.part(self.z, yb * 2 + self.x), rows_at(self.got1, yb, 1, self.rows))
        self.to_y().start()

    def two(self):
        self.to_y().wait_recv()
        self.add(self.own(), self.got2)

    def own(self):
        return self.part(self.z, self.y * 2 + self.x)

    def finish(self):
        for yb in range(2):
            self.to_x(yb).wait_send()
        self.to_y().wait_send()
        for d in (1, 2, 3):
            for i in range(4):
                self.far_copy(d, i).wait_send()


def front_kernel(
    given_ref, tokens_ref, gains_ref, cos_ref, sin_ref, lengths_ref,
    oa_ref, ob_ref, heads, wide_ref, lse_ref, mixed_ref, norm_ref,
    stack, rows, seen, low, mixed, got_a, got_b, new_a, new_b, own_a, own_b, got_c, new_c, own_c, send, recv, csem, ql, qsend, qrecv, ml, msend, mrecv, *sems
):
    n = 8
    z, y, x, core = place()
    ctx, shard = lax.axis_index("ctx"), lax.axis_index("shard")
    m = len(GATHER_SEMS)
    rows_a, rows_b = own_a.shape[0] // 2, own_b.shape[0] // 2
    ga = Gather(lambda h: rows_at(own_a, h, 1, rows_a), stack, rows_a, sems[:m])
    rows_c = own_c.shape[0]
    start_c = 64 * rows_b
    gb = Gather(lambda h: rows_at(own_b, h, 1, rows_b), ob_ref.at[pl.ds(0, start_c)], rows_b, sems[m : 2 * m])
    gc = LateGather(lambda: own_c, ob_ref.at[pl.ds(start_c, 32 * rows_c)], rows_c, sems[2 * m :])
    _, slots, block_len, width = rows.shape
    seq, my_width = seen.shape[2:]
    greet([ga.xn, ga.sib] + [(lax.rem(ctx + d, n), shard) for d in range(1, n)])
    jobs = (
        (0, got_a, new_a, own_a),
        (8 * rows_a, got_b, new_b, own_b),
        (8 * (rows_a + rows_b), got_c, new_c, own_c),
    )

    def share(i, c, xb):
        start, got, new, own = jobs[i]
        size = own.shape[0]
        at = start + c * 2 * size
        if xb is None:
            return given_ref.at[pl.ds(pl.multiple_of(at, 16), 2 * size)]
        return given_ref[pl.ds(pl.multiple_of(at + xb * size, 16), size), :]

    def held(i, xb):
        size = jobs[i][3].shape[0]
        return pl.ds(pl.multiple_of(xb * size, 16), size)

    def to_core(i):
        return remote(share(i, 1 - core, None), jobs[i][1], send.at[i], recv.at[i], ga.sib)

    def to_x(i):
        start, got, new, own = jobs[i]
        return remote(got.at[held(i, 1 - x)], new, send.at[3 + i], recv.at[3 + i], ga.xn)

    def spread(i):
        start, got, new, own = jobs[i]
        to_core(i).wait_recv()
        got[held(i, 1 - x), :] = got[held(i, 1 - x), :] + share(i, core, 1 - x)
        to_x(i).start()
        own[...] = got[held(i, x), :] + share(i, core, x)

    def cross(i):
        start, got, new, own = jobs[i]
        to_x(i).wait_recv()
        own[...] = own[...] + new[...]

    def peer(d):
        return lax.rem(ctx + d, n)

    def lanes(owner):
        return pl.ds(pl.multiple_of(owner * my_width, my_width), my_width)

    def block(owner):
        return pl.ds(pl.multiple_of(owner * block_len, block_len), block_len)

    def head_copy(j, owner):
        return remote(
            rows.at[j, :, :, lanes(owner)], seen.at[j, :, block(ctx), :], qsend.at[j, owner], qrecv.at[j, ctx], (owner, shard)
        )

    def head_own(j):
        return pltpu.make_async_copy(rows.at[j, :, :, lanes(ctx)], seen.at[j, :, block(ctx), :], ql.at[j])

    def mixed_copy(s, d):
        return remote(
            low.at[s, block(peer(d)), :], mixed.at[s, :, lanes(ctx)], msend.at[s, d], mrecv.at[s, d], (peer(d), shard)
        )

    def mixed_own(s):
        return pltpu.make_async_copy(low.at[s, block(ctx), :], mixed.at[s, :, lanes(ctx)], ml.at[s])

    cols = 256
    tiles = width // cols
    per_z = 16 * rows_a // cols

    def region(i):
        s = z // 2
        t = z % 2
        return (
            z,
            (1 - t) * (1 - s) + s * (1 + t),
            2 * (1 - s) + s * (3 - 2 * t),
            3 * (1 - s),
        )[i]

    def norm():
        def step(i, _):
            at = pl.ds(pl.multiple_of(i * 64, 64), 64)
            values = layer_norm(tokens_ref[at, :].astype(jnp.float32), gains_ref[0:1, :])
            norm_ref[at, :] = values.astype(jnp.bfloat16)
            return 0

        lax.fori_loop(0, slots * block_len // 64, step, 0)

    def table(ref):
        one = ref[block(ctx), :]
        one = jnp.concatenate([one] * (cols // my_width), axis=1)
        return jnp.concatenate([one] * slots, axis=0)

    def qkv(i):
        zb = region(i)
        ga.whole(zb, 1 - core).wait_recv()

        def tile_step(k, _):
            tile = zb * per_z + k
            j, t = tile // tiles, tile % tiles
            at = pl.ds(pl.multiple_of(t * cols, cols), cols)
            weight = stack[pl.ds(pl.multiple_of(tile * cols, cols), cols), :]
            values = transposed(norm_ref[...], weight)
            turn = (j < 2).astype(jnp.float32)
            cos = table(cos_ref) * turn + (1.0 - turn)
            values = values * cos + half_turned(values) * (table(sin_ref) * turn)
            rows[j, :, :, at] = values.astype(jnp.bfloat16).reshape(slots, block_len, cols)
            for q in range(cols // my_width):
                owner = t * (cols // my_width) + q

                @pl.when(owner == ctx)
                def _():
                    head_own(j).start()

                @pl.when(owner != ctx)
                def _():
                    head_copy(j, owner).start()

            return 0

        lax.fori_loop(0, per_z, tile_step, 0)

    def heads_wait(j):
        head_own(j).wait()
        for d in range(1, n):
            ref = seen.at[j, :, block(peer(d)), :]
            remote(ref, ref, qsend.at[j, peer(d)], qrecv.at[j, peer(d)], (peer(d), shard)).wait_recv()

    def mixed_wait():
        for s in range(slots):
            mixed_own(s).wait()
            for d in range(1, n):
                mixed_copy(s, d).wait_recv()

    for i in range(3):
        to_core(i).start()
    spread(0)
    spread(1)
    spread(2)
    cross(0)
    ga.start()
    norm()
    ga.line(-1), ga.line(1)
    ga.cross(0)
    cross(2)
    gc.start()
    ga.line(-2), ga.line(2)
    cross(1)
    gb.start()
    ga.cross(-1), ga.cross(1)
    gc.pass_on()
    ga.close(0)
    ga.line(-3), ga.line(3)
    ga.cross(-2), ga.cross(2)
    qkv(0)
    gb.line(-1), gb.line(1)
    ga.close(-1), ga.close(1)
    ga.cross(-3), ga.cross(3)
    qkv(1)
    gc.ready()
    gc.far(2, 0)
    gc.far(1, 0)
    gb.cross(0)
    gc.far(3, 0)
    gc.far(2, 1)
    ga.close(-2), ga.close(2)
    qkv(2)
    ga.close(-3), ga.close(3)
    gb.line(-2), gb.line(2)
    gc.far(1, 1)
    gc.far(3, 1)
    qkv(3)
    gb.cross(-1), gb.cross(1)
    gc.far(2, 2)
    gc.far(1, 2)
    gb.close(0)
    gc.far(3, 2)
    gc.far(2, 3)
    heads_wait(0)
    gb.line(-3), gb.line(3)
    gc.far(1, 3)
    gc.far(3, 3)
    gb.cross(-2), gb.cross(2)
    gb.close(-1), gb.close(1)
    heads_wait(1)
    heads_wait(2)
    keep_a = pltpu.make_async_copy(stack, oa_ref, csem.at[0])
    keep_heads = pltpu.make_async_copy(seen, heads, csem.at[1])
    keep_a.start()
    keep_heads.start()
    chunk = 256
    per_slot = seq // chunk

    def attend_at(i, _):
        s, c = i // per_slot, i % per_slot
        bias = key_bias(lengths_ref[s], seq)
        attend_step(
            c, seen.at[0, s], seen.at[1, s], seen.at[2, s], bias, low.at[s], wide_ref.at[s], lse_ref.at[s], chunk
        )

        @pl.when(c == per_slot - 1)
        def _():
            mixed_own(s).start()
            for d in range(1, n):
                mixed_copy(s, d).start()

        @pl.when(i == 0)
        def _():
            gb.cross(-3), gb.cross(3)
            gc.come(1)

        @pl.when(i == 4)
        def _():
            gb.close(-2), gb.close(2)
            gc.come(3)

        return 0

    lax.fori_loop(0, slots * per_slot, attend_at, 0)
    gb.close(-3), gb.close(3)
    gc.come(2)
    mixed_wait()
    mixed_ref[...] = mixed[...]
    keep_a.wait()
    keep_heads.wait()
    for i in range(3):
        to_core(i).wait_send()
        to_x(i).wait_send()
    for d in range(1, n):
        for j in range(3):
            head_copy(j, peer(d)).wait_send()
        for s in range(slots):
            mixed_copy(s, d).wait_send()
    ga.finish(False)
    gb.finish()
    gc.finish()


def front_call(given, rows_a, rows_b, rows_c, tokens, gains, cosine, sine, lengths, slots, block_len, collective_id):
    vmem = pl.BlockSpec(memory_space=pltpu.VMEM)
    any_ = pl.BlockSpec(memory_space=pl.ANY)
    low = jnp.bfloat16
    width = tokens.shape[1]
    seq = block_len * 8
    my_width = width // 8
    stack_a, stack_b = (
        jax.ShapeDtypeStruct((r, width), low) for r in (64 * rows_a, 64 * rows_b + 32 * rows_c)
    )
    scratch = [
        pltpu.VMEM(stack_a.shape, low),
        pltpu.VMEM((3, slots, block_len, width), low),
        pltpu.VMEM((3, slots, seq, my_width), low),
        pltpu.VMEM((slots, seq, my_width), low),
        pltpu.VMEM((slots, block_len, width), low),
    ]
    for pieces in (4, 2, 2):
        for r in (rows_a, rows_b):
            scratch.append(pltpu.VMEM((pieces * r, width), low))
    scratch += [pltpu.VMEM((pieces * rows_c, width), low) for pieces in (2, 1, 1)]
    return pl.pallas_call(
        front_kernel,
        out_shape=(
            stack_a,
            stack_b,
            jax.ShapeDtypeStruct((3, slots, seq, my_width), low),
            jax.ShapeDtypeStruct((slots, seq, my_width), jnp.float32),
            jax.ShapeDtypeStruct((slots, seq, my_width), jnp.float32),
            jax.ShapeDtypeStruct((slots, block_len, width), low),
            jax.ShapeDtypeStruct((slots * block_len, width), low),
        ),
        in_specs=[vmem] * 5 + [pl.BlockSpec(memory_space=pltpu.SMEM)],
        out_specs=(any_, any_, any_, vmem, vmem, vmem, vmem),
        scratch_shapes=scratch
        + [DMA((6,)), DMA((6,)), DMA((2,)), DMA((3,)), DMA((3, 8)), DMA((3, 8)), DMA((slots,)), DMA((slots, 8)), DMA((slots, 8))]
        + GATHER_SEMS * 2
        + LATE_GATHER_SEMS,
        compiler_params=pltpu.CompilerParams(
            collective_id=collective_id, has_side_effects=True, vmem_limit_bytes=VMEM_BYTES
        ),
        name="spread_and_attend",
    )(given, tokens, gains, cosine, sine, lengths)


GAIN_SEMS = [DMA((6,)), DMA((6,))]


class GainSum:
    def __init__(self, ref, got, line, sems):
        self.ref, self.got, self.all = ref, got, line
        self.send, self.recv = sems
        self.z, self.y, self.x, self.core = place()

    def step(self, i):
        z, y, x, core = self.z, self.y, self.x, self.core
        to = (device_at(z, y, x, 1 - core), device_at(z, y, 1 - x, core), device_at(z, 1 - y, x, core))[i]
        return remote(self.ref, self.got.at[i], self.send.at[i], self.recv.at[i], to)

    def far(self, d):
        to = device_at((self.z + d) % 4, self.y, self.x, self.core)
        return remote(self.ref, self.all.at[self.z], self.send.at[2 + d], self.recv.at[2 + d], to)

    def begin(self, i):
        self.step(i).start()

    def end(self, i):
        self.step(i).wait()
        self.ref[...] = self.ref[...] + self.got[i]

    def begin_far(self):
        for d in (1, 2, 3):
            self.far(d).start()
        self.all[self.z] = self.ref[...]

    def end_far(self, out):
        for d in (1, 2, 3):
            self.far(d).wait()
        total = self.all[0]
        for i in range(1, 4):
            total = total + self.all[i]
        out[...] = total


def back_kernel(
    g_ref, qkv_ref, wide_ref, lse_ref, cos_ref, sin_ref, norm_ref, tokens_ref, gains_ref, middle_ref, gain_ref,
    left_ref, right_ref, w_ref, lengths_ref,
    oa_ref, ob_ref, og_ref, tok_ref,
    left_got, late_got, right_got, norm_got, rows_got, weight_ref, xsend, xrecv, heads, grad, rows, acc_k, acc_v, dnorm, gain, gain_got, gain_all, wsem, gl, gsend, grecv, dl, dsend, drecv, *refs
):
    n = 8
    slots, block_len, width = g_ref.shape
    seq, my_width = qkv_ref.shape[2:]
    chunk = 256
    per_slot = seq // chunk
    m = len(GATHER_SEMS)
    rows_a, rows_b, rows_c = oa_ref.shape[0] // 64, left_got.shape[2] // 8, late_got.shape[2] // 4
    start_c = 64 * rows_b
    ra = Reduce(rows_a, refs[:REDUCE_REFS])
    rb = Reduce(rows_b, refs[REDUCE_REFS : 2 * REDUCE_REFS])
    refs = refs[2 * REDUCE_REFS :]
    rc = LateReduce(rows_c, refs[:LATE_REDUCE_REFS])
    refs = refs[LATE_REDUCE_REFS:]
    ga = Gather(ra.own, oa_ref, rows_a, refs[:m])
    gb = Gather(rb.own, ob_ref.at[pl.ds(0, start_c)], rows_b, refs[m : 2 * m])
    refs = refs[2 * m :]
    gc = LateGather(rc.own, ob_ref.at[pl.ds(start_c, 32 * rows_c)], rows_c, refs[: len(LATE_GATHER_SEMS)])
    gs = GainSum(gain, gain_got, gain_all, refs[len(LATE_GATHER_SEMS) :])
    z, y, x, core = place()
    ctx, shard = lax.axis_index("ctx"), lax.axis_index("shard")
    greet([ra.xn, ra.sib] + [(lax.rem(ctx + d, n), shard) for d in range(1, n)])

    def peer(d):
        return lax.rem(ctx + d, n)

    def lanes(owner):
        return pl.ds(pl.multiple_of(owner * my_width, my_width), my_width)

    def block(owner):
        return pl.ds(pl.multiple_of(owner * block_len, block_len), block_len)

    def go_copy(d):
        return remote(
            g_ref.at[:, :, lanes(peer(d))], grad.at[:, block(ctx), :], gsend.at[d], grecv.at[d], (peer(d), shard)
        )

    def back_copy(s, d):
        return remote(
            heads.at[:, s, block(peer(d)), :], rows.at[:, s, :, lanes(ctx)], dsend.at[s, d], drecv.at[s, d], (peer(d), shard)
        )

    def back_own(s):
        return pltpu.make_async_copy(heads.at[:, s, block(ctx), :], rows.at[:, s, :, lanes(ctx)], dl.at[s])

    go_own = pltpu.make_async_copy(g_ref.at[:, :, lanes(ctx)], grad.at[:, block(ctx), :], gl)
    w_copy = pltpu.make_async_copy(w_ref, weight_ref, wsem)
    cut = 128
    rows_all = slots * block_len

    def to_sib(src, dst, i):
        return remote(src, dst, xsend.at[i], xrecv.at[i], ra.sib)

    region_b, region_c = 8 * rows_b, 4 * rows_c

    def left_copy(t, c):
        lane = pl.ds(pl.multiple_of((rb.zb(t) * 2 + c) * region_b, cut), region_b)
        return to_sib(left_ref.at[:, lane], left_got.at[rb.zb(t)], t)

    def late_copy(zb, c):
        lane = pl.ds(pl.multiple_of(start_c + (zb * 2 + c) * region_c, cut), region_c)
        return to_sib(left_ref.at[:, lane], late_got.at[zb], 6 + slots + zb)

    right_copy = to_sib(right_ref, right_got, 4)
    norm_copy = to_sib(norm_ref, norm_got, 5)
    def rows_copy(s):
        return to_sib(rows.at[:, s], rows_got.at[:, s], 6 + s)

    def given():
        right_copy.start()
        left_copy(0, 1 - core).start()
        for t in range(4):
            late_copy(t, 1 - core).start()
        for t in range(1, 4):
            left_copy(t, 1 - core).start()
        norm_copy.start()
        right_copy.wait_recv()

    def product(zb, start, region, got, acc):
        count = region // cut

        def step(i, _):
            g = start // cut + (zb * 2 + core) * count + i
            kind = (g >= width // cut).astype(jnp.int32) + (g >= (width + 2 * FF_WIDE) // cut).astype(jnp.int32)
            mine = left_ref[:, pl.ds(pl.multiple_of(g * cut, cut), cut)]
            other = got[zb, :, pl.ds(pl.multiple_of(i * cut, cut), cut)]
            total = leading(mine, right_ref[kind]) + leading(other, right_got[kind])
            at = pl.ds(pl.multiple_of((zb * count + i) * cut, cut), cut)
            acc[at, :] = total.astype(jnp.bfloat16)
            return 0

        lax.fori_loop(0, count, step, 0)

    def fill(t):
        left_copy(t, core).wait_recv()
        product(rb.zb(t), 0, region_b, left_got, rb.acc)

    def late():
        for zb in range(4):
            late_copy(zb, core).wait_recv()

        def step(zb, _):
            product(zb, start_c, region_c, late_got, rc.acc)
            return 0

        lax.fori_loop(0, 4, step, 0)

    cols = 256
    tiles = width // cols

    def rows_wait(s):
        back_own(s).wait()
        for d in range(1, n):
            back_copy(s, d).wait_recv()
        rows_copy(s).start()

    def both():
        norm_copy.wait_recv()
        for s in range(slots):
            rows_copy(s).wait_recv()

    def weight(t):
        zb = ra.zb(t)
        count = 8 * rows_a // cut

        def step(i, _):
            g = (zb * 2 + core) * count + i
            j = g * cut // width
            lane = pl.ds(pl.multiple_of(g * cut - j * width, cut), cut)
            total = leading(rows[j, :, :, lane].reshape(rows_all, cut), norm_ref[...])
            total += leading(rows_got[j, :, :, lane].reshape(rows_all, cut), norm_got[...])
            at = pl.ds(pl.multiple_of(zb * 8 * rows_a + i * cut, cut), cut)
            ra.acc[at, :] = total.astype(jnp.bfloat16)
            return 0

        lax.fori_loop(0, count, step, 0)

    def norm_step(t, _):
        at = pl.ds(pl.multiple_of(t * cols, cols), cols)
        total = None
        for j in range(3):
            left = rows[j].reshape(slots * block_len, width)
            right = weight_ref[pl.ds(j * width, width), at]
            part = jnp.dot(left, right, preferred_element_type=jnp.float32)
            total = part if total is None else total + part
        dnorm[:, at] = total
        return 0

    some = 64
    def token_step(i, _):
        at = pl.ds(pl.multiple_of(i * some, some), some)
        values = tokens_ref[at, :].astype(jnp.float32)
        mean = jnp.mean(values, axis=-1, keepdims=True)
        centred = values - mean
        scale = lax.rsqrt(jnp.mean(centred * centred, axis=-1, keepdims=True) + eps_norm)
        unit = centred * scale
        given = dnorm[at, :]
        inner = given * gains_ref[0:1, :]
        inner_mean = jnp.mean(inner, axis=-1, keepdims=True)
        along = jnp.mean(inner * unit, axis=-1, keepdims=True)
        grads = middle_ref[at, :] + scale * (inner - inner_mean - unit * along)
        tok_ref[at, :] = grads.astype(jnp.bfloat16)
        gain[0:1, :] += jnp.sum(given * unit, axis=0, keepdims=True)
        return 0

    def token():
        w_copy.wait()
        lax.fori_loop(0, tiles, norm_step, 0)
        gain[...] = gain_ref[...]
        lax.fori_loop(0, slots * block_len // some, token_step, 0)
        gs.begin(0)

    for d in range(1, n):
        go_copy(d).start()
    go_own.start()
    given()
    fill(0)
    rb.go1(0, 0)
    rb.go1(0, 1)
    fill(1)
    fill(2)
    fill(3)
    late()
    w_copy.start()
    go_own.wait()
    for d in range(1, n):
        go_copy(d).wait_recv()

    def attend_step(i, _):
        s, c = i // per_slot, i % per_slot
        slot = (
            qkv_ref.at[0, s], qkv_ref.at[1, s], qkv_ref.at[2, s], grad.at[s], wide_ref.at[s], lse_ref.at[s],
            key_bias(lengths_ref[s], seq), cos_ref, sin_ref, heads.at[0, s], heads.at[1, s], heads.at[2, s], acc_k, acc_v, chunk,
        )

        @pl.when(c == 0)
        def _():
            acc_k[...] = jnp.zeros_like(acc_k)
            acc_v[...] = jnp.zeros_like(acc_v)

        attend_back_step(c, *slot)

        @pl.when(c == per_slot - 1)
        def _():
            attend_back_end(*slot)
            back_own(s).start()
            for d in range(1, n):
                back_copy(s, d).start()

        @pl.when(i == 1)
        def _():
            rb.one(0, 0)
            rb.go1(1, 0)
            rb.one(0, 1)
            rb.go1(1, 1)

        return 0

    lax.fori_loop(0, slots * per_slot, attend_step, 0)
    rb.two(0)
    rb.one(1, 0)
    rb.go1(2, 0)
    rb.one(1, 1)
    rb.go1(2, 1)
    rc.far(2, 0)
    rc.far(1, 0)
    rb.tri(0, 1)
    rb.tri(0, 0)
    rb.two(1)
    rb.one(2, 0)
    rb.go1(3, 0)
    rb.one(2, 1)
    rb.go1(3, 1)
    rc.far(3, 0)
    rc.far(2, 1)
    rb.tri(1, 1)
    rb.tri(1, 0)
    rb.two(2)
    rb.one(3, 0)
    rb.one(3, 1)
    rc.far(1, 1)
    rc.far(3, 1)
    rb.tri(2, 1)
    rb.tri(2, 0)
    rows_wait(0)
    rows_wait(1)
    both()
    weight(0)
    ra.go1(0, 0)
    ra.go1(0, 1)
    weight(1)
    ra.go1(1, 0)
    ra.go1(1, 1)
    rc.far(2, 2)
    rc.far(1, 2)
    rc.far(3, 2)
    rb.two(3)
    weight(2)
    ra.go1(2, 0)
    ra.go1(2, 1)
    weight(3)
    ra.go1(3, 0)
    ra.go1(3, 1)
    rc.far(2, 3)
    rc.far(1, 3)
    rc.far(3, 3)
    ra.one(0, 0)
    ra.one(0, 1)
    rb.three()
    gb.start()
    token()
    ra.one(1, 0)
    ra.one(1, 1)
    ra.two(0)
    rc.three()
    ra.one(2, 0)
    ra.one(2, 1)
    ra.tri(0, 1)
    ra.tri(0, 0)
    ra.two(1)
    rc.one()
    gb.line(-1), gb.line(1)
    ra.one(3, 0)
    ra.one(3, 1)
    ra.tri(1, 1)
    ra.tri(1, 0)
    ra.two(2)
    gb.cross(0)
    rc.two()
    gc.start()
    gs.end(0)
    gs.begin(1)
    ra.tri(2, 1)
    ra.tri(2, 0)
    ra.two(3)
    gb.line(-2), gb.line(2)
    gc.pass_on()
    ra.three()
    ga.start()
    gc.ready()
    gc.far(2, 0)
    gc.far(1, 0)
    gc.far(3, 0)
    gb.cross(-1), gb.cross(1)
    gs.end(1)
    gs.begin(2)
    gb.close(0)
    gc.far(2, 1)
    gc.far(1, 1)
    gc.far(3, 1)
    gb.line(-3), gb.line(3)
    gc.far(2, 2)
    gc.far(1, 2)
    gc.far(3, 2)
    ga.line(-1), ga.line(1)
    gb.cross(-2), gb.cross(2)
    gc.far(2, 3)
    gc.far(1, 3)
    gc.far(3, 3)
    gs.end(2)
    gs.begin_far()
    ga.cross(0)
    gb.close(-1), gb.close(1)
    ga.line(-2), ga.line(2)
    gb.cross(-3), gb.cross(3)
    gc.come(1)
    ga.cross(-1), ga.cross(1)
    ga.close(0)
    gb.close(-2), gb.close(2)
    gc.come(3)
    ga.line(-3), ga.line(3)
    ga.cross(-2), ga.cross(2)
    ga.close(-1), ga.close(1)
    gb.close(-3), gb.close(3)
    ga.cross(-3), ga.cross(3)
    ga.close(-2), ga.close(2)
    ga.close(-3), ga.close(3)
    gc.come(2)
    gs.end_far(og_ref)
    for d in range(1, n):
        go_copy(d).wait_send()
        for s in range(slots):
            back_copy(s, d).wait_send()
    for t in range(4):
        left_copy(t, 1 - core).wait_send()
        late_copy(t, 1 - core).wait_send()
    for copy in [right_copy, norm_copy] + [rows_copy(s) for s in range(slots)]:
        copy.wait_send()
    ra.finish(), rb.finish(), rc.finish()
    ga.finish(), gb.finish(), gc.finish()


def back_call(
    grad_rows, qkv_heads, wide, lse, cosine, sine, norm_one, tokens, gains, grad_middle, gain_part, left, right, w_qkv, lengths, collective_id
):
    any_ = pl.BlockSpec(memory_space=pl.ANY)
    vmem = pl.BlockSpec(memory_space=pltpu.VMEM)
    low = jnp.bfloat16
    slots, block_len, width = grad_rows.shape
    seq, my_width = qkv_heads.shape[2:]
    rows_all = slots * block_len
    gain = gain_part.shape
    rows_a, rows_c = w_qkv.shape[0] // 64, ROWS_C
    rows_b = left.shape[1] // 64 - rows_c // 2
    return pl.pallas_call(
        back_kernel,
        out_shape=(
            jax.ShapeDtypeStruct(w_qkv.shape, low),
            jax.ShapeDtypeStruct((left.shape[1], width), low),
            jax.ShapeDtypeStruct(gain, jnp.float32),
            jax.ShapeDtypeStruct((rows_all, width), low),
        ),
        in_specs=[vmem] * 13 + [any_, pl.BlockSpec(memory_space=pltpu.SMEM)],
        out_specs=(any_, any_, vmem, vmem),
        scratch_shapes=[
            pltpu.VMEM((4, rows_all, 8 * rows_b), low),
            pltpu.VMEM((4, rows_all, 4 * rows_c), low),
            pltpu.VMEM(right.shape, low),
            pltpu.VMEM((rows_all, width), low),
            pltpu.VMEM((3, slots, block_len, width), low),
            pltpu.VMEM(w_qkv.shape, low),
            DMA((10 + slots,)),
            DMA((10 + slots,)),
            pltpu.VMEM(qkv_heads.shape, low),
            pltpu.VMEM((slots, seq, my_width), low),
            pltpu.VMEM((3, slots, block_len, width), low),
            pltpu.VMEM((seq, my_width), jnp.float32),
            pltpu.VMEM((seq, my_width), jnp.float32),
            pltpu.VMEM((rows_all, width), jnp.float32),
            pltpu.VMEM(gain, jnp.float32),
            pltpu.VMEM((3,) + gain, jnp.float32),
            pltpu.VMEM((4,) + gain, jnp.float32),
            DMA,
            DMA,
            DMA((8,)),
            DMA((8,)),
            DMA((slots,)),
            DMA((slots, 8)),
            DMA((slots, 8)),
        ]
        + reduce_scratch(rows_a, width)
        + reduce_scratch(rows_b, width)
        + late_reduce_scratch(rows_c, width)
        + GATHER_SEMS * 2
        + LATE_GATHER_SEMS
        + GAIN_SEMS,
        compiler_params=pltpu.CompilerParams(
            collective_id=collective_id, has_side_effects=True, vmem_limit_bytes=VMEM_BYTES
        ),
        name="back_and_sum",
    )(
        grad_rows, qkv_heads, wide, lse, cosine, sine, norm_one, tokens, gains, grad_middle, gain_part, left, right, w_qkv, lengths
    )


def to_heads(values):
    return lax.all_to_all(values, "ctx", split_axis=3, concat_axis=2, tiled=True)


def to_rows(values):
    return lax.all_to_all(values, "ctx", split_axis=2, concat_axis=3, tiled=True)


def shards(
    fast,
    tokens,
    cotangent,
    lengths,
    unit_owner,
    master,
    first_moment,
    second_moment,
    norm_gains,
    gain_first,
    gain_second,
):
    slots, block_len, width = tokens.shape
    groups = lax.axis_size("shard")
    n = lax.axis_size("ctx")
    ctx, shard = lax.axis_index("ctx"), lax.axis_index("shard")
    capacity, unit_rows, _ = master.shape
    units = unit_owner.shape[0]
    rows_all = slots * block_len
    seq = block_len * n
    device_count = n * groups
    my_width = width // n

    low = jnp.bfloat16
    rows_a = 3 * width
    rows_b = width + 3 * FF_WIDE
    split = rows_a // unit_rows
    lead, ff_units, wide_units = (r // unit_rows for r in (width, FF, FF_WIDE))

    def unit_of(block, chunk):
        if chunk == 0:
            return jnp.where(block < split, block, -1)
        inner = block - lead
        third = inner // wide_units
        at = inner - third * wide_units
        there = (block < lead) | ((at < ff_units) & (third < 3))
        return jnp.where(there, split + jnp.where(block < lead, block, lead + third * ff_units + at), -1)

    def block_of(unit):
        inner = unit - split - lead
        third = jnp.maximum(inner, 0) // ff_units
        return unit - split + third * (wide_units - ff_units)

    part_rows = 16
    per_unit = unit_rows // part_rows
    parts = master.reshape(capacity * per_unit, part_rows, width)

    def units_at(chunk, per, wanted, start=0):
        at = wanted[..., None] * (per // part_rows) + jnp.arange(per // part_rows, dtype=jnp.int32)
        at = at + start // part_rows
        at = at.reshape(-1)
        return unit_of(at // per_unit, chunk), at % per_unit

    def pick(unit, inner):
        mine, rank = own_places(unit_owner, shard, unit)
        return pick_call(jnp.where(mine, rank * per_unit + inner, -1), parts)

    def piece_rows(count, pieces):
        return -(-count // (pieces * part_rows)) * part_rows

    cos_seq, sin_seq = rope_tables(seq, my_width // HEAD_DIM)
    flat_tokens = tokens.reshape(rows_all, width)

    if fast:
        z, y, x, core = place()
        wanted = jnp.stack(
            [
                jnp.stack([jnp.stack([piece_at(z, c, 0, y, q), piece_at(z, c, 1, q, y)]) for q in range(2)])
                for c in range(2)
            ]
        )
        late = jnp.stack([jnp.stack([((z * 2 + c) * 2 + y) * 2 + q for q in range(2)]) for c in range(2)])
        per_a, per_b = piece_rows(rows_a, 64), piece_rows(rows_b, 64) - ROWS_C // 2
        at_pieces = [
            units_at(0, per_a, wanted),
            units_at(1, per_b, wanted),
            units_at(1, ROWS_C, late, 64 * per_b),
        ]
        given = pick(*(jnp.concatenate(both) for both in zip(*at_pieces)))
        stack_a, stack_b, qkv_heads, wide, lse, mixed_low, norm_one = front_call(
            given, per_a, per_b, ROWS_C, flat_tokens, norm_gains, cos_seq, sin_seq, lengths, slots, block_len, 0
        )
    else:
        wanted = ctx * groups + jnp.arange(groups, dtype=jnp.int32)
        stacks = []
        for chunk, count in enumerate((rows_a, rows_b)):
            share = pick(*units_at(chunk, piece_rows(count, device_count), wanted))
            own = lax.psum_scatter(share, "shard", scatter_dimension=0, tiled=True)
            stacks.append(lax.all_gather(own, BOTH, axis=0, tiled=True))
        stack_a, stack_b = stacks
        inputs = flat_tokens.astype(jnp.float32)
        norm_one = layer_norm(inputs, norm_gains[0]).astype(low)
        cos_rows, sin_rows = (
            jnp.tile(lax.dynamic_slice_in_dim(table, ctx * block_len, block_len, 0), (slots, 256 // my_width))
            for table in (cos_seq, sin_seq)
        )
        qkv = qkv_call(norm_one, stack_a, cos_rows, sin_rows)
        qkv_heads = to_heads(qkv.reshape(3, slots, block_len, width))
        mixed_heads, wide, lse = attend_call(qkv_heads, lengths)
        mixed_low = to_rows(mixed_heads[None])
    mixed_low = mixed_low.reshape(rows_all, width)
    left_cols = 64 * piece_rows(rows_b, 64)
    output, left, right, grad_heads_rows, grad_middle, gain_part = middle_call(
        mixed_low, flat_tokens, cotangent.reshape(rows_all, width), norm_gains, lengths, stack_b, left_cols, block_len
    )
    output = output.reshape(slots, block_len, width)
    grad_heads_rows = grad_heads_rows.reshape(slots, block_len, width)

    if fast:
        all_a, all_b, gain_grad, token_grad = back_call(
            grad_heads_rows, qkv_heads, wide, lse, cos_seq, sin_seq, norm_one, flat_tokens,
            norm_gains, grad_middle, gain_part, left, right, stack_a, lengths, 1,
        )
    else:
        cuts = (0, width, width + 2 * FF_WIDE, rows_b)
        grads_b = jnp.concatenate(
            [leading(left[:, cuts[i] : cuts[i + 1]], right[i]).astype(low) for i in range(3)]
            + [jnp.zeros((stack_b.shape[0] - rows_b, width), low)],
            axis=0,
        )
        grad_heads = to_heads(grad_heads_rows[None])[0]
        grad_qkv_heads = attend_back_call(qkv_heads, grad_heads, wide, lse, lengths, cos_seq, sin_seq)
        grad_qkv_low = to_rows(grad_qkv_heads).reshape(3, rows_all, width)
        grad_norm_one = sum(
            jnp.dot(
                grad_qkv_low[i],
                stack_a[i * width : (i + 1) * width],
                preferred_element_type=jnp.float32,
            )
            for i in range(3)
        )
        _, norm_back_one = jax.vjp(layer_norm, inputs, norm_gains[0])
        grad_input_part, grad_gain_one = norm_back_one(grad_norm_one)
        token_grad = (grad_middle + grad_input_part).astype(low)
        grads_a = jnp.concatenate(
            [leading(grad_qkv_low[i], norm_one).astype(low) for i in range(3)]
            + [jnp.zeros((stack_a.shape[0] - rows_a, width), low)],
            axis=0,
        )
        all_a, all_b = (
            lax.all_gather(
                lax.psum_scatter(g, BOTH, scatter_dimension=0, tiled=True), BOTH, axis=0, tiled=True
            )
            for g in (grads_a, grads_b)
        )
        gain_grad = lax.psum(gain_part.at[0].set(grad_gain_one), BOTH)
    token_grad = token_grad.reshape(slots, block_len, width)
    all_a = all_a.reshape(-1, unit_rows, width)
    all_b = all_b.reshape(-1, unit_rows, width)

    every = jnp.arange(units, dtype=jnp.int32)
    rank = own_places(unit_owner, shard, every)[1]
    here = (unit_owner == shard) & (rank == jnp.arange(capacity, dtype=jnp.int32)[:, None])
    unit_of_slot = jnp.sum(jnp.where(here, every + 1, 0), axis=1) - 1
    kind = jnp.where(unit_of_slot < 0, -1, (unit_of_slot >= split).astype(jnp.int32))
    at_a = jnp.where(kind == 0, unit_of_slot, 0)
    at_b = jnp.where(kind == 1, block_of(unit_of_slot), 0)
    new_master, new_first, new_second, new_gains, new_gain_first, new_gain_second = adam_call(
        kind, at_a, at_b, all_a, all_b, gain_grad, (norm_gains, gain_first, gain_second), master, first_moment, second_moment
    )
    return (
        output,
        token_grad,
        new_master,
        new_first,
        new_second,
        new_gains,
        new_gain_first,
        new_gain_second,
    )


def solution(mesh):
    fast = dict(mesh.shape) == {"ctx": 8, "shard": 4}
    return jax.shard_map(
        functools.partial(shards, fast),
        mesh=mesh,
        in_specs=(
            P("shard", "ctx", None),
            P("shard", "ctx", None),
            P("shard"),
            P(),
            P("shard", None, None),
            P("shard", None, None),
            P("shard", None, None),
            P(),
            P(),
            P(),
        ),
        out_specs=(
            P("shard", "ctx", None),
            P("shard", "ctx", None),
            P("shard", None, None),
            P("shard", None, None),
            P("shard", None, None),
            P(),
            P(),
            P(),
        ),
        check_vma=False,
    )
```
